32 devices in a mesh: shard: 2 (over y), ctx: 4 (over x, core), tensor: 4 (over z).
Axes of the slice: x: 2, y: 2, z: 4, core: 2. Of those that a mesh axis runs over, the one named last changes fastest.
Arguments:
- inputs: bfloat16 [2, 1024, 2048], P('shard', 'ctx'), may hold values from -6 to 6
- cotangent: bfloat16 [2, 1024, 2048], P('shard', 'ctx'), may hold values from -6 to 6
- piece_starts: int32 [2, 3], P('shard'), may hold values from 0 to 768, as said below
- positions: int32 [2, 1024], P('shard', 'ctx'), may hold values from 0 to 303, as said below
- w_qkv: float32 [2048, 8, 768], P(('shard', 'ctx'), 'tensor'), may hold values from -0.125 to 0.125
- b_qkv: float32 [8, 768], P('tensor'), may hold values from -1.2 to 1.2
- w_dense: float32 [2048, 8, 256], P(('shard', 'ctx'), 'tensor'), may hold values from -0.5 to 0.5
- w_fc1: float32 [2048, 8192], P(('shard', 'ctx'), 'tensor'), may hold values from -0.125 to 0.125
- b_fc1: float32 [8192], P('tensor'), may hold values from -3 to 3
- w_fc2: float32 [2048, 8192], P(('shard', 'ctx'), 'tensor'), may hold values from -0.0625 to 0.0625
- out_bias: float32 [2048], replicated, may hold values from -3 to 3
- ln1_gain: float32 [2048], replicated, may hold values from 0.1 to 1.9
- ln1_bias: float32 [2048], replicated, may hold values from -2 to 2
- ln2_gain: float32 [2048], replicated, may hold values from 0.1 to 1.9
- ln2_bias: float32 [2048], replicated, may hold values from -2 to 2
Outputs:
- output: bfloat16 [2, 1024, 2048], P('shard', 'ctx')
- grad_inputs: float32 [2, 1024, 2048], P('shard', 'ctx')
- grad_w_qkv: float32 [2048, 8, 768], P(('shard', 'ctx'), 'tensor')
- grad_b_qkv: float32 [8, 768], P('tensor')
- grad_w_dense: float32 [2048, 8, 256], P(('shard', 'ctx'), 'tensor')
- grad_w_fc1: float32 [2048, 8192], P(('shard', 'ctx'), 'tensor')
- grad_b_fc1: float32 [8192], P('tensor')
- grad_w_fc2: float32 [2048, 8192], P(('shard', 'ctx'), 'tensor')
- grad_out_bias: float32 [2048], replicated
- grad_ln1_gain: float32 [2048], replicated
- grad_ln1_bias: float32 [2048], replicated
- grad_ln2_gain: float32 [2048], replicated
- grad_ln2_bias: float32 [2048], replicated
The draws below stay inside these ranges and needn't reach their ends.
Inputs may be any that keep to these rules, and one draw needn't show every extreme that they name: `piece_starts`: for each sequence, 3 starts in increasing order; its picture pieces of 256 tokens do not intersect and lie inside the sequence. `positions`: in each sequence the position starts at 0 and rises by one at every token outside the picture pieces and at the first of every 16 tokens of a piece; the other tokens of a piece keep the position before them.
All inputs are finite; a program needn't handle non-finite values.
Results may differ from the reference program's by a relative error of at most 0.012.
Values may be sent and summed in bfloat16 or wider, within the bound.
No kernel may reach another device: no remote copies, remote signals or barrier semaphores. Data moves between devices by JAX's collectives and lax.ppermute only.
A program may use at most 256 MiB of HBM per device.

```python
import jax
import jax.numpy as jnp
from jax import lax

D = 2048
HEADS = 8
HEAD = 256
FF = 8192
ROT = 64
PIECE = 256
GRID = 16
PIECES = 3
LENGTH = 1024
SEQS = 2


def piece_layout(key):
    base_key = jax.random.fold_in(key, 7)
    text_count = LENGTH - PIECES * PIECE
    cut_points = jnp.sort(jax.random.randint(base_key, (SEQS, PIECES), 0, text_count + 1), axis=1)
    row_ids = jnp.arange(SEQS)[:, None]
    col_ids = jnp.arange(PIECES)[None, :]
    cut_points = jnp.where((row_ids == 0) & (col_ids == PIECES - 1), text_count, cut_points)
    cut_points = jnp.where((row_ids == 1) & (col_ids == 0), 0, cut_points)
    starts = (cut_points + col_ids * PIECE).astype(jnp.int32)
    token_index = jnp.arange(LENGTH)[None, :, None]
    inside = (token_index >= starts[:, None, :]) & (token_index < starts[:, None, :] + PIECE)
    offset = token_index - starts[:, None, :]
    row_head = jnp.any(inside & (offset % GRID == 0), axis=2)
    covered = jnp.any(inside, axis=2)
    steps_up = jnp.where(covered, row_head, True).astype(jnp.int32)
    places = (jnp.cumsum(steps_up, axis=1) - 1).astype(jnp.int32)
    return (starts, places)


def draw_piece_starts(key, part):
    return piece_layout(key)[0]


def draw_positions(key, part):
    return piece_layout(key)[1]


def strengthened(array, own_key, source, target, blocks, factor):
    def block_of(position):
        return (jnp.arange(array.shape[position]) // (array.shape[position] // blocks)).reshape((-1,) + (1,) * (array.ndim - 1 - position))

    first = jax.random.permutation(own_key, blocks)[block_of(target)]
    far = (block_of(target) + blocks // 2) % blocks
    return jnp.where((block_of(source) == first) | (block_of(source) == far), factor * array, array)


def levels(stream_key, extent, pieces, low, top_value):
    def one(position, shards_of):
        draws = jax.random.uniform(jax.random.fold_in(jax.random.fold_in(stream_key, 6), position), (shards_of,), jnp.float32, low / len(pieces), top_value / len(pieces))
        return jnp.repeat(jnp.exp(draws), extent[position] // shards_of).reshape((-1,) + (1,) * (len(extent) - position - 1))

    gain = one(*pieces[0])
    for cut in pieces[1:]:
        gain = gain * one(*cut)
    return gain


def scatter_about(rng, dims, width, most, split=(), kind=jnp.bfloat16):
    result = width * jax.random.normal(rng, dims, jnp.float32)
    if split:
        result = result * levels(rng, dims, split, -0.22, 0.18)
    return jnp.clip(result, -most, most).astype(kind)


def bell_draw_with(rng, extent, scale, reach, split, heavy, held_as=jnp.bfloat16):
    entries = scale * jax.random.normal(rng, extent, jnp.float32)
    if split:
        entries = entries * levels(rng, extent, split, -0.22, 0.18)
    return jnp.clip(strengthened(entries, jax.random.fold_in(rng, 3), *heavy), -reach, reach).astype(held_as)


def setup_inputs(seed: int = 0) -> dict:
    splits = jax.random.split(jax.random.key(seed), 16)
    inputs = scatter_about(splits[0], (SEQS, LENGTH, D), 1.0, 6.0, ((0, 2), (1, 4)))
    cotangent = bell_draw_with(splits[1], (SEQS, LENGTH, D), 1.0, 6.0, ((0, 2), (1, 4)), (0, 2, 2, 2.0))
    piece_starts = draw_piece_starts(jax.random.fold_in(splits[15], 71), 0)
    positions = draw_positions(jax.random.fold_in(splits[15], 71), 0)
    w_qkv = scatter_about(splits[4], (D, HEADS, 3 * HEAD), D ** -0.5, 0.125, ((0, 8), (1, 4)), jnp.float32)
    b_qkv = scatter_about(splits[5], (HEADS, 3 * HEAD), 0.2, 1.2, ((0, 4),), jnp.float32)
    w_dense = scatter_about(splits[6], (D, HEADS, HEAD), (D // 16) ** -0.5, 0.5, ((0, 8), (1, 4)), jnp.float32)
    w_fc1 = scatter_about(splits[7], (D, FF), D ** -0.5, 0.125, ((0, 8), (1, 4)), jnp.float32)
    b_fc1 = scatter_about(splits[8], (FF,), 0.5, 3.0, ((0, 4),), jnp.float32)
    w_fc2 = scatter_about(splits[9], (D, FF), FF ** -0.5, 0.0625, ((0, 8), (1, 4)), jnp.float32)
    out_bias = scatter_about(splits[10], (D,), 0.5, 3.0, (), jnp.float32)
    ln1_gain = jnp.clip(1.0 + 0.18 * jax.random.normal(splits[11], (D,), jnp.float32), 0.1, 1.9)
    ln1_bias = scatter_about(splits[12], (D,), 0.3, 2.0, (), jnp.float32)
    ln2_gain = jnp.clip(1.0 + 0.18 * jax.random.normal(splits[13], (D,), jnp.float32), 0.1, 1.9)
    ln2_bias = scatter_about(splits[14], (D,), 0.3, 2.0, (), jnp.float32)
    return {"inputs": inputs, "cotangent": cotangent, "piece_starts": piece_starts, "positions": positions, "w_qkv": w_qkv, "b_qkv": b_qkv, "w_dense": w_dense, "w_fc1": w_fc1, "b_fc1": b_fc1, "w_fc2": w_fc2, "out_bias": out_bias, "ln1_gain": ln1_gain, "ln1_bias": ln1_bias, "ln2_gain": ln2_gain, "ln2_bias": ln2_bias}


EPSILON = 1e-05
ROPE_BASE = 10000.0

@jax.custom_vjp
def low(v):
    return lax.optimization_barrier(v.astype(jnp.bfloat16)).astype(jnp.float32)

@jax.custom_vjp
def low_back(v):
    return v

def low_keep(v):
    return (low(v), None)

def low_pass(kept, grad):
    return (grad,)

def back_keep(v):
    return (v, None)

def back_low(kept, grad):
    return (low(grad),)
low.defvjp(low_keep, low_pass)
low_back.defvjp(back_keep, back_low)

def matmul(left_side, right_side):
    return jnp.dot(left_side, right_side, precision=lax.Precision.HIGHEST, preferred_element_type=jnp.float32)

def layer_norm(values, norm_gain, norm_shift):
    centred = values - lax.optimization_barrier(jnp.mean(values, axis=-1, keepdims=True))
    spread = lax.optimization_barrier(jnp.mean(centred * centred, axis=-1, keepdims=True))
    return centred * lax.rsqrt(spread + EPSILON) * norm_gain + norm_shift

def rotary_tables(places):
    half_rot = ROT // 2
    frequency = ROPE_BASE ** (-(jnp.arange(half_rot, dtype=jnp.float32) * 2.0) / ROT)
    angles = places.astype(jnp.float32)[..., None] * frequency
    angles = jnp.concatenate([angles, angles], axis=-1)
    return (jnp.cos(angles)[..., None, :], jnp.sin(angles)[..., None, :])

def rotate(head_values, cosine, sine_part):
    half_rot = ROT // 2
    rotated_part = head_values[..., :ROT]
    turned = jnp.concatenate([-rotated_part[..., half_rot:], rotated_part[..., :half_rot]], axis=-1)
    return jnp.concatenate([rotated_part * cosine + turned * sine_part, head_values[..., ROT:]], axis=-1)

def piece_ids(token_index, starts):
    inside = (token_index[:, None] >= starts[None, :]) & (token_index[:, None] < starts[None, :] + PIECE)
    labels = jnp.arange(1, PIECES + 1, dtype=jnp.int32)
    return lax.optimization_barrier(jnp.sum(jnp.where(inside, labels[None, :], 0), axis=1)).astype(jnp.int32)

def sequence_forward(parameters, values, starts, places):
    w_qkv, b_qkv, w_dense, w_fc1, b_fc1, w_fc2, out_bias, ln1_gain, ln1_bias, ln2_gain, ln2_bias = parameters
    normed_one = low(layer_norm(values, ln1_gain, ln1_bias))
    normed_two = low(layer_norm(values, ln2_gain, ln2_bias))
    joined = matmul(normed_one, low(w_qkv).reshape(D, HEADS * 3 * HEAD)).reshape(LENGTH, HEADS, 3 * HEAD)
    joined = low_back(joined + b_qkv)
    cosine, sine_part = rotary_tables(places)
    queries = low(rotate(joined[..., :HEAD], cosine, sine_part))
    key_rows = low(rotate(joined[..., HEAD:2 * HEAD], cosine, sine_part))
    value_rows = low(joined[..., 2 * HEAD:])
    token_index = jnp.arange(LENGTH, dtype=jnp.int32)
    piece_labels = piece_ids(token_index, starts)
    block_rows = min(512, LENGTH)
    score_scale = HEAD ** (-0.5)

    def attend(block_item):
        query_block, query_index, query_piece = block_item
        scores = jnp.einsum('qhd,khd->hqk', query_block, key_rows, precision=lax.Precision.HIGHEST) * score_scale
        scores = low_back(scores)
        allowed = (token_index[None, :] <= query_index[:, None]) | (piece_labels[None, :] == query_piece[:, None]) & (query_piece[:, None] > 0)
        scores = jnp.where(allowed[None], scores, -1e+30)
        weights = low(jax.nn.softmax(scores, axis=-1))
        return jnp.einsum('hqk,khd->qhd', weights, value_rows, precision=lax.Precision.HIGHEST)
    attended = lax.map(jax.checkpoint(attend), (queries.reshape(LENGTH // block_rows, block_rows, HEADS, HEAD), token_index.reshape(-1, block_rows), piece_labels.reshape(-1, block_rows)))
    context = low(low_back(attended.reshape(LENGTH, HEADS * HEAD)))
    attn_out = matmul(context, low(w_dense).reshape(D, HEADS * HEAD).T)
    pre_gelu = low_back(matmul(normed_two, low(w_fc1)) + b_fc1)
    hidden = low(jax.nn.gelu(pre_gelu, approximate=False))
    mlp_out = matmul(hidden, low(w_fc2).T)
    return values + attn_out + mlp_out + out_bias

def add_pair(first_term, second_term):
    return first_term + second_term

def reference(inputs, cotangent, piece_starts, positions, w_qkv, b_qkv, w_dense, w_fc1, b_fc1, w_fc2, out_bias, ln1_gain, ln1_bias, ln2_gain, ln2_bias):
    parameters = tuple((item.astype(jnp.float32) for item in (w_qkv, b_qkv, w_dense, w_fc1, b_fc1, w_fc2, out_bias, ln1_gain, ln1_bias, ln2_gain, ln2_bias)))

    def per_sequence(totals, seq_item):
        seq_values, seq_grad, starts, places = seq_item

        def forward(params_in, values_in):
            return sequence_forward(params_in, values_in, starts, places)
        seq_out, pullback = jax.vjp(forward, parameters, seq_values.astype(jnp.float32))
        grad_params, grad_values = pullback(seq_grad.astype(jnp.float32))
        totals = jax.tree.map(add_pair, totals, grad_params)
        return (totals, (seq_out.astype(jnp.bfloat16), grad_values))
    zero_totals = jax.tree.map(jnp.zeros_like, parameters)
    totals, (outputs, input_grads) = lax.scan(per_sequence, zero_totals, (inputs, cotangent, piece_starts, positions))
    return (outputs, input_grads, totals[0], totals[1], totals[2], totals[3], totals[4], totals[5], totals[6], totals[7], totals[8], totals[9], totals[10])
```

```python
import functools

import jax
import jax.numpy as jnp
import numpy as np
from jax import lax
from jax.experimental import pallas as pl
from jax.experimental.pallas import tpu as pltpu
from jax.sharding import PartitionSpec as P

HEAD = 256
HALF = HEAD // 2
ROT = 64
PIECE = 256
GRID = 16
PIECES = 3

EPSILON = 1e-05
ROPE_BASE = 10000.0
ORDER = (0, 2, 1, 3)
BF16 = jnp.bfloat16
F32 = jnp.float32
VMEM = pl.BlockSpec(memory_space=pltpu.VMEM)
SMEM = pl.BlockSpec(memory_space=pltpu.SMEM)


def dot(left, right, dims):
    return lax.dot_general(left, right, ((dims[:1], dims[1:]), ((), ())), preferred_element_type=F32)


def shape(*dims, kind=BF16):
    return jax.ShapeDtypeStruct(dims, kind)


def call(kernel, outs, args, flops=0, grid=None, in_specs=None, out_specs=None, scratch=(), limit=40, prefetch=0):
    if grid is None:
        extra = dict(in_specs=[SMEM] * (1 + prefetch) + [VMEM] * (len(args) - 1 - prefetch), out_specs=[VMEM] * len(outs), scratch_shapes=scratch)
    else:
        extra = dict(grid_spec=pltpu.PrefetchScalarGridSpec(num_scalar_prefetch=1 + prefetch, grid=grid, in_specs=in_specs, out_specs=out_specs, scratch_shapes=scratch))
    size = sum(a.size * a.dtype.itemsize for a in args) + sum(int(np.prod(o.shape)) * o.dtype.itemsize for o in outs)
    return pl.pallas_call(
        kernel, out_shape=outs, compiler_params=pltpu.CompilerParams(vmem_limit_bytes=limit * 2**20),
        cost_estimate=pl.CostEstimate(flops=int(flops), bytes_accessed=int(size), transcendentals=0), **extra,
    )(*args)


def whole(array):
    return pl.BlockSpec(array.shape, lambda *_: (0,) * len(array.shape))


def swap(value, mask):
    return lax.ppermute(value, "ctx", [(i, i ^ mask) for i in range(4)])


def level_swap(value, mask):
    return lax.ppermute(value, "tensor", [(i, i ^ mask) for i in range(4)])


def shift(value, step):
    size = lax.axis_size("shard")
    return lax.ppermute(value, "shard", [(i, (i + step) % size) for i in range(size)])


def part(ref, start, size):
    return ref[:, pl.ds(pl.multiple_of(start, 128), size)]


def prepare_joint(place, qkv, dense, *outs):
    for mask, out in enumerate(outs):
        head, half = place[2] ^ (mask >> 1), place[1] ^ (mask & 1)
        out[:, :HEAD] = part(qkv, head * 3 * HEAD + half * HEAD, HEAD).astype(BF16)
        out[:, HEAD:HEAD + HALF] = part(qkv, head * 3 * HEAD + 2 * HEAD + half * HALF, HALF).astype(BF16)
        out[:, HEAD + HALF:] = part(dense, head * HEAD + half * HALF, HALF).astype(BF16)


def prepare_inner(place, one, two, own, core, one_x, one_d, two_x, two_d):
    rows, width = one_x.shape
    for mask, first, second in ((0, own.at[:rows], own.at[rows:]), (1, core.at[:rows], core.at[rows:]), (2, one_x, two_x), (3, one_d, two_d)):
        first[...] = part(one, (place[0] ^ mask) * width, width).astype(BF16)
        second[...] = part(two, (place[0] ^ mask) * width, width).astype(BF16)


def assemble(place, pieces, out, rows, shards):
    for ref, first, mask, step in pieces:
        to = lax.rem(place[3] + step, shards) * 4 * rows + (place[0] ^ mask) * rows
        out[pl.ds(pl.multiple_of(to, 16), rows), :] = ref[first:first + rows, :]


def token_block(place, step, parts, use):
    own, near, far, sib, near_sib, far_sib = parts
    same = place[4] & 1
    for base, one, first, second in ((0, own, near, far), (4, sib, near_sib, far_sib)):
        for k in (0, 1):
            pl.when(step == base + k)(lambda one=one, k=k: use(one[k * 128:(k + 1) * 128, :]))
        pl.when(step == base + 2 + same)(lambda first=first: use(first[...]))
        pl.when(step == base + 3 - same)(lambda second=second: use(second[...]))


def norm_kernel(place, own, near, far, sib, near_sib, far_sib, gain_one, shift_one, gain_two, shift_two, one, two, plain):
    def use(block):
        values = block.astype(F32)
        centred = values - jnp.mean(values, axis=1, keepdims=True)
        normal = centred * lax.rsqrt(jnp.mean(centred * centred, axis=1, keepdims=True) + EPSILON)
        one[...] = (normal * gain_one[...] + shift_one[...]).astype(BF16)
        two[...] = (normal * gain_two[...] + shift_two[...]).astype(BF16)
        plain[...] = normal.astype(BF16)

    token_block(place, pl.program_id(0), (own, near, far, sib, near_sib, far_sib), use)


def global_index(place, local, block):
    index = local
    for p in range(4):
        index = jnp.where(local // block == p, local % block + (place[0] ^ ORDER[p]) * block, index)
    return index


def turn(front, cosine, sine):
    lane = lax.broadcasted_iota(jnp.int32, front.shape, 1)
    swapped = jnp.where(lane < ROT // 2, pltpu.roll(front, HALF - ROT // 2, 1), pltpu.roll(front, ROT // 2, 1))
    return front * cosine + swapped * sine


def joint_kernel(rows, shards, pieces, place, starts, normed, bias, frequency, *refs):
    blocks, (mine, cosine, sine, weight) = refs[:-4], refs[-4:]
    step = pl.program_id(0)

    @pl.when(step == 0)
    def _():
        assemble(place, [(ref,) + p for ref, p in zip(blocks, pieces)], weight, rows, shards)

    span = normed.shape[0]
    index = lax.broadcasted_iota(jnp.int32, (span, 1), 0)
    order = jnp.where(step == 1, 2, jnp.where(step == 2, 1, step))
    index = index + (place[0] ^ order) * span
    places = index
    for j in range(PIECES):
        inside = jnp.clip(index - starts[j] + 1, 0, PIECE)
        places = places - inside + (inside + GRID - 1) // GRID
    angles = places.astype(F32) * frequency[...]
    lane = lax.broadcasted_iota(jnp.int32, (span, HALF), 1)
    cosine[...] = jnp.cos(angles)
    sine[...] = jnp.where(lane < ROT // 2, -1.0, 1.0) * jnp.sin(angles)
    joined = dot(normed[...], weight[:, :HEAD + HALF], (1, 0))
    head, half = place[2], place[1]
    joined_low = joined[:, :HEAD] + part(bias, head * 3 * HEAD + half * HEAD, HEAD)
    mine[:, :HALF] = turn(joined_low[:, :HALF], cosine[...], sine[...]).astype(BF16)
    mine[:, HALF:HEAD] = joined_low[:, HALF:].astype(BF16)
    mine[:, HEAD:] = (joined[:, HEAD:] + part(bias, head * 3 * HEAD + 2 * HEAD + half * HALF, HALF)).astype(BF16)


def context_kernel(place, own, near, far, sib, near_sib, far_sib, weight, mine, full, total):
    def use(block):
        full[...] = block
        mine[...] = dot(block, weight[:, HEAD + HALF:], (1, 0)).astype(BF16)

    token_block(place, pl.program_id(0), (own, near, far, sib, near_sib, far_sib), use)

    @pl.when(pl.program_id(0) == 0)
    def _():
        total[...] = jnp.sum(own[...].astype(F32), axis=0, keepdims=True)


def attention_kernel(place, starts, mine, got, grad_mine, grad_got, cosine, sine, context, grad, queries, keys, values, grads, acc, value_acc):
    core = place[1]
    length = mine.shape[0]
    half, block = length // 2, length // 4
    scale = HEAD ** (-0.5)
    for p in range(4):
        rows = slice(p * block, (p + 1) * block)
        first = (p * block + half) % length
        theirs = slice(first, first + block)

        @pl.when(core == 0)
        def _():
            queries[rows] = mine[rows, :HEAD]
            keys[rows] = got[theirs, :HEAD]

        @pl.when(core == 1)
        def _():
            queries[rows] = got[theirs, :HEAD]
            keys[rows] = mine[rows, :HEAD]

        values[rows, :HALF] = mine[rows, HEAD:]
        values[rows, HALF:] = got[theirs, HEAD:]
        grads[rows, :HALF] = grad_mine[rows]
        grads[rows, HALF:] = grad_got[theirs]

    def numbers(index):
        label = jnp.zeros_like(index)
        for j in range(PIECES):
            label = jnp.where((index >= starts[j]) & (index < starts[j] + PIECE), j + 1, label)
        return label

    key_index = global_index(place, lax.broadcasted_iota(jnp.int32, (1, length), 1), block)
    key_piece = numbers(key_index)
    for p in range(4):
        rows = slice(p * block, (p + 1) * block)
        query_index = lax.broadcasted_iota(jnp.int32, (block, 1), 0) + (place[0] ^ ORDER[p]) * block
        query_piece = numbers(query_index)
        allowed = (key_index <= query_index) | ((key_piece == query_piece) & (query_piece > 0))
        scores = jnp.where(allowed, dot(queries[rows], keys[...], (1, 1)) * scale, -1e30)
        weights = jnp.exp(scores - jnp.max(scores, axis=1, keepdims=True))
        weights = weights / jnp.sum(weights, axis=1, keepdims=True)
        low = weights.astype(BF16)
        context[rows] = dot(low, values[:, :HALF], (1, 0)).astype(BF16)
        term = dot(low, grads[rows, :HALF], (0, 0))
        value_acc[...] = term if p == 0 else value_acc[...] + term
        grad_weights = dot(grads[rows], values[...], (1, 1))
        centre = jnp.sum(weights * grad_weights, axis=1, keepdims=True)
        back = (weights * (grad_weights - centre)).astype(BF16)

        @pl.when(core == 0)
        def _():
            acc[rows] = dot(back, keys[...], (1, 0)) * scale

        @pl.when(core == 1)
        def _():
            term = dot(back, queries[rows], (0, 0)) * scale
            acc[...] = term if p == 0 else acc[...] + term

    grad[:, HEAD:] = value_acc[...].astype(BF16)
    grad[:, HALF:HEAD] = acc[:, HALF:].astype(BF16)
    grad[:, :HALF] = turn(acc[:, :HALF], cosine[...], -sine[...]).astype(BF16)


def hidden_kernel(rows, shards, pieces, place, normed, bias, *refs):
    blocks, (hidden, slope, weight) = refs[:-3], refs[-3:]

    @pl.when(pl.program_id(0) == 0)
    def _():
        assemble(place, [(ref,) + p for ref, p in zip(blocks, pieces)], weight, rows, shards)

    width = hidden.shape[1]
    pre = dot(normed[...], weight[...], (1, 0)) + part(bias, place[0] * width, width)
    cdf = 0.5 + 0.5 * lax.erf(pre * (0.5 ** 0.5))
    hidden[...] = (pre * cdf).astype(BF16)
    slope[...] = cdf + pre * jnp.exp(-0.5 * pre * pre) * ((0.5 / np.pi) ** 0.5)


def inner_kernel(rows, shards, pieces, place, grads, slope, *refs):
    blocks, (inner, weight) = refs[:-2], refs[-2:]

    @pl.when(pl.program_id(0) == 0)
    def _():
        assemble(place, [(ref,) + p for ref, p in zip(blocks, pieces)], weight, rows, shards)

    inner[...] = (dot(grads[...], weight[...], (1, 0)) * slope[...]).astype(BF16)


def weight_kernel(rows, shards, steps, place, *refs):
    pairs = len(refs) // 2 - 2
    lefts, rights, (near, far, own, held) = refs[:pairs], refs[pairs:2 * pairs], refs[2 * pairs:]
    turn_of, inner = pl.program_id(0), pl.program_id(1)
    size = 4 * rows // steps
    start = 0
    for left, right in zip(lefts, rights):
        width = right.shape[1]
        held[pl.ds(pl.multiple_of(inner * size, 16), size), start:start + width] = dot(left[...], right[...], (0, 0))
        start += width

    def rows_of(mask):
        return held[pl.ds(pl.multiple_of((place[0] ^ mask) * rows, 16), rows), :].astype(BF16)

    @pl.when((inner == steps - 1) & (turn_of < shards - 1))
    def _():
        near[0, :rows], near[0, rows:] = rows_of(0), rows_of(1)
        far[0, :rows], far[0, rows:] = rows_of(2), rows_of(3)

    @pl.when((inner == steps - 1) & (turn_of == shards - 1))
    def _():
        for mask in range(4):
            own[mask * rows:(mask + 1) * rows] = rows_of(mask)


def weight_grad(place, lefts, rights, rows, shards):
    width = sum(right.shape[1] for right in rights)
    length = lefts[0].shape[0]
    steps = max(1, 4 * rows // 256)
    others = max(shards - 1, 1)

    def block(turn_of, inner, place):
        step = jnp.where(turn_of == shards - 1, 0, turn_of + 1)
        return (0, lax.rem(place[3] + step, shards) * steps + inner)

    def other(turn_of, inner, place):
        return (jnp.minimum(turn_of, others - 1), 0, 0)

    near, far, own = call(
        functools.partial(weight_kernel, rows, shards, steps),
        [shape(others, 2 * rows, width), shape(others, 2 * rows, width), shape(4 * rows, width)],
        [place, *lefts, *rights], flops=2 * length * lefts[0].shape[1] * width, grid=(shards, steps),
        in_specs=[pl.BlockSpec((length, 4 * rows // steps), block)] * len(lefts) + [whole(right) for right in rights],
        out_specs=[pl.BlockSpec((1, 2 * rows, width), other)] * 2 + [pl.BlockSpec((4 * rows, width), lambda *_: (0, 0))],
        scratch=[pltpu.VMEM((4 * rows, width), F32)])
    return near, far, own


def add_two(mine, *got):
    total = mine.astype(F32)
    for value in got:
        total = total + value.astype(F32)
    return total.astype(BF16)


def reduce_weight(near, far, own, rows, shards):
    got_far = [shift(far[k - 1], k) for k in range(1, shards)]
    got_near = [shift(near[k - 1], k) for k in range(1, shards)]
    pick = lambda values, i: [value[i * rows:(i + 1) * rows] for value in values]
    cut = [own[m * rows:(m + 1) * rows] for m in range(4)]
    third = swap(add_two(cut[2], *pick(got_far, 0)), 2)
    fourth = swap(add_two(cut[3], *pick(got_far, 1)), 3)
    second = swap(add_two(cut[1], *pick(got_near, 1)), 1)
    return add_two(cut[0], *pick(got_near, 0)), second, third, fourth


def place_inner(place, *refs):
    pieces, out = refs[:-1], refs[-1]
    width = pieces[0].shape[1]
    for mask, piece in enumerate(pieces):
        out[:, pl.ds(pl.multiple_of((place[0] ^ mask) * width, 128), width)] = piece[...].astype(F32)


def place_joint(place, *refs):
    pieces, (qkv, dense) = refs[:-2], refs[-2:]
    for mask, piece in enumerate(pieces):
        head, half = place[2] ^ (mask >> 1), place[1] ^ (mask & 1)
        for out, start, size, first in ((qkv, head * 3 * HEAD + half * HEAD, HEAD, 0), (qkv, head * 3 * HEAD + 2 * HEAD + half * HALF, HALF, HEAD),
                                        (dense, head * HEAD + half * HALF, HALF, HEAD + HALF)):
            out[:, pl.ds(pl.multiple_of(start, 128), size)] = piece[:, first:first + size].astype(F32)


def output_kernel(place, context, hidden, joint, weight, keep, send):
    block = dot(context[...], joint[:, HEAD + HALF:], (1, 1)) + dot(hidden[...], weight[...], (1, 1))
    pl.when(pl.program_id(0) < 2)(lambda: keep.__setitem__(..., block.astype(BF16)))
    pl.when(pl.program_id(0) >= 2)(lambda: send.__setitem__(..., block.astype(BF16)))


def back_kernel(place, grad, inner, joint, weight, gain_one, gain_two, plain, total, keep, send, small):
    step = pl.program_id(0)
    one = dot(grad[...], joint[:, :HEAD + HALF], (1, 1))
    two = dot(inner[...], weight[...], (1, 1))
    mixed = (one * gain_one[...] + two * gain_two[...]).astype(BF16)
    pl.when(step < 2)(lambda: keep.__setitem__(..., mixed))
    pl.when(step >= 2)(lambda: send.__setitem__(..., mixed))

    @pl.when(step == 0)
    def _():
        small[...] = jnp.zeros_like(small)
        small[4:5] = total[...]

    normal = plain[...].astype(F32)
    for row, value in ((0, one * normal), (1, one), (2, two * normal), (3, two)):
        small[row:row + 1] += jnp.sum(value, axis=0, keepdims=True)
    head, half = place[2], place[1]
    joined = jnp.sum(grad[...].astype(F32), axis=0, keepdims=True)
    for first, start, size in ((0, head * 3 * HEAD + half * HEAD, HEAD), (HEAD, head * 3 * HEAD + 2 * HEAD + half * HALF, HALF)):
        small[5:6, pl.ds(pl.multiple_of(start, 128), size)] += joined[:, first:first + size]
    width = inner.shape[1]
    small[6:7, pl.ds(pl.multiple_of(place[0] * width, 128), width)] += jnp.sum(inner[...].astype(F32), axis=0, keepdims=True)


def split_kernel(place, mine, got, *outs):
    rows = outs[0].shape[0]
    for mask, out in enumerate(outs):
        here = pl.ds(pl.multiple_of((place[4] ^ mask) * rows, 16), rows)
        out[...] = (mine[here, :].astype(F32) + got[here, :].astype(F32)).astype(BF16)


def sum_rows(place, keep, send):
    got = swap(send, 1)
    span = keep.shape[0] // 2
    near = swap(add_two(keep[span:], got[span:]), 2)
    pieces = call(split_kernel, [shape(span // 4, keep.shape[1])] * 4, [place, add_two(keep[:span], got[:span]), near])
    total = add_two(pieces[0], *[level_swap(pieces[k], k) for k in (1, 2, 3)])
    return [total] + [level_swap(total, k) for k in (1, 2, 3)]


def finish_output(place, values, bias, *refs):
    pieces, out = refs[:-1], refs[-1]
    rows = pieces[0].shape[0]
    for mask, piece in enumerate(pieces):
        here = pl.ds(pl.multiple_of((place[4] ^ mask) * rows, 16), rows)
        out[here, :] = (values[here, :].astype(F32) + piece[...].astype(F32) + bias[...]).astype(BF16)


def finish_grad(place, values, grads, *refs):
    pieces, out = refs[:-1], refs[-1]
    rows = pieces[0].shape[0]
    for mask, piece in enumerate(pieces):
        here = pl.ds(pl.multiple_of((place[4] ^ mask) * rows, 16), rows)
        residual = values[here, :].astype(F32)
        centred = residual - jnp.mean(residual, axis=1, keepdims=True)
        scale = lax.rsqrt(jnp.mean(centred * centred, axis=1, keepdims=True) + EPSILON)
        normal = centred * scale
        total = piece[...].astype(F32)
        back = total - jnp.mean(total, axis=1, keepdims=True) - normal * jnp.mean(total * normal, axis=1, keepdims=True)
        out[here, :] = grads[here, :].astype(F32) + back * scale


def local(inputs, cotangent, piece_starts, positions, w_qkv, b_qkv, w_dense, w_fc1, b_fc1, w_fc2, out_bias,
          ln1_gain, ln1_bias, ln2_gain, ln2_bias):
    span, width = inputs.shape[1:]
    rows = w_fc1.shape[0]
    shards = lax.axis_size("shard")
    shard, ctx, level = lax.axis_index("shard"), lax.axis_index("ctx"), lax.axis_index("tensor")
    place = jnp.stack([ctx, ctx % 2, ctx // 2, shard, level])
    length = 4 * span
    quarter = w_fc1.shape[1] // 4
    joint = 2 * HEAD
    values, grads = inputs.reshape(span, width), cotangent.reshape(span, width)
    starts = piece_starts.reshape(-1)
    row = lambda vector: vector.reshape(1, -1)
    steps = range(1, shards)

    sent = call(prepare_joint, [shape(rows, joint)] * 4, [place, w_qkv.reshape(rows, -1), w_dense.reshape(rows, -1)])
    qd = [sent[0]] + [swap(sent[m], m) for m in (2, 3, 1)]
    qd = list(zip(qd, (0, 2, 3, 1)))

    def spread(block):
        size = span // 2
        return swap(lax.dynamic_slice(block, ((level % 2) * size, 0), (size, width)), 2)

    near_values = spread(values)
    near_grads = spread(grads)
    inner = [shape(2 * rows, quarter)] * 2 + [shape(rows, quarter)] * 4
    own, core, one_x, one_d, two_x, two_d = call(prepare_inner, inner, [place, w_fc1, w_fc2])
    core = swap(core, 1)
    one_x, one_d = swap(one_x, 2), swap(one_d, 3)
    two_x, two_d = swap(two_x, 2), swap(two_d, 3)

    joint_blocks = [(block, (0, m, 0)) for block, m in qd] + [(shift(block, -k), (0, m, k)) for block, m in qd for k in steps]
    both = [(own, 0, 0), (core, 1, 0)] + [(shift(own, -k), 0, k) for k in steps] + [(shift(core, -k), 1, k) for k in steps]

    def with_far(first, x, d):
        return ([(block, (first, m, k)) for block, m, k in both] + [(x, (0, 2, 0)), (d, (0, 3, 0))]
                + [(shift(x, -k), (0, 2, k)) for k in steps] + [(shift(d, -k), (0, 3, k)) for k in steps])

    one_blocks, two_blocks = with_far(0, one_x, one_d), with_far(rows, two_x, two_d)

    def all_tokens(block, near):
        far = level_swap(near, 1)
        return [block, near, far, swap(block, 1), swap(near, 1), swap(far, 1)]

    all_values = all_tokens(values, near_values)
    all_grads = all_tokens(grads, near_grads)
    gains = [row(ln1_gain), row(ln1_bias), row(ln2_gain), row(ln2_bias)]
    eighth = pl.BlockSpec((length // 8, width), lambda i, *_: (i, 0))
    normed_one, normed_two, plain = call(
        norm_kernel, [shape(length, width)] * 3, [place, *all_values, *gains], grid=(8,),
        in_specs=[whole(a) for a in all_values + gains], out_specs=[eighth] * 3)

    def blocked(array, count=4):
        return pl.BlockSpec((array.shape[0] // count, array.shape[1]), lambda i, *_: (i, 0))

    lanes = np.arange(HALF)
    frequency = np.where(lanes < ROT, ROPE_BASE ** (-(lanes % (ROT // 2)) * 2.0 / ROT), 0.0).astype(np.float32)[None]
    bias = row(b_qkv.reshape(-1))
    blocks = [block for block, _ in joint_blocks]
    table = shape(length, HALF, kind=F32)
    outs = [shape(length, HEAD + HALF), table, table, shape(width, joint)]
    mine, cosine, sine, w_joint = call(
        functools.partial(joint_kernel, rows, shards, [p for _, p in joint_blocks]), outs,
        [place, starts, normed_one, bias, jnp.asarray(frequency), *blocks], flops=2 * length * width * (HEAD + HALF), grid=(4,), prefetch=1,
        in_specs=[blocked(normed_one), whole(bias), whole(frequency)] + [whole(b) for b in blocks],
        out_specs=[blocked(o) for o in outs[:3]] + [whole(outs[3])])
    outs = [shape(length, HALF), shape(length, width), shape(1, width, kind=F32)]
    grad_mine, grads_full, grad_total = call(
        context_kernel, outs, [place, *all_grads, w_joint], flops=2 * length * width * HALF, grid=(8,),
        in_specs=[whole(a) for a in all_grads + [w_joint]], out_specs=[blocked(outs[0], 8), blocked(outs[1], 8), whole(outs[2])])
    context, grad_joined = call(
        attention_kernel, [shape(length, HALF), shape(length, HEAD + HALF)],
        [place, starts, mine, swap(mine, 1), grad_mine, swap(grad_mine, 1), cosine, sine], prefetch=1, flops=8 * length * length * HEAD,
        scratch=[pltpu.VMEM((length, HEAD), BF16)] * 4 + [pltpu.VMEM((length, HEAD), F32), pltpu.VMEM((length, HALF), F32)])

    bias = row(b_fc1)
    blocks = [block for block, _ in one_blocks]
    outs = [shape(length, quarter), shape(length, quarter, kind=F32), shape(width, quarter)]
    hidden, slope, fc1 = call(
        functools.partial(hidden_kernel, rows, shards, [p for _, p in one_blocks]), outs, [place, normed_two, bias, *blocks],
        flops=2 * length * width * quarter, grid=(4,), in_specs=[blocked(normed_two), whole(bias)] + [whole(b) for b in blocks],
        out_specs=[blocked(o) for o in outs[:2]] + [whole(outs[2])])
    fc2_parts = weight_grad(place, [grads_full], [hidden], rows, shards)
    qd_parts = weight_grad(place, [normed_one, grads_full], [grad_joined, context], rows, shards)
    blocks = [block for block, _ in two_blocks]
    outs = [shape(length, quarter), shape(width, quarter)]
    grad_inner, fc2 = call(
        functools.partial(inner_kernel, rows, shards, [p for _, p in two_blocks]), outs, [place, grads_full, slope, *blocks],
        flops=2 * length * width * quarter, grid=(4,), in_specs=[blocked(grads_full), blocked(slope)] + [whole(b) for b in blocks],
        out_specs=[blocked(outs[0]), whole(outs[1])])
    fc1_parts = weight_grad(place, [normed_two], [grad_inner], rows, shards)

    first_half = pl.BlockSpec((span, width), lambda i, *_: (jnp.minimum(i, 1), 0))
    second_half = pl.BlockSpec((span, width), lambda i, *_: (jnp.maximum(i - 2, 0), 0))
    args = [grad_joined, grad_inner, w_joint, fc1, gains[0], gains[2], plain, grad_total]
    keep, send, small = call(
        back_kernel, [shape(2 * span, width)] * 2 + [shape(8, width, kind=F32)], [place, *args], flops=2 * length * width * (HEAD + HALF + quarter), grid=(4,),
        in_specs=[blocked(args[0]), blocked(args[1])] + [whole(a) for a in args[2:6]] + [blocked(plain), whole(grad_total)],
        out_specs=[first_half, second_half, pl.BlockSpec((8, width), lambda *_: (0, 0))])
    pieces = sum_rows(place, keep, send)
    grad_inputs, = call(finish_grad, [shape(span, width, kind=F32)], [place, values, grads, *pieces])

    args = [context, hidden, w_joint, fc2]
    keep, send = call(
        output_kernel, [shape(2 * span, width)] * 2, [place, *args], flops=2 * length * width * (HALF + quarter), grid=(4,),
        in_specs=[blocked(context), blocked(hidden), whole(w_joint), whole(fc2)], out_specs=[first_half, second_half])
    pieces = sum_rows(place, keep, send)
    output, = call(finish_output, [shape(span, width)], [place, values, row(out_bias), *pieces])

    small = small + swap(small, 1)
    small = small + swap(small, 2)
    front = small[:4]
    front = front + level_swap(front, 1)
    front = front + level_swap(front, 2)
    small = jnp.concatenate([front, small[4:]])
    step = 1
    while step < shards:
        small = small + lax.ppermute(small, "shard", [(i, i ^ step) for i in range(shards)])
        step *= 2

    grad_w_fc2, = call(place_inner, [shape(rows, 4 * quarter, kind=F32)], [place, *reduce_weight(*fc2_parts, rows, shards)])
    grad_w_qkv, grad_w_dense = call(place_joint, [shape(rows, 6 * HEAD, kind=F32), shape(rows, 2 * HEAD, kind=F32)],
                                    [place, *reduce_weight(*qd_parts, rows, shards)])
    grad_w_fc1, = call(place_inner, [shape(rows, 4 * quarter, kind=F32)], [place, *reduce_weight(*fc1_parts, rows, shards)])
    return (
        output[None],
        grad_inputs[None],
        grad_w_qkv.reshape(w_qkv.shape),
        small[5, :b_qkv.size].reshape(b_qkv.shape),
        grad_w_dense.reshape(w_dense.shape),
        grad_w_fc1,
        small[6, :b_fc1.size],
        grad_w_fc2,
        small[4],
        small[0],
        small[1],
        small[2],
        small[3],
    )


def solution(mesh):
    rows = P(("shard", "ctx"), "tensor")
    tokens = P("shard", "ctx", None)
    heads = P(("shard", "ctx"), "tensor", None)
    in_specs = (tokens, tokens, P("shard", None), P("shard", "ctx"), heads, P("tensor", None), heads, rows, P("tensor"), rows,
                P(), P(), P(), P(), P())
    out_specs = (tokens, tokens, heads, P("tensor", None), heads, rows, P("tensor"), rows, P(), P(), P(), P(), P())
    return jax.shard_map(local, mesh=mesh, in_specs=in_specs, out_specs=out_specs, check_vma=False)
```

```python
import functools

import jax
import jax.numpy as jnp
import numpy as np
from jax import lax
from jax.experimental import pallas as pl
from jax.experimental.pallas import tpu as pltpu
from jax.sharding import PartitionSpec as P

HEAD = 256
HALF = HEAD // 2
ROT = 64
PIECE = 256
GRID = 16
PIECES = 3

EPSILON = 1e-05
ROPE_BASE = 10000.0
ORDER = (0, 2, 1, 3)
BF16 = jnp.bfloat16
F32 = jnp.float32
VMEM = pl.BlockSpec(memory_space=pltpu.VMEM)
LIMIT = 40
SMEM = pl.BlockSpec(memory_space=pltpu.SMEM)


def dot(left, right, dims):
    return lax.dot_general(left, right, ((dims[:1], dims[1:]), ((), ())), preferred_element_type=F32)


def shape(*dims, kind=BF16):
    return jax.ShapeDtypeStruct(dims, kind)


def call(kernel, outs, args, flops=0, grid=None, in_specs=None, out_specs=None, scratch=(), limit=LIMIT, prefetch=0):
    if grid is None:
        extra = dict(in_specs=[SMEM] * (1 + prefetch) + [VMEM] * (len(args) - 1 - prefetch), out_specs=[VMEM] * len(outs), scratch_shapes=scratch)
    else:
        extra = dict(grid_spec=pltpu.PrefetchScalarGridSpec(num_scalar_prefetch=1 + prefetch, grid=grid, in_specs=in_specs, out_specs=out_specs, scratch_shapes=scratch))
    size = sum(a.size * a.dtype.itemsize for a in args) + sum(int(np.prod(o.shape)) * o.dtype.itemsize for o in outs)
    return pl.pallas_call(
        kernel, out_shape=outs, compiler_params=pltpu.CompilerParams(vmem_limit_bytes=limit * 2**20),
        cost_estimate=pl.CostEstimate(flops=1, bytes_accessed=1, transcendentals=0), **extra,
    )(*args)


def whole(array):
    return pl.BlockSpec(array.shape, lambda *_: (0,) * len(array.shape))


def swap(value, mask):
    return lax.ppermute(value, "ctx", [(i, i ^ mask) for i in range(4)])


def level_swap(value, mask):
    return lax.ppermute(value, "tensor", [(i, i ^ mask) for i in range(4)])


def after(value, *others):
    return lax.optimization_barrier((value,) + others)[0]


def shift(value, step):
    size = lax.axis_size("shard")
    return lax.ppermute(value, "shard", [(i, (i + step) % size) for i in range(size)])


def part(ref, start, size):
    return ref[:, pl.ds(pl.multiple_of(start, 128), size)]


def prepare_joint(place, qkv, dense, *outs):
    for mask, out in enumerate(outs):
        head, half = place[2] ^ (mask >> 1), place[1] ^ (mask & 1)
        out[:, :HEAD] = part(qkv, head * 3 * HEAD + half * HEAD, HEAD).astype(BF16)
        out[:, HEAD:HEAD + HALF] = part(qkv, head * 3 * HEAD + 2 * HEAD + half * HALF, HALF).astype(BF16)
        out[:, HEAD + HALF:] = part(dense, head * HEAD + half * HALF, HALF).astype(BF16)


def prepare_near(place, one, two, own, core):
    rows = one.shape[0]
    for mask, out in ((0, own), (1, core)):
        @pl.when(pl.program_id(0) == mask)
        def _(out=out):
            out[:rows] = one[...].astype(BF16)
            out[rows:] = two[...].astype(BF16)


def prepare_far(place, one, two, one_x, one_d, two_x, two_d):
    for mask, first, second in ((0, one_x, two_x), (1, one_d, two_d)):
        @pl.when(pl.program_id(0) == mask)
        def _(first=first, second=second):
            first[...] = one[...].astype(BF16)
            second[...] = two[...].astype(BF16)


def assemble(place, pieces, out, rows, shards):
    for ref, first, mask, step in pieces:
        to = lax.rem(place[3] + step, shards) * 4 * rows + (place[0] ^ mask) * rows
        out[pl.ds(pl.multiple_of(to, 16), rows), :] = ref[first:first + rows, :]


def token_block(place, own, near, far, use):
    step, same = pl.program_id(0), place[4] & 1
    for k in (0, 1):
        pl.when(step == k)(lambda k=k: use(own[k * 128:(k + 1) * 128, :]))
    pl.when(step == 2 + same)(lambda: use(near[...]))
    pl.when(step == 3 - same)(lambda: use(far[...]))


def pair_kernel(place, own, near, far, out, total):
    token_block(place, own, near, far, lambda block: out.__setitem__(..., block))

    @pl.when(pl.program_id(0) == 0)
    def _():
        total[...] = jnp.sum(own[...].astype(F32), axis=0, keepdims=True)


def copy_kernel(place, own, near, far, out):
    token_block(place, own, near, far, lambda block: out.__setitem__(..., block))


def norm_kernel(place, first, second, gain_one, shift_one, gain_two, shift_two, one, two, plain):
    values = either(first, second).astype(F32)
    centred = values - jnp.mean(values, axis=1, keepdims=True)
    normal = centred * lax.rsqrt(jnp.mean(centred * centred, axis=1, keepdims=True) + EPSILON)
    one[...] = (normal * gain_one[...] + shift_one[...]).astype(BF16)
    two[...] = (normal * gain_two[...] + shift_two[...]).astype(BF16)
    plain[...] = normal.astype(BF16)


def either(first, second):
    return jnp.where(pl.program_id(0) < 2, first[...], second[...])


def global_index(place, local, block):
    index = local
    for p in range(4):
        index = jnp.where(local // block == p, local % block + (place[0] ^ ORDER[p]) * block, index)
    return index


def turn(front, cosine, sine):
    lane = lax.broadcasted_iota(jnp.int32, front.shape, 1)
    swapped = jnp.where(lane < ROT // 2, pltpu.roll(front, HALF - ROT // 2, 1), pltpu.roll(front, ROT // 2, 1))
    return front * cosine + swapped * sine


def table_kernel(place, starts, frequency, cosine, sine):
    length = cosine.shape[0]
    index = global_index(place, lax.broadcasted_iota(jnp.int32, (length, 1), 0), length // 4)
    places = index
    for j in range(PIECES):
        inside = jnp.clip(index - starts[j] + 1, 0, PIECE)
        places = places - inside + (inside + GRID - 1) // GRID
    angles = places.astype(F32) * frequency[...]
    lane = lax.broadcasted_iota(jnp.int32, cosine.shape, 1)
    cosine[...] = jnp.cos(angles)
    sine[...] = jnp.where(lane < ROT // 2, -1.0, 1.0) * jnp.sin(angles)


def joint_kernel(rows, shards, pieces, place, normed, cosine, sine, bias, *refs):
    blocks, (mine, weight) = refs[:-2], refs[-2:]

    @pl.when(pl.program_id(0) == 0)
    def _():
        assemble(place, [(ref,) + p for ref, p in zip(blocks, pieces)], weight, rows, shards)

    joined = dot(normed[...], weight[:, :HEAD + HALF], (1, 0))
    head, half = place[2], place[1]
    joined_low = joined[:, :HEAD] + part(bias, head * 3 * HEAD + half * HEAD, HEAD)
    mine[:, :HALF] = turn(joined_low[:, :HALF], cosine[...], sine[...]).astype(BF16)
    mine[:, HALF:HEAD] = joined_low[:, HALF:].astype(BF16)
    mine[:, HEAD:] = (joined[:, HEAD:] + part(bias, head * 3 * HEAD + 2 * HEAD + half * HALF, HALF)).astype(BF16)


def context_kernel(place, first, second, weight, mine):
    mine[...] = dot(either(first, second), weight[:, HEAD + HALF:], (1, 0)).astype(BF16)


def attention_kernel(place, starts, mine, got, grad_mine, grad_got, cosine, sine, context, grad, queries, keys, values, grads, acc, value_acc):
    core = place[1]
    length = mine.shape[0]
    half, block = length // 2, length // 4
    scale = HEAD ** (-0.5)
    for p in range(4):
        rows = slice(p * block, (p + 1) * block)
        first = (p * block + half) % length
        theirs = slice(first, first + block)

        @pl.when(core == 0)
        def _():
            queries[rows] = mine[rows, :HEAD]
            keys[rows] = got[theirs, :HEAD]

        @pl.when(core == 1)
        def _():
            queries[rows] = got[theirs, :HEAD]
            keys[rows] = mine[rows, :HEAD]

        values[rows, :HALF] = mine[rows, HEAD:]
        values[rows, HALF:] = got[theirs, HEAD:]
        grads[rows, :HALF] = grad_mine[rows]
        grads[rows, HALF:] = grad_got[theirs]

    def numbers(index):
        label = jnp.zeros_like(index)
        for j in range(PIECES):
            label = jnp.where((index >= starts[j]) & (index < starts[j] + PIECE), j + 1, label)
        return label

    key_index = global_index(place, lax.broadcasted_iota(jnp.int32, (1, length), 1), block)
    key_piece = numbers(key_index)
    for p in range(4):
        rows = slice(p * block, (p + 1) * block)
        query_index = lax.broadcasted_iota(jnp.int32, (block, 1), 0) + (place[0] ^ ORDER[p]) * block
        query_piece = numbers(query_index)
        allowed = (key_index <= query_index) | ((key_piece == query_piece) & (query_piece > 0))
        scores = jnp.where(allowed, dot(queries[rows], keys[...], (1, 1)) * scale, -1e30)
        weights = jnp.exp(scores - jnp.max(scores, axis=1, keepdims=True))
        weights = weights / jnp.sum(weights, axis=1, keepdims=True)
        low = weights.astype(BF16)
        context[rows] = dot(low, values[:, :HALF], (1, 0)).astype(BF16)
        term = dot(low, grads[rows, :HALF], (0, 0))
        value_acc[...] = term if p == 0 else value_acc[...] + term
        grad_weights = dot(grads[rows], values[...], (1, 1))
        centre = jnp.sum(weights * grad_weights, axis=1, keepdims=True)
        back = (weights * (grad_weights - centre)).astype(BF16)

        @pl.when(core == 0)
        def _():
            acc[rows] = dot(back, keys[...], (1, 0)) * scale

        @pl.when(core == 1)
        def _():
            term = dot(back, queries[rows], (0, 0)) * scale
            acc[...] = term if p == 0 else acc[...] + term

    grad[:, HEAD:] = value_acc[...].astype(BF16)
    grad[:, HALF:HEAD] = acc[:, HALF:].astype(BF16)
    grad[:, :HALF] = turn(acc[:, :HALF], cosine[...], -sine[...]).astype(BF16)


def hidden_kernel(rows, shards, pieces, place, normed, bias, *refs):
    blocks, (hidden, slope, weight) = refs[:-3], refs[-3:]

    @pl.when(pl.program_id(0) == 0)
    def _():
        assemble(place, [(ref,) + p for ref, p in zip(blocks, pieces)], weight, rows, shards)

    width = hidden.shape[1]
    pre = dot(normed[...], weight[...], (1, 0)) + part(bias, place[0] * width, width)
    cdf = 0.5 + 0.5 * lax.erf(pre * (0.5 ** 0.5))
    hidden[...] = (pre * cdf).astype(BF16)
    slope[...] = cdf + pre * jnp.exp(-0.5 * pre * pre) * ((0.5 / np.pi) ** 0.5)


def inner_kernel(rows, shards, pieces, place, first, second, slope, *refs):
    blocks, (inner, weight) = refs[:-2], refs[-2:]

    @pl.when(pl.program_id(0) == 0)
    def _():
        assemble(place, [(ref,) + p for ref, p in zip(blocks, pieces)], weight, rows, shards)

    inner[...] = (dot(either(first, second), weight[...], (1, 0)) * slope[...]).astype(BF16)


def weight_kernel(rows, shards, steps, counts, groups, place, *refs):
    lefts, rights, outs = refs[:sum(counts)], refs[sum(counts):sum(counts) + len(counts)], refs[sum(counts) + len(counts):]
    outs, own, held = outs[:-2], outs[-2], outs[-1]
    turn_of, inner = pl.program_id(0), pl.program_id(1)
    size = 4 * rows // steps
    start = 0
    for count, right in zip(counts, rights):
        width, length = right.shape[1], right.shape[0] // count
        block = sum(dot(lefts[k][...], right[k * length:(k + 1) * length], (0, 0)) for k in range(count))
        held[pl.ds(pl.multiple_of(inner * size, 16), size), start:start + width] = block
        start, lefts = start + width, lefts[count:]

    def rows_of(mask):
        return held[pl.ds(pl.multiple_of((place[0] ^ mask) * rows, 16), rows), :].astype(BF16)

    @pl.when((inner == steps - 1) & (turn_of < shards - 1))
    def _():
        for out, masks in zip(outs, groups):
            for k, mask in enumerate(masks):
                out[0, k * rows:(k + 1) * rows] = rows_of(mask)

    @pl.when((inner == steps - 1) & (turn_of == shards - 1))
    def _():
        for mask in range(4):
            own[mask * rows:(mask + 1) * rows] = rows_of(mask)


def weight_grad(place, lefts, rights, rows, shards, groups):
    width = sum(right.shape[1] for right in rights)
    flat = [array for arrays in lefts for array in arrays]
    steps = max(1, 4 * rows // 256)
    others = max(shards - 1, 1)

    def block(turn_of, inner, place):
        step = jnp.where(turn_of == shards - 1, 0, turn_of + 1)
        return (0, lax.rem(place[3] + step, shards) * steps + inner)

    def other(turn_of, inner, place):
        return (jnp.minimum(turn_of, others - 1), 0, 0)

    return call(
        functools.partial(weight_kernel, rows, shards, steps, [len(arrays) for arrays in lefts], groups),
        [shape(others, len(masks) * rows, width) for masks in groups] + [shape(4 * rows, width)],
        [place, *flat, *rights], flops=2 * rights[0].shape[0] * flat[0].shape[1] * width, grid=(shards, steps),
        in_specs=[pl.BlockSpec((array.shape[0], 4 * rows // steps), block) for array in flat] + [whole(right) for right in rights],
        out_specs=[pl.BlockSpec((1, len(masks) * rows, width), other) for masks in groups] + [pl.BlockSpec((4 * rows, width), lambda *_: (0, 0))],
        scratch=[pltpu.VMEM((4 * rows, width), F32)])


def gather_kernel(masks, place, own, *refs):
    got, outs = refs[:-len(masks)], refs[-len(masks):]
    rows = outs[0].shape[0]
    for k, (mask, out) in enumerate(zip(masks, outs)):
        total = own[mask * rows:(mask + 1) * rows].astype(F32)
        for array in got:
            total = total + array[k * rows:(k + 1) * rows].astype(F32)
        out[...] = total.astype(BF16)


def place_inner(place, *refs):
    pieces, out = refs[:-1], refs[-1]
    width = pieces[0].shape[1]
    for mask, piece in enumerate(pieces):
        out[:, pl.ds(pl.multiple_of((place[0] ^ mask) * width, 128), width)] = piece[...].astype(F32)


def place_joint(place, *refs):
    pieces, (qkv, dense) = refs[:-2], refs[-2:]
    for mask, piece in enumerate(pieces):
        head, half = place[2] ^ (mask >> 1), place[1] ^ (mask & 1)
        for out, start, size, first in ((qkv, head * 3 * HEAD + half * HEAD, HEAD, 0), (qkv, head * 3 * HEAD + 2 * HEAD + half * HALF, HALF, HEAD),
                                        (dense, head * HEAD + half * HALF, HALF, HEAD + HALF)):
            out[:, pl.ds(pl.multiple_of(start, 128), size)] = piece[:, first:first + size].astype(F32)


def output_kernel(place, context, hidden, joint, weight, keep, send):
    block = dot(context[...], joint[:, HEAD + HALF:], (1, 1)) + dot(hidden[...], weight[...], (1, 1))
    pl.when(pl.program_id(0) < 2)(lambda: keep.__setitem__(..., block.astype(BF16)))
    pl.when(pl.program_id(0) >= 2)(lambda: send.__setitem__(..., block.astype(BF16)))


def back_kernel(place, grad, inner, joint, weight, gain_one, gain_two, plain, total, keep, send, small):
    step = pl.program_id(0)
    one = dot(grad[...], joint[:, :HEAD + HALF], (1, 1))
    two = dot(inner[...], weight[...], (1, 1))
    mixed = (one * gain_one[...] + two * gain_two[...]).astype(BF16)
    pl.when(step < 2)(lambda: keep.__setitem__(..., mixed))
    pl.when(step >= 2)(lambda: send.__setitem__(..., mixed))

    @pl.when(step == 0)
    def _():
        small[...] = jnp.zeros_like(small)
        small[4:5] = total[...]

    normal = plain[...].astype(F32)
    for row, value in ((0, one * normal), (1, one), (2, two * normal), (3, two)):
        small[row:row + 1] += jnp.sum(value, axis=0, keepdims=True)
    head, half = place[2], place[1]
    joined = jnp.sum(grad[...].astype(F32), axis=0, keepdims=True)
    for first, start, size in ((0, head * 3 * HEAD + half * HEAD, HEAD), (HEAD, head * 3 * HEAD + 2 * HEAD + half * HALF, HALF)):
        small[5:6, pl.ds(pl.multiple_of(start, 128), size)] += joined[:, first:first + size]
    width = inner.shape[1]
    small[6:7, pl.ds(pl.multiple_of(place[0] * width, 128), width)] += jnp.sum(inner[...].astype(F32), axis=0, keepdims=True)


def core_kernel(place, keep, got, *outs):
    rows = outs[0].shape[0]
    for k, out in enumerate(outs):
        here = slice(k * rows, (k + 1) * rows)
        out[...] = (keep[here].astype(F32) + got[here].astype(F32)).astype(BF16)


def add_kernel(place, mine, got, out):
    out[...] = (mine[...].astype(F32) + got[...].astype(F32)).astype(BF16)


def finished(place, refs, use):
    outer = (place[4] == 0) | (place[4] == 3)
    for k in range(0, len(refs), 2):
        rows = refs[k].shape[0]
        here = slice(k // 2 * rows, (k // 2 + 1) * rows)
        pl.when(outer)(lambda here=here, k=k: use(here, refs[k + 1][...].astype(F32)))
        pl.when(jnp.logical_not(outer))(lambda here=here, k=k: use(here, refs[k][...].astype(F32)))


def finish_output(place, values, bias, *refs):
    out = refs[-1]

    def use(here, total):
        out[here] = (values[here].astype(F32) + total + bias[...]).astype(BF16)

    finished(place, refs[:-1], use)


def finish_grad(place, values, grads, *refs):
    out = refs[-1]

    def use(here, total):
        residual = values[here].astype(F32)
        centred = residual - jnp.mean(residual, axis=1, keepdims=True)
        scale = lax.rsqrt(jnp.mean(centred * centred, axis=1, keepdims=True) + EPSILON)
        normal = centred * scale
        back = total - jnp.mean(total, axis=1, keepdims=True) - normal * jnp.mean(total * normal, axis=1, keepdims=True)
        out[here] = grads[here].astype(F32) + back * scale

    finished(place, refs[:-1], use)


def local(inputs, cotangent, piece_starts, positions, w_qkv, b_qkv, w_dense, w_fc1, b_fc1, w_fc2, out_bias,
          ln1_gain, ln1_bias, ln2_gain, ln2_bias):
    span, width = inputs.shape[1:]
    rows = w_fc1.shape[0]
    shards = lax.axis_size("shard")
    shard, ctx, level = lax.axis_index("shard"), lax.axis_index("ctx"), lax.axis_index("tensor")
    place = jnp.stack([ctx, ctx % 2, ctx // 2, shard, level])
    length = 4 * span
    quarter = w_fc1.shape[1] // 4
    joint = 2 * HEAD
    values, grads = inputs.reshape(span, width), cotangent.reshape(span, width)
    starts = piece_starts.reshape(-1)
    row = lambda vector: vector.reshape(1, -1)
    steps = range(1, shards)

    recent = []

    def done(*values):
        recent.extend(values)
        del recent[:-8]

    def go(value):
        return after(value, *recent) if recent else value

    def half_of(block):
        size = span // 2
        return lax.dynamic_slice(block, ((level % 2) * size, 0), (size, width))

    def send(value, mask):
        return swap(go(value), mask)

    def send_y(value, sign=-1):
        value = go(value)
        return [shift(value if value.ndim == 2 else value[k - 1], sign * k) for k in steps]

    def send_z(value, mask):
        return level_swap(go(value), mask)

    def run(kernel, outs, args, **options):
        results = call(kernel, outs, [go(args[0]), *args[1:]], **options)
        done(results[0])
        return results

    def grad_of(lefts, rights, groups=((0, 1, 2, 3),)):
        results = weight_grad(go(place), lefts, rights, rows, shards, groups)
        done(results[-1])
        return results

    def columns(first):
        return [pl.BlockSpec((rows, quarter), lambda i, place: (0, place[0] ^ (first + i)))] * 2

    def blocked(array, count=4):
        return pl.BlockSpec((array.shape[0] // count, array.shape[1]), lambda i, *_: (i, 0))

    def gathered(near, near_y, x, x_y, d, d_y, first=0):
        found = [(array, (first, mask, 0)) for array, first, mask in near]
        found += [(array, (first, mask, k)) for arrays, first, mask in near_y for k, array in zip(steps, arrays)]
        for mask, array, arrays in ((2, x, x_y), (3, d, d_y)):
            found += [(array, (0, mask, 0))] + [(value, (0, mask, k)) for k, value in zip(steps, arrays)]
        return [array for array, _ in found], [piece for _, piece in found]

    def sum_shards(own, got, masks):
        return run(functools.partial(gather_kernel, masks), [shape(rows, own.shape[1])] * len(masks), [place, own, *got])

    def add(mine, got):
        return run(add_kernel, [shape(*mine.shape)], [place, mine, got])[0]

    def level_send(value, pairs):
        return lax.ppermute(go(value), "tensor", pairs)

    inward, across, outward = [(0, 1), (3, 2)], [(1, 2), (2, 1)], [(1, 0), (2, 3)]

    first_half = pl.BlockSpec((span, width), lambda i, *_: (jnp.minimum(i, 1), 0))
    second_half = pl.BlockSpec((span, width), lambda i, *_: (jnp.maximum(i - 2, 0), 0))
    halves = [first_half, second_half]
    eighth = pl.BlockSpec((span // 2, width), lambda i, *_: (i, 0))
    gains = [row(vector) for vector in (ln1_gain, ln1_bias, ln2_gain, ln2_bias)]
    lanes = np.arange(HALF)
    frequency = np.where(lanes < ROT, ROPE_BASE ** (-(lanes % (ROT // 2)) * 2.0 / ROT), 0.0).astype(np.float32)[None]

    near_values = send(half_of(values), 2)
    outs = [shape(2 * rows, quarter)] * 2
    own, core = run(prepare_near, outs, [place, w_fc1, w_fc2], grid=(2,), in_specs=columns(0), out_specs=[whole(o) for o in outs])
    own_y = send_y(own)
    core = send(core, 1)
    near_grads = send(half_of(grads), 2)
    joint_own, joint_core, joint_x, joint_d = run(
        prepare_joint, [shape(rows, joint)] * 4, [place, w_qkv.reshape(rows, -1), w_dense.reshape(rows, -1)])
    joint_core = send(joint_core, 1)
    done(core)
    core_y = send_y(core)
    done(joint_core)
    cosine, sine = run(table_kernel, [shape(length, HALF, kind=F32)] * 2, [place, starts, jnp.asarray(frequency)], prefetch=1)
    done(*own_y)
    joint_near = jnp.concatenate([joint_own, joint_core])
    joint_near_y = send_y(joint_near)
    done(near_values)
    far_values = send_z(near_values, 1)
    joint_x = send(joint_x, 2)
    outs = [shape(rows, quarter)] * 4
    one_x, one_d, two_x, two_d = run(prepare_far, outs, [place, w_fc1, w_fc2], grid=(2,), in_specs=columns(2), out_specs=[whole(o) for o in outs])
    done(near_grads)
    joint_d = send(joint_d, 3)
    done(*core_y)
    far_grads = send_z(near_grads, 1)
    done(far_values)
    values_mine, = run(copy_kernel, [shape(2 * span, width)], [place, values, near_values, far_values], grid=(4,),
                       in_specs=[whole(values), whole(near_values), whole(far_values)], out_specs=[eighth])
    values_sib = send(values_mine, 1)
    done(joint_x)
    joint_x_y = send_y(joint_x)
    done(values_sib)
    one_x = send(one_x, 2)
    outs = [shape(length, width)] * 3
    normed_one, normed_two, plain = run(norm_kernel, outs, [place, values_mine, values_sib, *gains], grid=(4,),
                                        in_specs=halves + [whole(a) for a in gains], out_specs=[blocked(o) for o in outs])
    done(*joint_near_y, joint_d)
    joint_d_y = send_y(joint_d)
    one_d = send(one_d, 3)
    done(far_grads)
    grads_mine, grad_total = run(
        pair_kernel, [shape(2 * span, width), shape(1, width, kind=F32)], [place, grads, near_grads, far_grads], grid=(4,),
        in_specs=[whole(grads), whole(near_grads), whole(far_grads)], out_specs=[eighth, pl.BlockSpec((1, width), lambda *_: (0, 0))])
    pair = (grads_mine, send(grads_mine, 1))
    done(*joint_x_y, one_x)
    two_x = send(two_x, 2)
    one_x_y = send_y(one_x)
    done(*joint_d_y, pair[1], one_d)
    two_d = send(two_d, 3)
    one_d_y = send_y(one_d)
    joint_blocks = gathered([(joint_near, 0, 0), (joint_near, rows, 1)], [(joint_near_y, 0, 0), (joint_near_y, rows, 1)], joint_x, joint_x_y, joint_d, joint_d_y)
    args = [row(b_qkv.reshape(-1)), *joint_blocks[0]]
    outs = [shape(length, HEAD + HALF), shape(width, joint)]
    mine, w_joint = run(
        functools.partial(joint_kernel, rows, shards, joint_blocks[1]), outs, [place, normed_one, cosine, sine, *args],
        flops=2 * length * width * (HEAD + HALF), grid=(4,), in_specs=[blocked(normed_one), blocked(cosine), blocked(sine)] + [whole(a) for a in args],
        out_specs=[blocked(outs[0]), whole(outs[1])])
    got = send(mine, 1)
    outs = [shape(length, HALF)]
    grad_mine, = run(context_kernel, outs, [place, *pair, w_joint], flops=2 * length * width * HALF, grid=(4,),
                     in_specs=halves + [whole(w_joint)], out_specs=[blocked(outs[0])])
    done(*one_x_y)
    grad_got = send(grad_mine, 1)
    done(two_x)
    two_x_y = send_y(two_x)
    done(got, grad_got, two_d, *one_d_y)
    two_d_y = send_y(two_d)
    one_blocks = gathered([(own, 0, 0), (core, 0, 1)], [(own_y, 0, 0), (core_y, 0, 1)], one_x, one_x_y, one_d, one_d_y)
    args = [row(b_fc1), *one_blocks[0]]
    outs = [shape(length, quarter), shape(length, quarter, kind=F32), shape(width, quarter)]
    hidden, slope, fc1 = run(
        functools.partial(hidden_kernel, rows, shards, one_blocks[1]), outs, [place, normed_two, *args],
        flops=2 * length * width * quarter, grid=(4,), in_specs=[blocked(normed_two)] + [whole(a) for a in args],
        out_specs=[blocked(o) for o in outs[:2]] + [whole(outs[2])])
    done(*two_x_y, *two_d_y)
    context, grad_joined = run(
        attention_kernel, [shape(length, HALF), shape(length, HEAD + HALF)],
        [place, starts, mine, got, grad_mine, grad_got, cosine, sine], prefetch=1, flops=8 * length * length * HEAD,
        scratch=[pltpu.VMEM((length, HEAD), BF16)] * 4 + [pltpu.VMEM((length, HEAD), F32), pltpu.VMEM((length, HALF), F32)])
    two_blocks = gathered([(own, rows, 0), (core, rows, 1)], [(own_y, rows, 0), (core_y, rows, 1)], two_x, two_x_y, two_d, two_d_y)
    outs = [shape(length, quarter), shape(width, quarter)]
    grad_inner, fc2 = run(
        functools.partial(inner_kernel, rows, shards, two_blocks[1]), outs, [place, *pair, slope, *two_blocks[0]],
        flops=2 * length * width * quarter, grid=(4,), in_specs=halves + [blocked(slope)] + [whole(a) for a in two_blocks[0]],
        out_specs=[blocked(outs[0]), whole(outs[1])])
    args = [context, hidden, w_joint, fc2]
    keep, away = run(
        output_kernel, [shape(2 * span, width)] * 2, [place, *args], flops=2 * length * width * (HALF + quarter), grid=(4,),
        in_specs=[blocked(context), blocked(hidden), whole(w_joint), whole(fc2)], out_specs=halves)
    got = send(away, 1)
    others, two_own = grad_of([pair], [hidden])
    two_got = send_y(others, 1)
    done(got)
    quarters = [shape(span // 2, width)] * 4
    out_a, out_b, away_a, away_b = run(core_kernel, quarters, [place, keep, got])
    got_a, got_b = send(away_a, 2), send(away_b, 2)
    args = [grad_joined, grad_inner, w_joint, fc1, gains[0], gains[2], plain, grad_total]
    keep, away, small = run(
        back_kernel, [shape(2 * span, width)] * 2 + [shape(8, width, kind=F32)], [place, *args], flops=2 * length * width * (HEAD + HALF + quarter), grid=(4,),
        in_specs=[blocked(args[0]), blocked(args[1])] + [whole(a) for a in args[2:6]] + [blocked(plain), whole(grad_total)],
        out_specs=halves + [pl.BlockSpec((8, width), lambda *_: (0, 0))])
    got = send(away, 1)
    done(got_a)
    out_a = add(out_a, got_a)
    got_a = level_send(out_a, inward)
    done(got)
    back_a, back_b, away_a, away_b = run(core_kernel, quarters, [place, keep, got])
    back_got_a = send(away_a, 2)
    done(got_b)
    out_b = add(out_b, got_b)
    got_b = level_send(out_b, inward)
    back_got_b = send(away_b, 2)
    others, qd_own = grad_of([(normed_one,), pair], [grad_joined, context])
    done(got_a)
    out_a = add(out_a, got_a)
    got_a = level_send(out_a, across)
    done(*two_got)
    qd_got = send_y(others, 1)
    two_a, two_b, two_c, two_e = sum_shards(two_own, two_got, (0, 1, 2, 3))
    done(got_b)
    out_b = add(out_b, got_b)
    got_b = level_send(out_b, across)
    done(back_got_a)
    back_a = add(back_a, back_got_a)
    back_got_a = level_send(back_a, inward)
    done(got_a)
    out_a = add(out_a, got_a)
    got_a = level_send(out_a, outward)
    far, near, one_own = grad_of([(normed_two,)], [grad_inner], ((2, 3), (0, 1)))
    done(back_got_b)
    back_b = add(back_b, back_got_b)
    back_got_b = level_send(back_b, inward)
    done(got_b)
    out_b = add(out_b, got_b)
    got_b = level_send(out_b, outward)
    done(got_a)
    two_c = send(two_c, 2)
    done(back_got_a)
    back_a = add(back_a, back_got_a)
    back_got_a = level_send(back_a, across)
    done(got_b)
    two_e = send(two_e, 3)
    output, = run(finish_output, [shape(span, width)], [place, values, row(out_bias), out_a, got_a, out_b, got_b])
    done(back_got_b)
    back_b = add(back_b, back_got_b)
    back_got_b = level_send(back_b, across)
    done(*qd_got)
    one_far = send_y(far, 1)
    qd_a, qd_b, qd_c, qd_e = sum_shards(qd_own, qd_got, (0, 1, 2, 3))
    done(two_c)
    one_near = send_y(near, 1)
    done(back_got_a)
    back_a = add(back_a, back_got_a)
    back_got_a = level_send(back_a, outward)
    done(two_e)
    two_b = send(two_b, 1)
    done(back_got_b)
    back_b = add(back_b, back_got_b)
    back_got_b = level_send(back_b, outward)
    done(two_b)
    grad_w_fc2, = run(place_inner, [shape(rows, 4 * quarter, kind=F32)], [place, two_a, two_b, two_c, two_e])
    qd_c = send(qd_c, 2)
    done(back_got_a)
    qd_e = send(qd_e, 3)
    done(back_got_b)
    grad_inputs, = run(finish_grad, [shape(span, width, kind=F32)], [place, values, grads, back_a, back_got_a, back_b, back_got_b])
    done(*one_far)
    one_c, one_e = sum_shards(one_own, one_far, (2, 3))
    small = small + send(small, 1)
    small = small + send(small, 2)
    qd_b = send(qd_b, 1)
    done(qd_c, small)
    one_c = send(one_c, 2)
    front = small[:4]
    front = front + send_z(front, 1)
    front = front + send_z(front, 2)
    small = jnp.concatenate([front, small[4:]])
    done(qd_e, qd_b)
    one_e = send(one_e, 3)
    qd_q, qd_d = run(place_joint, [shape(rows, 6 * HEAD, kind=F32), shape(rows, 2 * HEAD, kind=F32)], [place, qd_a, qd_b, qd_c, qd_e])
    grad_w_qkv, grad_w_dense = qd_q.reshape(w_qkv.shape), qd_d.reshape(w_dense.shape)
    done(*one_near)
    one_a, one_b = sum_shards(one_own, one_near, (0, 1))
    one_b = send(one_b, 1)
    step = 1
    while step < shards:
        small = small + lax.ppermute(go(small), "shard", [(i, i ^ step) for i in range(shards)])
        step *= 2
    done(one_b, one_c, one_e)
    grad_w_fc1, = run(place_inner, [shape(rows, 4 * quarter, kind=F32)], [place, one_a, one_b, one_c, one_e])
    return (
        output[None],
        grad_inputs[None],
        grad_w_qkv,
        small[5, :b_qkv.size].reshape(b_qkv.shape),
        grad_w_dense,
        grad_w_fc1,
        small[6, :b_fc1.size],
        grad_w_fc2,
        small[4],
        small[0],
        small[1],
        small[2],
        small[3],
    )


def solution(mesh):
    rows = P(("shard", "ctx"), "tensor")
    tokens = P("shard", "ctx", None)
    heads = P(("shard", "ctx"), "tensor", None)
    in_specs = (tokens, tokens, P("shard", None), P("shard", "ctx"), heads, P("tensor", None), heads, rows, P("tensor"), rows,
                P(), P(), P(), P(), P())
    out_specs = (tokens, tokens, heads, P("tensor", None), heads, rows, P("tensor"), rows, P(), P(), P(), P(), P())
    return jax.shard_map(local, mesh=mesh, in_specs=in_specs, out_specs=out_specs, check_vma=False)
```

```python
import functools

import jax
import jax.numpy as jnp
import numpy as np
from jax import lax
from jax.experimental import pallas as pl
from jax.experimental.pallas import tpu as pltpu
from jax.sharding import PartitionSpec as P

HEAD = 256
HALF = HEAD // 2
ROT = 64
PIECE = 256
GRID = 16
PIECES = 3

EPSILON = 1e-05
ROPE_BASE = 10000.0
ORDER = (0, 2, 1, 3)
BF16 = jnp.bfloat16
F32 = jnp.float32
VMEM = pl.BlockSpec(memory_space=pltpu.VMEM)
LIMIT = 40
SMEM = pl.BlockSpec(memory_space=pltpu.SMEM)


def dot(left, right, dims):
    return lax.dot_general(left, right, ((dims[:1], dims[1:]), ((), ())), preferred_element_type=F32)


def shape(*dims, kind=BF16):
    return jax.ShapeDtypeStruct(dims, kind)


def call(kernel, outs, args, flops=0, grid=None, in_specs=None, out_specs=None, scratch=(), limit=LIMIT, prefetch=0):
    if grid is None:
        extra = dict(in_specs=[SMEM] * (1 + prefetch) + [VMEM] * (len(args) - 1 - prefetch), out_specs=[VMEM] * len(outs), scratch_shapes=scratch)
    else:
        extra = dict(grid_spec=pltpu.PrefetchScalarGridSpec(num_scalar_prefetch=1 + prefetch, grid=grid, in_specs=in_specs, out_specs=out_specs, scratch_shapes=scratch))
    size = sum(a.size * a.dtype.itemsize for a in args) + sum(int(np.prod(o.shape)) * o.dtype.itemsize for o in outs)
    return pl.pallas_call(
        kernel, out_shape=outs, compiler_params=pltpu.CompilerParams(vmem_limit_bytes=limit * 2**20),
        cost_estimate=pl.CostEstimate(flops=1, bytes_accessed=1, transcendentals=0), **extra,
    )(*args)


def whole(array):
    return pl.BlockSpec(array.shape, lambda *_: (0,) * len(array.shape))


def swap(value, mask):
    return lax.ppermute(value, "ctx", [(i, i ^ mask) for i in range(4)])


def level_swap(value, mask):
    return lax.ppermute(value, "tensor", [(i, i ^ mask) for i in range(4)])


def after(value, *others):
    return lax.optimization_barrier((value,) + others)[0]


def shift(value, step):
    size = lax.axis_size("shard")
    return lax.ppermute(value, "shard", [(i, (i + step) % size) for i in range(size)])


def part(ref, start, size):
    return ref[:, pl.ds(pl.multiple_of(start, 128), size)]


def prepare_joint(place, qkv, dense, *outs):
    for mask, out in enumerate(outs):
        head, half = place[2] ^ (mask >> 1), place[1] ^ (mask & 1)
        out[:, :HEAD] = part(qkv, head * 3 * HEAD + half * HEAD, HEAD).astype(BF16)
        out[:, HEAD:HEAD + HALF] = part(qkv, head * 3 * HEAD + 2 * HEAD + half * HALF, HALF).astype(BF16)
        out[:, HEAD + HALF:] = part(dense, head * HEAD + half * HALF, HALF).astype(BF16)


def prepare_near(place, one, two, own, core):
    rows = one.shape[0]
    for mask, out in ((0, own), (1, core)):
        @pl.when(pl.program_id(0) == mask)
        def _(out=out):
            out[:rows] = one[...].astype(BF16)
            out[rows:] = two[...].astype(BF16)


def prepare_far(place, one, two, one_x, one_d, two_x, two_d):
    for mask, first, second in ((0, one_x, two_x), (1, one_d, two_d)):
        @pl.when(pl.program_id(0) == mask)
        def _(first=first, second=second):
            first[...] = one[...].astype(BF16)
            second[...] = two[...].astype(BF16)


def assemble(place, pieces, out, rows, shards):
    for ref, first, mask, step in pieces:
        to = lax.rem(place[3] + step, shards) * 4 * rows + (place[0] ^ mask) * rows
        out[pl.ds(pl.multiple_of(to, 16), rows), :] = ref[first:first + rows, :]


def token_block(place, own, near, far, use):
    step, same = pl.program_id(0), place[4] & 1
    for k in (0, 1):
        pl.when(step == k)(lambda k=k: use(own[k * 128:(k + 1) * 128, :]))
    pl.when(step == 2 + same)(lambda: use(near[...]))
    pl.when(step == 3 - same)(lambda: use(far[...]))


def pair_kernel(place, own, near, far, out, total):
    token_block(place, own, near, far, lambda block: out.__setitem__(..., block))

    @pl.when(pl.program_id(0) == 0)
    def _():
        total[...] = jnp.sum(own[...].astype(F32), axis=0, keepdims=True)


def copy_kernel(place, own, near, far, out):
    token_block(place, own, near, far, lambda block: out.__setitem__(..., block))


def norm_kernel(place, first, second, gain_one, shift_one, gain_two, shift_two, one, two, plain):
    values = either(first, second).astype(F32)
    centred = values - jnp.mean(values, axis=1, keepdims=True)
    normal = centred * lax.rsqrt(jnp.mean(centred * centred, axis=1, keepdims=True) + EPSILON)
    one[...] = (normal * gain_one[...] + shift_one[...]).astype(BF16)
    two[...] = (normal * gain_two[...] + shift_two[...]).astype(BF16)
    plain[...] = normal.astype(BF16)


def either(first, second):
    return jnp.where(pl.program_id(0) < 2, first[...], second[...])


def global_index(place, local, block):
    index = local
    for p in range(4):
        index = jnp.where(local // block == p, local % block + (place[0] ^ ORDER[p]) * block, index)
    return index


def turn(front, cosine, sine):
    lane = lax.broadcasted_iota(jnp.int32, front.shape, 1)
    swapped = jnp.where(lane < ROT // 2, pltpu.roll(front, HALF - ROT // 2, 1), pltpu.roll(front, ROT // 2, 1))
    return front * cosine + swapped * sine


def table_kernel(place, starts, frequency, cosine, sine):
    length = cosine.shape[0]
    index = global_index(place, lax.broadcasted_iota(jnp.int32, (length, 1), 0), length // 4)
    places = index
    for j in range(PIECES):
        inside = jnp.clip(index - starts[j] + 1, 0, PIECE)
        places = places - inside + (inside + GRID - 1) // GRID
    angles = places.astype(F32) * frequency[...]
    lane = lax.broadcasted_iota(jnp.int32, cosine.shape, 1)
    cosine[...] = jnp.cos(angles)
    sine[...] = jnp.where(lane < ROT // 2, -1.0, 1.0) * jnp.sin(angles)


def joint_kernel(rows, shards, pieces, place, normed, cosine, sine, bias, *refs):
    blocks, (mine, weight) = refs[:-2], refs[-2:]

    @pl.when(pl.program_id(0) == 0)
    def _():
        assemble(place, [(ref,) + p for ref, p in zip(blocks, pieces)], weight, rows, shards)

    joined = dot(normed[...], weight[:, :HEAD + HALF], (1, 0))
    head, half = place[2], place[1]
    joined_low = joined[:, :HEAD] + part(bias, head * 3 * HEAD + half * HEAD, HEAD)
    mine[:, :HALF] = turn(joined_low[:, :HALF], cosine[...], sine[...]).astype(BF16)
    mine[:, HALF:HEAD] = joined_low[:, HALF:].astype(BF16)
    mine[:, HEAD:] = (joined[:, HEAD:] + part(bias, head * 3 * HEAD + 2 * HEAD + half * HALF, HALF)).astype(BF16)


def context_kernel(place, first, second, weight, mine):
    mine[...] = dot(either(first, second), weight[:, HEAD + HALF:], (1, 0)).astype(BF16)


def attention_kernel(place, starts, mine, got, grad_mine, grad_got, cosine, sine, context, grad, queries, keys, values, grads, acc, value_acc):
    core = place[1]
    length = mine.shape[0]
    half, block = length // 2, length // 4
    scale = HEAD ** (-0.5)
    for p in range(4):
        rows = slice(p * block, (p + 1) * block)
        first = (p * block + half) % length
        theirs = slice(first, first + block)

        @pl.when(core == 0)
        def _():
            queries[rows] = mine[rows, :HEAD]
            keys[rows] = got[theirs, :HEAD]

        @pl.when(core == 1)
        def _():
            queries[rows] = got[theirs, :HEAD]
            keys[rows] = mine[rows, :HEAD]

        values[rows, :HALF] = mine[rows, HEAD:]
        values[rows, HALF:] = got[theirs, HEAD:]
        grads[rows, :HALF] = grad_mine[rows]
        grads[rows, HALF:] = grad_got[theirs]

    def numbers(index):
        label = jnp.zeros_like(index)
        for j in range(PIECES):
            label = jnp.where((index >= starts[j]) & (index < starts[j] + PIECE), j + 1, label)
        return label

    key_index = global_index(place, lax.broadcasted_iota(jnp.int32, (1, length), 1), block)
    key_piece = numbers(key_index)
    for p in range(4):
        rows = slice(p * block, (p + 1) * block)
        query_index = lax.broadcasted_iota(jnp.int32, (block, 1), 0) + (place[0] ^ ORDER[p]) * block
        query_piece = numbers(query_index)
        allowed = (key_index <= query_index) | ((key_piece == query_piece) & (query_piece > 0))
        scores = jnp.where(allowed, dot(queries[rows], keys[...], (1, 1)) * scale, -1e30)
        weights = jnp.exp(scores - jnp.max(scores, axis=1, keepdims=True))
        weights = weights / jnp.sum(weights, axis=1, keepdims=True)
        low = weights.astype(BF16)
        context[rows] = dot(low, values[:, :HALF], (1, 0)).astype(BF16)
        term = dot(low, grads[rows, :HALF], (0, 0))
        value_acc[...] = term if p == 0 else value_acc[...] + term
        grad_weights = dot(grads[rows], values[...], (1, 1))
        centre = jnp.sum(weights * grad_weights, axis=1, keepdims=True)
        back = (weights * (grad_weights - centre)).astype(BF16)

        @pl.when(core == 0)
        def _():
            acc[rows] = dot(back, keys[...], (1, 0)) * scale

        @pl.when(core == 1)
        def _():
            term = dot(back, queries[rows], (0, 0)) * scale
            acc[...] = term if p == 0 else acc[...] + term

    grad[:, HEAD:] = value_acc[...].astype(BF16)
    grad[:, HALF:HEAD] = acc[:, HALF:].astype(BF16)
    grad[:, :HALF] = turn(acc[:, :HALF], cosine[...], -sine[...]).astype(BF16)


def hidden_kernel(rows, shards, pieces, place, normed, bias, *refs):
    blocks, (hidden, slope, weight) = refs[:-3], refs[-3:]

    @pl.when(pl.program_id(0) == 0)
    def _():
        assemble(place, [(ref,) + p for ref, p in zip(blocks, pieces)], weight, rows, shards)

    width = hidden.shape[1]
    pre = dot(normed[...], weight[...], (1, 0)) + part(bias, place[0] * width, width)
    cdf = 0.5 + 0.5 * lax.erf(pre * (0.5 ** 0.5))
    hidden[...] = (pre * cdf).astype(BF16)
    slope[...] = cdf + pre * jnp.exp(-0.5 * pre * pre) * ((0.5 / np.pi) ** 0.5)


def inner_kernel(rows, shards, pieces, place, first, second, slope, *refs):
    blocks, (inner, weight) = refs[:-2], refs[-2:]

    @pl.when(pl.program_id(0) == 0)
    def _():
        assemble(place, [(ref,) + p for ref, p in zip(blocks, pieces)], weight, rows, shards)

    inner[...] = (dot(either(first, second), weight[...], (1, 0)) * slope[...]).astype(BF16)


def weight_kernel(rows, shards, steps, counts, groups, own_groups, place, *refs):
    lefts, rights, outs = refs[:sum(counts)], refs[sum(counts):sum(counts) + len(counts)], refs[sum(counts) + len(counts):]
    outs, owns, held = outs[:len(groups)], outs[len(groups):-1], outs[-1]
    turn_of, inner = pl.program_id(0), pl.program_id(1)
    size = 4 * rows // steps
    start = 0
    for count, right in zip(counts, rights):
        width, length = right.shape[1], right.shape[0] // count
        block = sum(dot(lefts[k][...], right[k * length:(k + 1) * length], (0, 0)) for k in range(count))
        held[pl.ds(pl.multiple_of(inner * size, 16), size), start:start + width] = block
        start, lefts = start + width, lefts[count:]

    def rows_of(mask):
        return held[pl.ds(pl.multiple_of((place[0] ^ mask) * rows, 16), rows), :].astype(BF16)

    @pl.when((inner == steps - 1) & (turn_of < shards - 1))
    def _():
        for out, masks in zip(outs, groups):
            for k, mask in enumerate(masks):
                out[0, k * rows:(k + 1) * rows] = rows_of(mask)

    @pl.when((inner == steps - 1) & (turn_of == shards - 1))
    def _():
        for out, masks in zip(owns, own_groups):
            for k, mask in enumerate(masks):
                out[k * rows:(k + 1) * rows] = rows_of(mask)


def weight_grad(place, lefts, rights, rows, shards, groups, own_groups):
    width = sum(right.shape[1] for right in rights)
    flat = [array for arrays in lefts for array in arrays]
    steps = max(1, 4 * rows // 256)
    others = max(shards - 1, 1)

    def block(turn_of, inner, place):
        step = jnp.where(turn_of == shards - 1, 0, turn_of + 1)
        return (0, lax.rem(place[3] + step, shards) * steps + inner)

    def other(turn_of, inner, place):
        return (jnp.minimum(turn_of, others - 1), 0, 0)

    return call(
        functools.partial(weight_kernel, rows, shards, steps, [len(arrays) for arrays in lefts], groups, own_groups),
        [shape(others, len(masks) * rows, width) for masks in groups] + [shape(len(masks) * rows, width) for masks in own_groups],
        [place, *flat, *rights], flops=2 * rights[0].shape[0] * flat[0].shape[1] * width, grid=(shards, steps),
        in_specs=[pl.BlockSpec((array.shape[0], 4 * rows // steps), block) for array in flat] + [whole(right) for right in rights],
        out_specs=[pl.BlockSpec((1, len(masks) * rows, width), other) for masks in groups]
        + [pl.BlockSpec((len(masks) * rows, width), lambda *_: (0, 0)) for masks in own_groups],
        scratch=[pltpu.VMEM((4 * rows, width), F32)])


def total_of(own, first, got, start, rows):
    total = own[first:first + rows].astype(F32)
    for array in got:
        total = total + array[start:start + rows].astype(F32)
    return total.astype(BF16)


def sum_kernel(first, place, own, *refs):
    refs[-1][...] = total_of(own, first, refs[:-1], 0, refs[-1].shape[0])


def sum_two_kernel(place, keep, give, *refs):
    got, (first, second, away) = refs[:-3], refs[-3:]
    rows, half = first.shape[0], len(got) // 2
    for own, arrays, out, start in ((keep, got[:half], first, 0), (give, got[half:], second, rows)):
        out[...] = total_of(own, 0, arrays, 0, rows)
        away[start:start + rows] = total_of(own, rows, arrays, rows, rows)


def place_inner(column, starts, place, *refs):
    pieces, out = refs[:-1], refs[-1]
    rows, width = out.shape[0], out.shape[1] // 4
    for mask, (piece, start) in enumerate(zip(pieces, starts)):
        out[:, pl.ds(pl.multiple_of((place[0] ^ mask) * width, 128), width)] = piece[start:start + rows, column:column + width].astype(F32)


def place_joint(place, *refs):
    pieces, (qkv, dense) = refs[:-2], refs[-2:]
    for mask, piece in enumerate(pieces):
        head, half = place[2] ^ (mask >> 1), place[1] ^ (mask & 1)
        for out, start, size, first in ((qkv, head * 3 * HEAD + half * HEAD, HEAD, 0), (qkv, head * 3 * HEAD + 2 * HEAD + half * HALF, HALF, HEAD),
                                        (dense, head * HEAD + half * HALF, HALF, HEAD + HALF)):
            out[:, pl.ds(pl.multiple_of(start, 128), size)] = piece[:, first:first + size].astype(F32)


def output_kernel(place, context, hidden, joint, weight, keep, send):
    block = dot(context[...], joint[:, HEAD + HALF:], (1, 1)) + dot(hidden[...], weight[...], (1, 1))
    pl.when(pl.program_id(0) < 2)(lambda: keep.__setitem__(..., block.astype(BF16)))
    pl.when(pl.program_id(0) >= 2)(lambda: send.__setitem__(..., block.astype(BF16)))


def back_kernel(place, grad, inner, joint, weight, gain_one, gain_two, plain, total, keep, send, small):
    step = pl.program_id(0)
    one = dot(grad[...], joint[:, :HEAD + HALF], (1, 1))
    two = dot(inner[...], weight[...], (1, 1))
    mixed = (one * gain_one[...] + two * gain_two[...]).astype(BF16)
    pl.when(step < 2)(lambda: keep.__setitem__(..., mixed))
    pl.when(step >= 2)(lambda: send.__setitem__(..., mixed))

    @pl.when(step == 0)
    def _():
        small[...] = jnp.zeros_like(small)
        small[4:5] = total[...]

    normal = plain[...].astype(F32)
    for row, value in ((0, one * normal), (1, one), (2, two * normal), (3, two)):
        small[row:row + 1] += jnp.sum(value, axis=0, keepdims=True)
    head, half = place[2], place[1]
    joined = jnp.sum(grad[...].astype(F32), axis=0, keepdims=True)
    for first, start, size in ((0, head * 3 * HEAD + half * HEAD, HEAD), (HEAD, head * 3 * HEAD + 2 * HEAD + half * HALF, HALF)):
        small[5:6, pl.ds(pl.multiple_of(start, 128), size)] += joined[:, first:first + size]
    width = inner.shape[1]
    small[6:7, pl.ds(pl.multiple_of(place[0] * width, 128), width)] += jnp.sum(inner[...].astype(F32), axis=0, keepdims=True)


def core_kernel(place, keep, got, *outs):
    rows = outs[0].shape[0]
    for k, out in enumerate(outs):
        here = slice(k * rows, (k + 1) * rows)
        out[...] = (keep[here].astype(F32) + got[here].astype(F32)).astype(BF16)


def add_kernel(place, mine, got, out):
    out[...] = (mine[...].astype(F32) + got[...].astype(F32)).astype(BF16)


def finished(place, refs, use):
    outer = (place[4] == 0) | (place[4] == 3)
    for k in range(0, len(refs), 2):
        rows = refs[k].shape[0]
        here = slice(k // 2 * rows, (k // 2 + 1) * rows)
        pl.when(outer)(lambda here=here, k=k: use(here, refs[k + 1][...].astype(F32)))
        pl.when(jnp.logical_not(outer))(lambda here=here, k=k: use(here, refs[k][...].astype(F32)))


def finish_output(place, values, bias, *refs):
    out = refs[-1]

    def use(here, total):
        out[here] = (values[here].astype(F32) + total + bias[...]).astype(BF16)

    finished(place, refs[:-1], use)


def finish_grad(place, values, grads, *refs):
    out = refs[-1]

    def use(here, total):
        residual = values[here].astype(F32)
        centred = residual - jnp.mean(residual, axis=1, keepdims=True)
        scale = lax.rsqrt(jnp.mean(centred * centred, axis=1, keepdims=True) + EPSILON)
        normal = centred * scale
        back = total - jnp.mean(total, axis=1, keepdims=True) - normal * jnp.mean(total * normal, axis=1, keepdims=True)
        out[here] = grads[here].astype(F32) + back * scale

    finished(place, refs[:-1], use)


def local(inputs, cotangent, piece_starts, positions, w_qkv, b_qkv, w_dense, w_fc1, b_fc1, w_fc2, out_bias,
          ln1_gain, ln1_bias, ln2_gain, ln2_bias):
    span, width = inputs.shape[1:]
    rows = w_fc1.shape[0]
    shards = lax.axis_size("shard")
    shard, ctx, level = lax.axis_index("shard"), lax.axis_index("ctx"), lax.axis_index("tensor")
    place = jnp.stack([ctx, ctx % 2, ctx // 2, shard, level])
    length = 4 * span
    quarter = w_fc1.shape[1] // 4
    joint = 2 * HEAD
    values, grads = inputs.reshape(span, width), cotangent.reshape(span, width)
    starts = piece_starts.reshape(-1)
    row = lambda vector: vector.reshape(1, -1)
    steps = range(1, shards)

    recent = []

    def done(*values):
        recent.extend(values)
        del recent[:-8]

    def go(value):
        return after(value, *recent) if recent else value

    def half_of(block):
        size = span // 2
        return lax.dynamic_slice(block, ((level % 2) * size, 0), (size, width))

    def send(value, mask):
        return swap(go(value), mask)

    def send_y(value, sign=-1):
        value = go(value)
        return [shift(value if value.ndim == 2 else value[k - 1], sign * k) for k in steps]

    def send_z(value, mask):
        return level_swap(go(value), mask)

    def run(kernel, outs, args, **options):
        results = call(kernel, outs, [go(args[0]), *args[1:]], **options)
        done(results[0])
        return results

    def grad_of(lefts, rights, groups, own_groups):
        results = weight_grad(go(place), lefts, rights, rows, shards, groups, own_groups)
        done(results[-1])
        return results

    def columns(first):
        return [pl.BlockSpec((rows, quarter), lambda i, place: (0, place[0] ^ (first + i)))] * 2

    def blocked(array, count=4):
        return pl.BlockSpec((array.shape[0] // count, array.shape[1]), lambda i, *_: (i, 0))

    def gathered(near, near_y, x, x_y, d, d_y, first=0):
        found = [(array, (first, mask, 0)) for array, first, mask in near]
        found += [(array, (first, mask, k)) for arrays, first, mask in near_y for k, array in zip(steps, arrays)]
        for mask, array, arrays in ((2, x, x_y), (3, d, d_y)):
            found += [(array, (0, mask, 0))] + [(value, (0, mask, k)) for k, value in zip(steps, arrays)]
        return [array for array, _ in found], [piece for _, piece in found]

    def add(mine, got):
        return run(add_kernel, [shape(*mine.shape)], [place, mine, got])[0]

    def level_send(value, pairs):
        return lax.ppermute(go(value), "tensor", pairs)

    inward, across, outward = [(0, 1), (3, 2)], [(1, 2), (2, 1)], [(1, 0), (2, 3)]

    first_half = pl.BlockSpec((span, width), lambda i, *_: (jnp.minimum(i, 1), 0))
    second_half = pl.BlockSpec((span, width), lambda i, *_: (jnp.maximum(i - 2, 0), 0))
    halves = [first_half, second_half]
    eighth = pl.BlockSpec((span // 2, width), lambda i, *_: (i, 0))
    gains = [row(vector) for vector in (ln1_gain, ln1_bias, ln2_gain, ln2_bias)]
    lanes = np.arange(HALF)
    frequency = np.where(lanes < ROT, ROPE_BASE ** (-(lanes % (ROT // 2)) * 2.0 / ROT), 0.0).astype(np.float32)[None]

    near_values = send(half_of(values), 2)
    outs = [shape(2 * rows, quarter)] * 2
    own, core = run(prepare_near, outs, [place, w_fc1, w_fc2], grid=(2,), in_specs=columns(0), out_specs=[whole(o) for o in outs])
    own_y = send_y(own)
    core = send(core, 1)
    near_grads = send(half_of(grads), 2)
    joint_own, joint_core, joint_x, joint_d = run(
        prepare_joint, [shape(rows, joint)] * 4, [place, w_qkv.reshape(rows, -1), w_dense.reshape(rows, -1)])
    joint_core = send(joint_core, 1)
    done(core)
    core_y = send_y(core)
    done(joint_core)
    cosine, sine = run(table_kernel, [shape(length, HALF, kind=F32)] * 2, [place, starts, jnp.asarray(frequency)], prefetch=1)
    done(*own_y)
    joint_near = jnp.concatenate([joint_own, joint_core])
    joint_near_y = send_y(joint_near)
    done(near_values)
    far_values = send_z(near_values, 1)
    joint_x = send(joint_x, 2)
    outs = [shape(rows, quarter)] * 4
    one_x, one_d, two_x, two_d = run(prepare_far, outs, [place, w_fc1, w_fc2], grid=(2,), in_specs=columns(2), out_specs=[whole(o) for o in outs])
    done(near_grads)
    joint_d = send(joint_d, 3)
    done(*core_y)
    far_grads = send_z(near_grads, 1)
    done(far_values)
    values_mine, = run(copy_kernel, [shape(2 * span, width)], [place, values, near_values, far_values], grid=(4,),
                       in_specs=[whole(values), whole(near_values), whole(far_values)], out_specs=[eighth])
    values_sib = send(values_mine, 1)
    done(joint_x)
    joint_x_y = send_y(joint_x)
    done(values_sib)
    one_x = send(one_x, 2)
    outs = [shape(length, width)] * 3
    normed_one, normed_two, plain = run(norm_kernel, outs, [place, values_mine, values_sib, *gains], grid=(4,),
                                        in_specs=halves + [whole(a) for a in gains], out_specs=[blocked(o) for o in outs])
    done(*joint_near_y, joint_d)
    joint_d_y = send_y(joint_d)
    one_d = send(one_d, 3)
    done(far_grads)
    grads_mine, grad_total = run(
        pair_kernel, [shape(2 * span, width), shape(1, width, kind=F32)], [place, grads, near_grads, far_grads], grid=(4,),
        in_specs=[whole(grads), whole(near_grads), whole(far_grads)], out_specs=[eighth, pl.BlockSpec((1, width), lambda *_: (0, 0))])
    pair = (grads_mine, send(grads_mine, 1))
    done(*joint_x_y, one_x)
    two_x = send(two_x, 2)
    one_x_y = send_y(one_x)
    done(*joint_d_y, pair[1], one_d)
    two_d = send(two_d, 3)
    one_d_y = send_y(one_d)
    joint_blocks = gathered([(joint_near, 0, 0), (joint_near, rows, 1)], [(joint_near_y, 0, 0), (joint_near_y, rows, 1)], joint_x, joint_x_y, joint_d, joint_d_y)
    args = [row(b_qkv.reshape(-1)), *joint_blocks[0]]
    outs = [shape(length, HEAD + HALF), shape(width, joint)]
    mine, w_joint = run(
        functools.partial(joint_kernel, rows, shards, joint_blocks[1]), outs, [place, normed_one, cosine, sine, *args],
        flops=2 * length * width * (HEAD + HALF), grid=(4,), in_specs=[blocked(normed_one), blocked(cosine), blocked(sine)] + [whole(a) for a in args],
        out_specs=[blocked(outs[0]), whole(outs[1])])
    got = send(mine, 1)
    outs = [shape(length, HALF)]
    grad_mine, = run(context_kernel, outs, [place, *pair, w_joint], flops=2 * length * width * HALF, grid=(4,),
                     in_specs=halves + [whole(w_joint)], out_specs=[blocked(outs[0])])
    done(*one_x_y)
    grad_got = send(grad_mine, 1)
    done(two_x)
    two_x_y = send_y(two_x)
    done(got, grad_got, two_d, *one_d_y)
    two_d_y = send_y(two_d)
    one_blocks = gathered([(own, 0, 0), (core, 0, 1)], [(own_y, 0, 0), (core_y, 0, 1)], one_x, one_x_y, one_d, one_d_y)
    args = [row(b_fc1), *one_blocks[0]]
    outs = [shape(length, quarter), shape(length, quarter, kind=F32), shape(width, quarter)]
    hidden, slope, fc1 = run(
        functools.partial(hidden_kernel, rows, shards, one_blocks[1]), outs, [place, normed_two, *args],
        flops=2 * length * width * quarter, grid=(4,), in_specs=[blocked(normed_two)] + [whole(a) for a in args],
        out_specs=[blocked(o) for o in outs[:2]] + [whole(outs[2])])
    context, grad_joined = run(
        attention_kernel, [shape(length, HALF), shape(length, HEAD + HALF)],
        [place, starts, mine, got, grad_mine, grad_got, cosine, sine], prefetch=1, flops=8 * length * length * HEAD,
        scratch=[pltpu.VMEM((length, HEAD), BF16)] * 4 + [pltpu.VMEM((length, HEAD), F32), pltpu.VMEM((length, HALF), F32)])
    done(*two_x_y, *two_d_y)
    two_blocks = gathered([(own, rows, 0), (core, rows, 1)], [(own_y, rows, 0), (core_y, rows, 1)], two_x, two_x_y, two_d, two_d_y)
    outs = [shape(length, quarter), shape(width, quarter)]
    grad_inner, fc2 = run(
        functools.partial(inner_kernel, rows, shards, two_blocks[1]), outs, [place, *pair, slope, *two_blocks[0]],
        flops=2 * length * width * quarter, grid=(4,), in_specs=halves + [blocked(slope)] + [whole(a) for a in two_blocks[0]],
        out_specs=[blocked(outs[0]), whole(outs[1])])
    args = [context, hidden, w_joint, fc2]
    keep, away = run(
        output_kernel, [shape(2 * span, width)] * 2, [place, *args], flops=2 * length * width * (HALF + quarter), grid=(4,),
        in_specs=[blocked(context), blocked(hidden), whole(w_joint), whole(fc2)], out_specs=halves)
    got = send(away, 1)
    two_keep_y, two_give_y, two_keep, two_give = grad_of([pair], [hidden], ((0, 2), (1, 3)), ((0, 2), (1, 3)))
    two_give, two_give_y = send(two_give, 1), send(two_give_y, 1)
    done(got, two_give, two_give_y)
    quarters = [shape(span // 2, width)] * 4
    out_a, out_b, away_a, away_b = run(core_kernel, quarters, [place, keep, got])

    got_a = send(away_a, 2)
    two_keep_y = send_y(two_keep_y, 1)
    args = [grad_joined, grad_inner, w_joint, fc1, gains[0], gains[2], plain, grad_total]
    keep, away, small = run(
        back_kernel, [shape(2 * span, width)] * 2 + [shape(8, width, kind=F32)], [place, *args], flops=2 * length * width * (HEAD + HALF + quarter), grid=(4,),
        in_specs=[blocked(args[0]), blocked(args[1])] + [whole(a) for a in args[2:6]] + [blocked(plain), whole(grad_total)],
        out_specs=halves + [pl.BlockSpec((8, width), lambda *_: (0, 0))])
    done(got_a, *two_keep_y)
    out_a = add(out_a, got_a)

    got_a = level_send(out_a, inward)
    got_b = send(away_b, 2)
    two_give_y = send_y(two_give_y, 1)
    got, small_got = send(away, 1), send(small, 1)
    far_y, near_y, give_y, rest, rest_give = grad_of(
        [(normed_one,), pair, (normed_two,)], [grad_joined, context, grad_inner], ((2,), (0,), (3, 1)), ((2, 0), (3, 1)))
    done(small_got, got_a, got_b, *two_give_y, got)
    back_a, back_b, back_away_a, back_away_b = run(core_kernel, quarters, [place, keep, got])
    out_b, out_a = add(out_b, got_b), add(out_a, got_a)

    got_b = level_send(out_b, inward)
    got_a = level_send(out_a, across)
    back_got_a = send(back_away_a, 2)
    far_y = send_y(far_y, 1)
    give_y = send(give_y, 1)
    two_first, two_second, two_away = run(sum_two_kernel, [shape(rows, quarter)] * 2 + [shape(2 * rows, quarter)],
                                          [place, two_keep, two_give, *two_keep_y, *two_give_y])
    done(back_got_a, got_b, got_a, *far_y, give_y)
    back_a, out_b, out_a = add(back_a, back_got_a), add(out_b, got_b), add(out_a, got_a)

    back_got_a = level_send(back_a, inward)
    got_b = level_send(out_b, across)
    got_a = level_send(out_a, outward)
    back_got_b = send(back_away_b, 2)
    give_far_y = send_y(give_y[:, :rows], 1)
    wide = [shape(rows, joint + quarter)]
    away_one, = run(functools.partial(sum_kernel, 0), wide, [place, rest, *far_y])
    done(back_got_b, back_got_a, got_b, got_a, *give_far_y)
    back_b, back_a, out_b = add(back_b, back_got_b), add(back_a, back_got_a), add(out_b, got_b)

    back_got_b = level_send(back_b, inward)
    back_got_a = level_send(back_a, across)
    got_b = level_send(out_b, outward)
    two_got = send(two_away, 2)
    near_y = send_y(near_y, 1)
    done(two_got, back_got_b, back_got_a, got_b, *near_y)
    back_b, back_a = add(back_b, back_got_b), add(back_a, back_got_a)

    back_got_b = level_send(back_b, across)
    back_got_a = level_send(back_a, outward)
    got_one = send(away_one, 2)
    give_near_y = send_y(give_y[:, rows:], 1)
    rest_give = send(rest_give, 1)
    full = [shape(rows, 4 * quarter, kind=F32)]
    grad_w_fc2, = run(functools.partial(place_inner, 0, (0, 0, 0, rows)), full, [place, two_first, two_second, two_got, two_got])
    output, = run(finish_output, [shape(span, width)], [place, values, row(out_bias), out_a, got_a, out_b, got_b])
    first, = run(functools.partial(sum_kernel, rows), wide, [place, rest, *near_y])
    small = small + small_got
    done(got_one, back_got_b, back_got_a, *give_near_y, rest_give)
    back_b = add(back_b, back_got_b)

    back_got_b = level_send(back_b, outward)
    away_two, = run(functools.partial(sum_kernel, 0), wide, [place, rest_give, *give_far_y])
    got_two = send(away_two, 2)
    front = [send_z(small[:4], mask) for mask in (1, 2, 3)]
    second, = run(functools.partial(sum_kernel, rows), wide, [place, rest_give, *give_near_y])
    done(got_two, back_got_b, *front)
    small = jnp.concatenate([sum(front, small[:4]), small[4:]])
    small = small + send(small, 2)
    pieces = [first, second, got_one, got_two]
    qd_q, qd_d = run(place_joint, [shape(rows, 6 * HEAD, kind=F32), shape(rows, 2 * HEAD, kind=F32)], [place, *pieces])
    grad_w_qkv, grad_w_dense = qd_q.reshape(w_qkv.shape), qd_d.reshape(w_dense.shape)
    step = 1
    while step < shards:
        small = small + lax.ppermute(small, "shard", [(i, i ^ step) for i in range(shards)])
        step *= 2
    grad_inputs, = run(finish_grad, [shape(span, width, kind=F32)], [place, values, grads, back_a, back_got_a, back_b, back_got_b])
    grad_w_fc1, = run(functools.partial(place_inner, joint, (0, 0, 0, 0)), full, [place, *pieces])
    return (
        output[None],
        grad_inputs[None],
        grad_w_qkv,
        small[5, :b_qkv.size].reshape(b_qkv.shape),
        grad_w_dense,
        grad_w_fc1,
        small[6, :b_fc1.size],
        grad_w_fc2,
        small[4],
        small[0],
        small[1],
        small[2],
        small[3],
    )


def solution(mesh):
    rows = P(("shard", "ctx"), "tensor")
    tokens = P("shard", "ctx", None)
    heads = P(("shard", "ctx"), "tensor", None)
    in_specs = (tokens, tokens, P("shard", None), P("shard", "ctx"), heads, P("tensor", None), heads, rows, P("tensor"), rows,
                P(), P(), P(), P(), P())
    out_specs = (tokens, tokens, heads, P("tensor", None), heads, rows, P("tensor"), rows, P(), P(), P(), P(), P())
    return jax.shard_map(local, mesh=mesh, in_specs=in_specs, out_specs=out_specs, check_vma=False)
```

```python
import functools

import jax
import jax.numpy as jnp
import numpy as np
from jax import lax
from jax.experimental import pallas as pl
from jax.experimental.pallas import tpu as pltpu
from jax.sharding import PartitionSpec as P

HEAD = 256
HALF = HEAD // 2
ROT = 64
PIECE = 256
GRID = 16
PIECES = 3

EPSILON = 1e-05
ROPE_BASE = 10000.0
ORDER = (0, 2, 1, 3)
BF16 = jnp.bfloat16
F32 = jnp.float32
VMEM = pl.BlockSpec(memory_space=pltpu.VMEM)
LIMIT = 40
SMEM = pl.BlockSpec(memory_space=pltpu.SMEM)


def dot(left, right, dims):
    return lax.dot_general(left, right, ((dims[:1], dims[1:]), ((), ())), preferred_element_type=F32)


def shape(*dims, kind=BF16):
    return jax.ShapeDtypeStruct(dims, kind)


def call(kernel, outs, args, flops=0, grid=None, in_specs=None, out_specs=None, scratch=(), limit=LIMIT, prefetch=0):
    if grid is None:
        extra = dict(in_specs=[SMEM] * (1 + prefetch) + [VMEM] * (len(args) - 1 - prefetch), out_specs=[VMEM] * len(outs), scratch_shapes=scratch)
    else:
        extra = dict(grid_spec=pltpu.PrefetchScalarGridSpec(num_scalar_prefetch=1 + prefetch, grid=grid, in_specs=in_specs, out_specs=out_specs, scratch_shapes=scratch))
    size = sum(a.size * a.dtype.itemsize for a in args) + sum(int(np.prod(o.shape)) * o.dtype.itemsize for o in outs)
    return pl.pallas_call(
        kernel, out_shape=outs, compiler_params=pltpu.CompilerParams(vmem_limit_bytes=limit * 2**20),
        cost_estimate=pl.CostEstimate(flops=1, bytes_accessed=1, transcendentals=0), **extra,
    )(*args)


def whole(array):
    return pl.BlockSpec(array.shape, lambda *_: (0,) * len(array.shape))


def swap(value, mask):
    return lax.ppermute(value, "ctx", [(i, i ^ mask) for i in range(4)])


def level_swap(value, mask):
    return lax.ppermute(value, "tensor", [(i, i ^ mask) for i in range(4)])


def after(value, *others):
    return lax.optimization_barrier((value,) + others)[0]


def shift(value, step):
    size = lax.axis_size("shard")
    return lax.ppermute(value, "shard", [(i, (i + step) % size) for i in range(size)])


def part(ref, start, size):
    return ref[:, pl.ds(pl.multiple_of(start, 128), size)]


def prepare_joint(place, qkv, dense, *outs):
    for mask, out in enumerate(outs):
        head, half = place[2] ^ (mask >> 1), place[1] ^ (mask & 1)
        out[:, :HEAD] = part(qkv, head * 3 * HEAD + half * HEAD, HEAD).astype(BF16)
        out[:, HEAD:HEAD + HALF] = part(qkv, head * 3 * HEAD + 2 * HEAD + half * HALF, HALF).astype(BF16)
        out[:, HEAD + HALF:] = part(dense, head * HEAD + half * HALF, HALF).astype(BF16)


def prepare_near(place, one, two, own, core):
    rows = one.shape[0]
    for mask, out in ((0, own), (1, core)):
        @pl.when(pl.program_id(0) == mask)
        def _(out=out):
            out[:rows] = one[...].astype(BF16)
            out[rows:] = two[...].astype(BF16)


def prepare_far(place, one, two, one_x, one_d, two_x, two_d):
    for mask, first, second in ((0, one_x, two_x), (1, one_d, two_d)):
        @pl.when(pl.program_id(0) == mask)
        def _(first=first, second=second):
            first[...] = one[...].astype(BF16)
            second[...] = two[...].astype(BF16)


def assemble(place, pieces, out, rows, shards):
    for ref, first, mask, step in pieces:
        to = lax.rem(place[3] + step, shards) * 4 * rows + (place[0] ^ mask) * rows
        out[pl.ds(pl.multiple_of(to, 16), rows), :] = ref[first:first + rows, :]


def token_block(place, own, near, far, use):
    step, same = pl.program_id(0), place[4] & 1
    for k in (0, 1):
        pl.when(step == k)(lambda k=k: use(own[k * 128:(k + 1) * 128, :]))
    pl.when(step == 2 + same)(lambda: use(near[...]))
    pl.when(step == 3 - same)(lambda: use(far[...]))


def pair_kernel(place, own, near, far, out, total):
    token_block(place, own, near, far, lambda block: out.__setitem__(..., block))

    @pl.when(pl.program_id(0) == 0)
    def _():
        total[...] = jnp.sum(own[...].astype(F32), axis=0, keepdims=True)


def copy_kernel(place, own, near, far, out):
    token_block(place, own, near, far, lambda block: out.__setitem__(..., block))


def norm_kernel(place, first, second, gain_one, shift_one, gain_two, shift_two, one, two, plain):
    values = either(first, second).astype(F32)
    centred = values - jnp.mean(values, axis=1, keepdims=True)
    normal = centred * lax.rsqrt(jnp.mean(centred * centred, axis=1, keepdims=True) + EPSILON)
    one[...] = (normal * gain_one[...] + shift_one[...]).astype(BF16)
    two[...] = (normal * gain_two[...] + shift_two[...]).astype(BF16)
    plain[...] = normal.astype(BF16)


def either(first, second):
    return jnp.where(pl.program_id(0) < 2, first[...], second[...])


def global_index(place, local, block):
    index = local
    for p in range(4):
        index = jnp.where(local // block == p, local % block + (place[0] ^ ORDER[p]) * block, index)
    return index


def turn(front, cosine, sine):
    lane = lax.broadcasted_iota(jnp.int32, front.shape, 1)
    swapped = jnp.where(lane < ROT // 2, pltpu.roll(front, HALF - ROT // 2, 1), pltpu.roll(front, ROT // 2, 1))
    return front * cosine + swapped * sine


def table_kernel(place, starts, frequency, cosine, sine):
    length = cosine.shape[0]
    index = global_index(place, lax.broadcasted_iota(jnp.int32, (length, 1), 0), length // 4)
    places = index
    for j in range(PIECES):
        inside = jnp.clip(index - starts[j] + 1, 0, PIECE)
        places = places - inside + (inside + GRID - 1) // GRID
    angles = places.astype(F32) * frequency[...]
    lane = lax.broadcasted_iota(jnp.int32, cosine.shape, 1)
    cosine[...] = jnp.cos(angles)
    sine[...] = jnp.where(lane < ROT // 2, -1.0, 1.0) * jnp.sin(angles)


def joint_kernel(rows, shards, pieces, place, normed, cosine, sine, bias, *refs):
    blocks, (mine, weight) = refs[:-2], refs[-2:]

    @pl.when(pl.program_id(0) == 0)
    def _():
        assemble(place, [(ref,) + p for ref, p in zip(blocks, pieces)], weight, rows, shards)

    joined = dot(normed[...], weight[:, :HEAD + HALF], (1, 0))
    head, half = place[2], place[1]
    joined_low = joined[:, :HEAD] + part(bias, head * 3 * HEAD + half * HEAD, HEAD)
    mine[:, :HALF] = turn(joined_low[:, :HALF], cosine[...], sine[...]).astype(BF16)
    mine[:, HALF:HEAD] = joined_low[:, HALF:].astype(BF16)
    mine[:, HEAD:] = (joined[:, HEAD:] + part(bias, head * 3 * HEAD + 2 * HEAD + half * HALF, HALF)).astype(BF16)


def context_kernel(place, first, second, weight, mine):
    mine[...] = dot(either(first, second), weight[:, HEAD + HALF:], (1, 0)).astype(BF16)


def attention_kernel(place, starts, mine, got, grad_mine, grad_got, cosine, sine, context, grad, queries, keys, values, grads, acc, value_acc, back):
    core = place[1]
    length = mine.shape[0]
    half, block = length // 2, length // 4
    scale = HEAD ** (-0.5)
    for p in range(4):
        rows = slice(p * block, (p + 1) * block)
        first = (p * block + half) % length
        theirs = slice(first, first + block)

        @pl.when(core == 0)
        def _():
            queries[rows] = mine[rows, :HEAD]
            keys[rows] = got[theirs, :HEAD]

        @pl.when(core == 1)
        def _():
            queries[rows] = got[theirs, :HEAD]
            keys[rows] = mine[rows, :HEAD]

        values[rows, :HALF] = mine[rows, HEAD:]
        values[rows, HALF:] = got[theirs, HEAD:]
        grads[rows, :HALF] = grad_mine[rows]
        grads[rows, HALF:] = grad_got[theirs]

    def numbers(index):
        label = jnp.zeros_like(index)
        for j in range(PIECES):
            label = jnp.where((index >= starts[j]) & (index < starts[j] + PIECE), j + 1, label)
        return label

    key_index = global_index(place, lax.broadcasted_iota(jnp.int32, (1, length), 1), block)
    key_piece = numbers(key_index)
    for p in range(4):
        rows = slice(p * block, (p + 1) * block)
        query_index = lax.broadcasted_iota(jnp.int32, (block, 1), 0) + (place[0] ^ ORDER[p]) * block
        query_piece = numbers(query_index)
        allowed = (key_index <= query_index) | ((key_piece == query_piece) & (query_piece > 0))
        scores = jnp.where(allowed, dot(queries[rows], keys[...], (1, 1)) * scale, -1e30)
        weights = jnp.exp(scores - jnp.max(scores, axis=1, keepdims=True))
        weights = weights / jnp.sum(weights, axis=1, keepdims=True)
        low = weights.astype(BF16)
        context[rows] = dot(low, values[:, :HALF], (1, 0)).astype(BF16)
        term = dot(low, grads[rows, :HALF], (0, 0))
        value_acc[...] = term if p == 0 else value_acc[...] + term
        grad_weights = dot(grads[rows], values[...], (1, 1))
        centre = jnp.sum(weights * grad_weights, axis=1, keepdims=True)
        back[rows] = (weights * (grad_weights - centre)).astype(BF16)

    @pl.when(core == 0)
    def _():
        acc[...] = dot(back[...], keys[...], (1, 0)) * scale

    @pl.when(core == 1)
    def _():
        acc[...] = dot(back[...], queries[...], (0, 0)) * scale

    grad[:, HEAD:] = value_acc[...].astype(BF16)
    grad[:, HALF:HEAD] = acc[:, HALF:].astype(BF16)
    grad[:, :HALF] = turn(acc[:, :HALF], cosine[...], -sine[...]).astype(BF16)


def hidden_kernel(rows, shards, pieces, place, normed, bias, *refs):
    blocks, (hidden, slope, weight) = refs[:-3], refs[-3:]

    @pl.when(pl.program_id(0) == 0)
    def _():
        assemble(place, [(ref,) + p for ref, p in zip(blocks, pieces)], weight, rows, shards)

    width = hidden.shape[1]
    pre = dot(normed[...], weight[...], (1, 0)) + part(bias, place[0] * width, width)
    cdf = 0.5 + 0.5 * lax.erf(pre * (0.5 ** 0.5))
    hidden[...] = (pre * cdf).astype(BF16)
    slope[...] = cdf + pre * jnp.exp(-0.5 * pre * pre) * ((0.5 / np.pi) ** 0.5)


def inner_kernel(rows, shards, pieces, place, first, second, slope, *refs):
    blocks, (inner, weight) = refs[:-2], refs[-2:]

    @pl.when(pl.program_id(0) == 0)
    def _():
        assemble(place, [(ref,) + p for ref, p in zip(blocks, pieces)], weight, rows, shards)

    inner[...] = (dot(either(first, second), weight[...], (1, 0)) * slope[...]).astype(BF16)


def weight_kernel(rows, shards, steps, counts, groups, own_groups, place, *refs):
    lefts, rights, outs = refs[:sum(counts)], refs[sum(counts):sum(counts) + len(counts)], refs[sum(counts) + len(counts):]
    outs, owns, held = outs[:len(groups)], outs[len(groups):-1], outs[-1]
    turn_of, inner = pl.program_id(0), pl.program_id(1)
    size = 4 * rows // steps
    start = 0
    give, owns = owns[-1], owns[:-1]
    for count, right in zip(counts, rights):
        width, length = right.shape[1], right.shape[0] // count
        block = sum(dot(lefts[k][...], right[k * length:(k + 1) * length], (0, 0)) for k in range(count))
        held[pl.ds(pl.multiple_of(inner * size, 16), size), start:start + width] = block
        start, lefts = start + width, lefts[count:]

    def rows_of(mask):
        return held[pl.ds(pl.multiple_of((place[0] ^ mask) * rows, 16), rows), :].astype(BF16)

    @pl.when(inner == steps - 1)
    def _():
        for k, mask in enumerate(own_groups[-1]):
            give[0, k * rows:(k + 1) * rows] = rows_of(mask)

    @pl.when((inner == steps - 1) & (turn_of < shards - 1))
    def _():
        for out, masks in zip(outs, groups):
            for k, mask in enumerate(masks):
                out[0, k * rows:(k + 1) * rows] = rows_of(mask)

    @pl.when((inner == steps - 1) & (turn_of == shards - 1))
    def _():
        for out, masks in zip(owns, own_groups):
            for k, mask in enumerate(masks):
                out[k * rows:(k + 1) * rows] = rows_of(mask)


def weight_grad(place, lefts, rights, rows, shards, groups, own_groups):
    width = sum(right.shape[1] for right in rights)
    flat = [array for arrays in lefts for array in arrays]
    steps = max(1, 4 * rows // 512)
    others = max(shards - 1, 1)

    def block(turn_of, inner, place):
        step = jnp.where(turn_of == shards - 1, 0, turn_of + 1)
        return (0, lax.rem(place[3] + step, shards) * steps + inner)

    def other(turn_of, inner, place):
        return (jnp.minimum(turn_of, others - 1), 0, 0)

    return call(
        functools.partial(weight_kernel, rows, shards, steps, [len(arrays) for arrays in lefts], groups, own_groups),
        [shape(others, len(masks) * rows, width) for masks in groups] + [shape(len(masks) * rows, width) for masks in own_groups[:-1]] + [shape(shards, len(own_groups[-1]) * rows, width)],
        [place, *flat, *rights], flops=2 * rights[0].shape[0] * flat[0].shape[1] * width, grid=(shards, steps),
        in_specs=[pl.BlockSpec((array.shape[0], 4 * rows // steps), block) for array in flat] + [whole(right) for right in rights],
        out_specs=[pl.BlockSpec((1, len(masks) * rows, width), other) for masks in groups]
        + [pl.BlockSpec((len(masks) * rows, width), lambda *_: (0, 0)) for masks in own_groups[:-1]]
        + [pl.BlockSpec((1, len(own_groups[-1]) * rows, width), lambda turn_of, inner, place: (turn_of, 0, 0))],
        scratch=[pltpu.VMEM((4 * rows, width), F32)])


def total_of(own, first, got, start, rows):
    own = own.at[own.shape[0] - 1] if len(own.shape) == 3 else own
    total = own[first:first + rows].astype(F32)
    for array in got:
        total = total + array[start:start + rows].astype(F32)
    return total.astype(BF16)


def sum_kernel(first, place, own, *refs):
    refs[-1][...] = total_of(own, first, refs[:-1], 0, refs[-1].shape[0])


def sum_two_kernel(place, keep, give, *refs):
    got, (first, second, away) = refs[:-3], refs[-3:]
    rows, half = first.shape[0], len(got) // 2
    for own, arrays, out, start in ((keep, got[:half], first, 0), (give, got[half:], second, rows)):
        out[...] = total_of(own, 0, arrays, 0, rows)
        away[start:start + rows] = total_of(own, rows, arrays, rows, rows)


def place_inner(column, starts, place, *refs):
    pieces, out = refs[:-1], refs[-1]
    rows, width = out.shape[0], out.shape[1] // 4
    for mask, (piece, start) in enumerate(zip(pieces, starts)):
        out[:, pl.ds(pl.multiple_of((place[0] ^ mask) * width, 128), width)] = piece[start:start + rows, column:column + width].astype(F32)


def place_joint(place, *refs):
    pieces, (qkv, dense) = refs[:-2], refs[-2:]
    for mask, piece in enumerate(pieces):
        head, half = place[2] ^ (mask >> 1), place[1] ^ (mask & 1)
        for out, start, size, first in ((qkv, head * 3 * HEAD + half * HEAD, HEAD, 0), (qkv, head * 3 * HEAD + 2 * HEAD + half * HALF, HALF, HEAD),
                                        (dense, head * HEAD + half * HALF, HALF, HEAD + HALF)):
            out[:, pl.ds(pl.multiple_of(start, 128), size)] = piece[:, first:first + size].astype(F32)


def output_kernel(place, context, hidden, joint, weight, keep, send):
    block = dot(context[...], joint[:, HEAD + HALF:], (1, 1)) + dot(hidden[...], weight[...], (1, 1))
    pl.when(pl.program_id(0) < 2)(lambda: keep.__setitem__(..., block.astype(BF16)))
    pl.when(pl.program_id(0) >= 2)(lambda: send.__setitem__(..., block.astype(BF16)))


def back_kernel(place, grad, inner, joint, weight, gain_one, gain_two, plain, total, keep, send, small):
    step = pl.program_id(0)

    @pl.when(step == 0)
    def _():
        small[...] = jnp.zeros_like(small)
        small[4:5] = total[...]

    size = 512
    for first in range(0, keep.shape[1], size):
        here = slice(first, first + size)
        one = dot(grad[...], joint[here, :HEAD + HALF], (1, 1))
        two = dot(inner[...], weight[here], (1, 1))
        mixed = (one * gain_one[:, here] + two * gain_two[:, here]).astype(BF16)
        keep[:, here] = jnp.where(step < 2, mixed, keep[:, here])
        send[:, here] = mixed
        normal = plain[:, here].astype(F32)
        for row, value in ((0, one * normal), (1, one), (2, two * normal), (3, two)):
            small[row:row + 1, here] += jnp.sum(value, axis=0, keepdims=True)
    head, half = place[2], place[1]
    joined = jnp.sum(grad[...].astype(F32), axis=0, keepdims=True)
    for first, start, size in ((0, head * 3 * HEAD + half * HEAD, HEAD), (HEAD, head * 3 * HEAD + 2 * HEAD + half * HALF, HALF)):
        small[5:6, pl.ds(pl.multiple_of(start, 128), size)] += joined[:, first:first + size]
    width = inner.shape[1]
    small[6:7, pl.ds(pl.multiple_of(place[0] * width, 128), width)] += jnp.sum(inner[...].astype(F32), axis=0, keepdims=True)


def core_kernel(place, keep, got, *outs):
    rows = outs[0].shape[0]
    for k, out in enumerate(outs):
        here = slice(k * rows, (k + 1) * rows)
        out[...] = (keep[here].astype(F32) + got[here].astype(F32)).astype(BF16)


def add_kernel(choice, place, *refs):
    count = len(refs) // 3
    outer = (place[4] == 0) | (place[4] == 3)
    for k, out in enumerate(refs[2 * count:3 * count]):
        total = (refs[2 * k][...].astype(F32) + refs[2 * k + 1][...].astype(F32)).astype(BF16)
        out[...] = total
        if choice and k in choice:
            pl.when(outer if k == choice[0] else jnp.logical_not(outer))(lambda total=total: refs[-1].__setitem__(..., total))


def finished(place, refs, use):
    outer = (place[4] == 0) | (place[4] == 3)
    for k in range(0, len(refs), 2):
        rows = refs[k].shape[0]
        here = slice(k // 2 * rows, (k // 2 + 1) * rows)
        pl.when(outer)(lambda here=here, k=k: use(here, refs[k + 1][...].astype(F32)))
        pl.when(jnp.logical_not(outer))(lambda here=here, k=k: use(here, refs[k][...].astype(F32)))


def finish_output(place, values, bias, *refs):
    out = refs[-1]

    def use(here, total):
        out[here] = (values[here].astype(F32) + total + bias[...]).astype(BF16)

    finished(place, refs[:-1], use)


def finish_grad(place, values, grads, *refs):
    out = refs[-1]

    def use(here, total):
        residual = values[here].astype(F32)
        centred = residual - jnp.mean(residual, axis=1, keepdims=True)
        scale = lax.rsqrt(jnp.mean(centred * centred, axis=1, keepdims=True) + EPSILON)
        normal = centred * scale
        back = total - jnp.mean(total, axis=1, keepdims=True) - normal * jnp.mean(total * normal, axis=1, keepdims=True)
        out[here] = grads[here].astype(F32) + back * scale

    finished(place, refs[:-1], use)


def local(inputs, cotangent, piece_starts, positions, w_qkv, b_qkv, w_dense, w_fc1, b_fc1, w_fc2, out_bias,
          ln1_gain, ln1_bias, ln2_gain, ln2_bias):
    span, width = inputs.shape[1:]
    rows = w_fc1.shape[0]
    shards = lax.axis_size("shard")
    shard, ctx, level = lax.axis_index("shard"), lax.axis_index("ctx"), lax.axis_index("tensor")
    place = jnp.stack([ctx, ctx % 2, ctx // 2, shard, level])
    length = 4 * span
    quarter = w_fc1.shape[1] // 4
    joint = 2 * HEAD
    values, grads = inputs.reshape(span, width), cotangent.reshape(span, width)
    starts = piece_starts.reshape(-1)
    row = lambda vector: vector.reshape(1, -1)
    steps = range(1, shards)

    recent = []

    def done(*values):
        recent.extend(values)
        del recent[:-8]

    def go(value):
        return after(value, *recent) if recent else value

    def half_of(block):
        size = span // 2
        return lax.dynamic_slice(block, ((level % 2) * size, 0), (size, width))

    def send(value, mask):
        return swap(go(value), mask)

    def send_y(value, sign=-1):
        value = go(value)
        return [shift(value if value.ndim == 2 else value[k - 1], sign * k) for k in steps]

    def send_z(value, mask):
        return level_swap(go(value), mask)

    def run(kernel, outs, args, **options):
        results = call(kernel, outs, [go(args[0]), *args[1:]], **options)
        done(results[0])
        return results

    def grad_of(lefts, rights, groups, own_groups):
        results = weight_grad(go(place), lefts, rights, rows, shards, groups, own_groups)
        done(results[-1])
        return results

    def columns(first):
        return [pl.BlockSpec((rows, quarter), lambda i, place: (0, place[0] ^ (first + i)))] * 2

    def blocked(array, count=4):
        return pl.BlockSpec((array.shape[0] // count, array.shape[1]), lambda i, *_: (i, 0))

    def gathered(near, near_y, x, x_y, d, d_y, first=0):
        found = [(array, (first, mask, 0)) for array, first, mask in near]
        found += [(array, (first, mask, k)) for arrays, first, mask in near_y for k, array in zip(steps, arrays)]
        for mask, array, arrays in ((2, x, x_y), (3, d, d_y)):
            found += [(array, (0, mask, 0))] + [(value, (0, mask, k)) for k, value in zip(steps, arrays)]
        return [array for array, _ in found], [piece for _, piece in found]

    def add(*pairs):
        return run(functools.partial(add_kernel, ()), [shape(*mine.shape) for mine, _ in pairs], [place, *[array for both in pairs for array in both]])

    def level_send(value, pairs):
        return lax.ppermute(go(value), "tensor", pairs)

    inward, across, outward, ends = [(0, 1), (3, 2)], [(1, 2), (2, 1)], [(1, 0), (2, 3)], [(0, 1), (1, 0), (2, 3), (3, 2)]

    def add_choose(choice, *pairs):
        some = pairs[0][0]
        return run(functools.partial(add_kernel, choice), [shape(*some.shape)] * (len(pairs) + 1), [place, *[array for both in pairs for array in both]])

    first_half = pl.BlockSpec((span, width), lambda i, *_: (jnp.minimum(i, 1), 0))
    second_half = pl.BlockSpec((span, width), lambda i, *_: (jnp.maximum(i - 2, 0), 0))
    halves = [first_half, second_half]
    eighth = pl.BlockSpec((span // 2, width), lambda i, *_: (i, 0))
    gains = [row(vector) for vector in (ln1_gain, ln1_bias, ln2_gain, ln2_bias)]
    lanes = np.arange(HALF)
    frequency = np.where(lanes < ROT, ROPE_BASE ** (-(lanes % (ROT // 2)) * 2.0 / ROT), 0.0).astype(np.float32)[None]

    near_values = send(half_of(values), 2)
    outs = [shape(2 * rows, quarter)] * 2
    own, core = run(prepare_near, outs, [place, w_fc1, w_fc2], grid=(2,), in_specs=columns(0), out_specs=[whole(o) for o in outs])
    own_y = send_y(own)
    core = send(core, 1)
    near_grads = send(half_of(grads), 2)
    joint_own, joint_core, joint_x, joint_d = run(
        prepare_joint, [shape(rows, joint)] * 4, [place, w_qkv.reshape(rows, -1), w_dense.reshape(rows, -1)])
    joint_core = send(joint_core, 1)
    done(core)
    core_y = send_y(core)
    done(joint_core)
    cosine, sine = run(table_kernel, [shape(length, HALF, kind=F32)] * 2, [place, starts, jnp.asarray(frequency)], prefetch=1)
    done(*own_y)
    joint_near = jnp.concatenate([joint_own, joint_core])
    joint_near_y = send_y(joint_near)
    done(near_values)
    far_values = send_z(near_values, 1)
    joint_x = send(joint_x, 2)
    outs = [shape(rows, quarter)] * 4
    one_x, one_d, two_x, two_d = run(prepare_far, outs, [place, w_fc1, w_fc2], grid=(2,), in_specs=columns(2), out_specs=[whole(o) for o in outs])
    done(near_grads)
    joint_d = send(joint_d, 3)
    done(*core_y)
    far_grads = send_z(near_grads, 1)
    done(far_values)
    values_mine, = run(copy_kernel, [shape(2 * span, width)], [place, values, near_values, far_values], grid=(4,),
                       in_specs=[whole(values), whole(near_values), whole(far_values)], out_specs=[eighth])
    values_sib = send(values_mine, 1)
    done(values_sib)
    outs = [shape(length, width)] * 3
    normed_one, normed_two, plain = run(norm_kernel, outs, [place, values_mine, values_sib, *gains], grid=(4,),
                                        in_specs=halves + [whole(a) for a in gains], out_specs=[blocked(o) for o in outs])
    done(joint_x, joint_d, *joint_near_y, far_grads)
    joint_x_y = send_y(joint_x)
    joint_d_y = send_y(joint_d)
    one_x = send(one_x, 2)
    one_d = send(one_d, 3)
    grads_mine, grad_total = run(
        pair_kernel, [shape(2 * span, width), shape(1, width, kind=F32)], [place, grads, near_grads, far_grads], grid=(4,),
        in_specs=[whole(grads), whole(near_grads), whole(far_grads)], out_specs=[eighth, pl.BlockSpec((1, width), lambda *_: (0, 0))])
    pair = (grads_mine, send(grads_mine, 1))
    done(*joint_x_y, one_x, *joint_d_y, one_d, pair[1])
    two_x = send(two_x, 2)
    one_x_y = send_y(one_x)
    two_d = send(two_d, 3)
    one_d_y = send_y(one_d)
    joint_blocks = gathered([(joint_near, 0, 0), (joint_near, rows, 1)], [(joint_near_y, 0, 0), (joint_near_y, rows, 1)], joint_x, joint_x_y, joint_d, joint_d_y)
    args = [row(b_qkv.reshape(-1)), *joint_blocks[0]]
    outs = [shape(length, HEAD + HALF), shape(width, joint)]
    mine, w_joint = run(
        functools.partial(joint_kernel, rows, shards, joint_blocks[1]), outs, [place, normed_one, cosine, sine, *args],
        flops=2 * length * width * (HEAD + HALF), grid=(4,), in_specs=[blocked(normed_one), blocked(cosine), blocked(sine)] + [whole(a) for a in args],
        out_specs=[blocked(outs[0]), whole(outs[1])])
    outs = [shape(length, HALF)]
    grad_mine, = run(context_kernel, outs, [place, *pair, w_joint], flops=2 * length * width * HALF, grid=(4,),
                     in_specs=halves + [whole(w_joint)], out_specs=[blocked(outs[0])])
    done(*one_x_y, two_x, *one_d_y, two_d)
    two_x_y = send_y(two_x)
    two_d_y = send_y(two_d)
    got, grad_got = send(mine, 1), send(grad_mine, 1)
    one_blocks = gathered([(own, 0, 0), (core, 0, 1)], [(own_y, 0, 0), (core_y, 0, 1)], one_x, one_x_y, one_d, one_d_y)
    args = [row(b_fc1), *one_blocks[0]]
    outs = [shape(length, quarter), shape(length, quarter, kind=F32), shape(width, quarter)]
    hidden, slope, fc1 = run(
        functools.partial(hidden_kernel, rows, shards, one_blocks[1]), outs, [place, normed_two, *args],
        flops=2 * length * width * quarter, grid=(4,), in_specs=[blocked(normed_two)] + [whole(a) for a in args],
        out_specs=[blocked(o) for o in outs[:2]] + [whole(outs[2])])
    done(got, grad_got)
    context, grad_joined = run(
        attention_kernel, [shape(length, HALF), shape(length, HEAD + HALF)],
        [place, starts, mine, got, grad_mine, grad_got, cosine, sine], prefetch=1, flops=8 * length * length * HEAD,
        scratch=[pltpu.VMEM((length, HEAD), BF16)] * 4 + [pltpu.VMEM((length, HEAD), F32), pltpu.VMEM((length, HALF), F32), pltpu.VMEM((length, length), BF16)])
    done(*two_x_y, *two_d_y)
    two_blocks = gathered([(own, rows, 0), (core, rows, 1)], [(own_y, rows, 0), (core_y, rows, 1)], two_x, two_x_y, two_d, two_d_y)
    outs = [shape(length, quarter), shape(width, quarter)]
    grad_inner, fc2 = run(
        functools.partial(inner_kernel, rows, shards, two_blocks[1]), outs, [place, *pair, slope, *two_blocks[0]],
        flops=2 * length * width * quarter, grid=(4,), in_specs=halves + [blocked(slope)] + [whole(a) for a in two_blocks[0]],
        out_specs=[blocked(outs[0]), whole(outs[1])])
    args = [context, hidden, w_joint, fc2]
    keep, away = run(
        output_kernel, [shape(2 * span, width)] * 2, [place, *args], flops=2 * length * width * (HALF + quarter), grid=(4,),
        in_specs=[blocked(context), blocked(hidden), whole(w_joint), whole(fc2)], out_specs=halves)
    got = send(away, 1)
    two_keep_y, two_keep, two_give = grad_of([pair], [hidden], ((0, 2),), ((0, 2), (1, 3)))
    done(got)
    quarters = [shape(span // 2, width)] * 4
    out_a, out_b, away_a, away_b = run(core_kernel, quarters, [place, keep, got])

    got_a = send(away_a, 2)
    two_keep_y = send_y(two_keep_y, 1)
    two_give = send(two_give, 1)
    args = [grad_joined, grad_inner, w_joint, fc1, gains[0], gains[2], plain, grad_total]
    keep, away, small = run(
        back_kernel, [shape(2 * span, width)] * 2 + [shape(8, width, kind=F32)], [place, *args], flops=2 * length * width * (HEAD + HALF + quarter), grid=(4,),
        in_specs=[blocked(args[0]), blocked(args[1])] + [whole(a) for a in args[2:6]] + [blocked(plain), whole(grad_total)],
        out_specs=halves + [pl.BlockSpec((8, width), lambda *_: (0, 0))])
    done(got_a, *two_keep_y, two_give)
    out_a, = add((out_a, got_a))

    got_a = level_send(out_a, inward)
    got_b = send(away_b, 2)
    two_give_y = send_y(two_give, 1)
    got, small_got = send(away, 1), send(small, 1)
    far_y, near_y, rest, give = grad_of(
        [(normed_one,), pair, (normed_two,)], [grad_joined, context, grad_inner], ((2,), (0,)), ((2, 0), (3, 1)))
    done(small_got, got_a, got_b, *two_give_y, got)
    out_b, out_a = add((out_b, got_b), (out_a, got_a))
    back_a, back_b, back_away_a, back_away_b = run(core_kernel, quarters, [place, keep, got])

    got_b = level_send(out_b, inward)
    got_a = level_send(out_a, across)
    back_got_a = send(back_away_a, 2)
    far_y = send_y(far_y, 1)
    give = send(give, 1)
    two_first, two_second, two_away = run(sum_two_kernel, [shape(rows, quarter)] * 2 + [shape(2 * rows, quarter)],
                                          [place, two_keep, two_give, *two_keep_y, *two_give_y])
    small = small + small_got
    done(give, back_got_a, got_b, got_a, *far_y)
    back_a, out_a, out_b, away = add_choose((0, 1), (back_a, back_got_a), (out_a, got_a), (out_b, got_b))

    back_got_a = outer_a = level_send(away, ends)
    got_b = level_send(out_b, across)
    back_got_b = send(back_away_b, 2)
    give_far_y = send_y(give[:, :rows], 1)
    small_got = send(small, 2)
    wide = [shape(rows, joint + quarter)]
    away_one, = run(functools.partial(sum_kernel, 0), wide, [place, rest, *far_y])
    done(small_got, back_got_b, got_b, back_got_a, *give_far_y)
    back_b, out_b, back_a, away = add_choose((0, 1), (back_b, back_got_b), (out_b, got_b), (back_a, back_got_a))

    back_got_b = outer_b = level_send(away, ends)
    back_got_a = level_send(back_a, across)
    got_one = send(away_one, 2)
    near_y = send_y(near_y, 1)
    small = small + small_got
    small_got = send_z(small[:4], 1)
    away_two, = run(functools.partial(sum_kernel, 0), wide, [place, give, *give_far_y])
    done(small_got, got_one, back_got_b, back_got_a, *near_y)
    back_a, back_b = add((back_a, back_got_a), (back_b, back_got_b))

    back_got_a = level_send(back_a, outward)
    back_got_b = level_send(back_b, across)
    got_two = send(away_two, 2)
    give_near_y = send_y(give[:, rows:], 1)
    front = small[:4] + small_got
    small_got = send_z(front, 2)
    output, = run(finish_output, [shape(span, width)], [place, values, row(out_bias), out_a, outer_a, out_b, outer_b])
    first, = run(functools.partial(sum_kernel, rows), wide, [place, rest, *near_y])
    done(small_got, got_two, back_got_b, back_got_a, *give_near_y)
    back_b, = add((back_b, back_got_b))

    back_got_b = level_send(back_b, outward)
    two_got = send(two_away, 2)
    small = jnp.concatenate([front + small_got, small[4:]])
    small_got = send_y(small)
    second, = run(functools.partial(sum_kernel, rows), wide, [place, give, *give_near_y])
    pieces = [first, second, got_one, got_two]
    qd_q, qd_d = run(place_joint, [shape(rows, 6 * HEAD, kind=F32), shape(rows, 2 * HEAD, kind=F32)], [place, *pieces])
    grad_w_qkv, grad_w_dense = qd_q.reshape(w_qkv.shape), qd_d.reshape(w_dense.shape)
    full = [shape(rows, 4 * quarter, kind=F32)]
    grad_w_fc1, = run(functools.partial(place_inner, joint, (0, 0, 0, 0)), full, [place, *pieces])
    done(grad_w_qkv, grad_w_dense, *small_got)
    small = sum(small_got, small)
    done(two_got, back_got_b)
    grad_inputs, = run(finish_grad, [shape(span, width, kind=F32)], [place, values, grads, back_a, back_got_a, back_b, back_got_b])
    grad_w_fc2, = run(functools.partial(place_inner, 0, (0, 0, 0, rows)), full, [place, two_first, two_second, two_got, two_got])
    return (
        output[None],
        grad_inputs[None],
        grad_w_qkv,
        small[5, :b_qkv.size].reshape(b_qkv.shape),
        grad_w_dense,
        grad_w_fc1,
        small[6, :b_fc1.size],
        grad_w_fc2,
        small[4],
        small[0],
        small[1],
        small[2],
        small[3],
    )


def solution(mesh):
    rows = P(("shard", "ctx"), "tensor")
    tokens = P("shard", "ctx", None)
    heads = P(("shard", "ctx"), "tensor", None)
    in_specs = (tokens, tokens, P("shard", None), P("shard", "ctx"), heads, P("tensor", None), heads, rows, P("tensor"), rows,
                P(), P(), P(), P(), P())
    out_specs = (tokens, tokens, heads, P("tensor", None), heads, rows, P("tensor"), rows, P(), P(), P(), P(), P())
    return jax.shard_map(local, mesh=mesh, in_specs=in_specs, out_specs=out_specs, check_vma=False)
```

```python
import functools

import jax
import jax.numpy as jnp
import numpy as np
from jax import lax
from jax.experimental import pallas as pl
from jax.experimental.pallas import tpu as pltpu
from jax.sharding import PartitionSpec as P

HEAD = 256
HALF = HEAD // 2
ROT = 64
PIECE = 256
GRID = 16
PIECES = 3

EPSILON = 1e-05
ROPE_BASE = 10000.0
ORDER = (0, 2, 1, 3)
BF16 = jnp.bfloat16
F32 = jnp.float32
VMEM = pl.BlockSpec(memory_space=pltpu.VMEM)
LIMIT = 20
SMEM = pl.BlockSpec(memory_space=pltpu.SMEM)


def dot(left, right, dims):
    return lax.dot_general(left, right, ((dims[:1], dims[1:]), ((), ())), preferred_element_type=F32)


def shape(*dims, kind=BF16):
    return jax.ShapeDtypeStruct(dims, kind)


def call(kernel, outs, args, flops=0, grid=None, in_specs=None, out_specs=None, scratch=(), limit=LIMIT, prefetch=0, alias=()):
    if grid is None:
        extra = dict(in_specs=[SMEM] * (1 + prefetch) + [VMEM] * (len(args) - 1 - prefetch), out_specs=[VMEM] * len(outs), scratch_shapes=scratch)
    else:
        extra = dict(grid_spec=pltpu.PrefetchScalarGridSpec(num_scalar_prefetch=1 + prefetch, grid=grid, in_specs=in_specs, out_specs=out_specs, scratch_shapes=scratch))
    size = sum(a.size * a.dtype.itemsize for a in args) + sum(int(np.prod(o.shape)) * o.dtype.itemsize for o in outs)
    return pl.pallas_call(
        kernel, out_shape=outs, compiler_params=pltpu.CompilerParams(vmem_limit_bytes=limit * 2**20),
        cost_estimate=pl.CostEstimate(flops=1, bytes_accessed=1, transcendentals=0), input_output_aliases=dict(alias), **extra,
    )(*args)


def whole(array):
    return pl.BlockSpec(array.shape, lambda *_: (0,) * len(array.shape))


def swap(value, mask):
    return lax.ppermute(value, "ctx", [(i, i ^ mask) for i in range(4)])


def level_swap(value, mask):
    return lax.ppermute(value, "tensor", [(i, i ^ mask) for i in range(4)])


def after(value, *others):
    return lax.optimization_barrier((value,) + others)[0]


def shift(value, step):
    size = lax.axis_size("shard")
    return lax.ppermute(value, "shard", [(i, (i + step) % size) for i in range(size)])


def part(ref, start, size):
    return ref[:, pl.ds(pl.multiple_of(start, 128), size)]


def prepare_joint(place, qkv, dense, *outs):
    for ctx in range(4):
        @pl.when(place[0] == ctx)
        def _(ctx=ctx):
            for mask, out in enumerate(outs):
                head, half = (ctx ^ mask) // 2, (ctx ^ mask) % 2
                out[:, :HEAD] = qkv[:, head, half * HEAD:half * HEAD + HEAD].astype(BF16)
                out[:, HEAD:HEAD + HALF] = qkv[:, head, 2 * HEAD + half * HALF:2 * HEAD + half * HALF + HALF].astype(BF16)
                out[:, HEAD + HALF:] = dense[:, head, half * HALF:half * HALF + HALF].astype(BF16)


def prepare_near(place, one, two, own, core):
    rows = one.shape[0]
    for mask, out in ((0, own), (1, core)):
        @pl.when(pl.program_id(0) == mask)
        def _(out=out):
            out[:rows] = one[...].astype(BF16)
            out[rows:] = two[...].astype(BF16)


def prepare_far(place, one, two, one_x, one_d, two_x, two_d):
    for mask, first, second in ((0, one_x, two_x), (1, one_d, two_d)):
        @pl.when(pl.program_id(0) == mask)
        def _(first=first, second=second):
            first[...] = one[...].astype(BF16)
            second[...] = two[...].astype(BF16)


def assemble(place, pieces, out, rows, shards):
    for ref, first, mask, step in pieces:
        to = lax.rem(place[3] + step, shards) * 4 * rows + (place[0] ^ mask) * rows
        out[pl.ds(pl.multiple_of(to, 16), rows), :] = ref[first:first + rows, :]


def token_block(place, own, near, far, use):
    step, same = pl.program_id(0), place[4] & 1
    for k in (0, 1):
        pl.when(step == k)(lambda k=k: use(own[k * 128:(k + 1) * 128, :]))
    pl.when(step == 2 + same)(lambda: use(near[...]))
    pl.when(step == 3 - same)(lambda: use(far[...]))


def pair_kernel(place, own, near, far, out, total):
    token_block(place, own, near, far, lambda block: out.__setitem__(..., block))

    @pl.when(pl.program_id(0) == 0)
    def _():
        total[...] = jnp.sum(own[...].astype(F32), axis=0, keepdims=True)


def copy_kernel(place, own, near, far, out):
    token_block(place, own, near, far, lambda block: out.__setitem__(..., block))


def norm_kernel(place, first, second, gain_one, shift_one, gain_two, shift_two, one, two, plain):
    values = either(first, second).astype(F32)
    centred = values - jnp.mean(values, axis=1, keepdims=True)
    normal = centred * lax.rsqrt(jnp.mean(centred * centred, axis=1, keepdims=True) + EPSILON)
    one[...] = (normal * gain_one[...] + shift_one[...]).astype(BF16)
    two[...] = (normal * gain_two[...] + shift_two[...]).astype(BF16)
    plain[...] = normal.astype(BF16)


def either(first, second):
    return jnp.where(pl.program_id(0) < 2, first[...], second[...])


def global_index(place, local, block):
    index = local
    for p in range(4):
        index = jnp.where(local // block == p, local % block + (place[0] ^ ORDER[p]) * block, index)
    return index


def turn(front, cosine, sine):
    lane = lax.broadcasted_iota(jnp.int32, front.shape, 1)
    swapped = jnp.where(lane < ROT // 2, pltpu.roll(front, HALF - ROT // 2, 1), pltpu.roll(front, ROT // 2, 1))
    return front * cosine + swapped * sine


def table_kernel(place, starts, frequency, cosine, sine):
    length = cosine.shape[0]
    index = global_index(place, lax.broadcasted_iota(jnp.int32, (length, 1), 0), length // 4)
    places = index
    for j in range(PIECES):
        inside = jnp.clip(index - starts[j] + 1, 0, PIECE)
        places = places - inside + (inside + GRID - 1) // GRID
    angles = places.astype(F32) * frequency[...]
    lane = lax.broadcasted_iota(jnp.int32, cosine.shape, 1)
    cosine[...] = jnp.cos(angles)
    sine[...] = jnp.where(lane < ROT // 2, -1.0, 1.0) * jnp.sin(angles)


def joint_kernel(rows, shards, pieces, place, normed, cosine, sine, bias, *refs):
    blocks, (mine, weight) = refs[:-2], refs[-2:]

    @pl.when(pl.program_id(0) == 0)
    def _():
        assemble(place, [(ref,) + p for ref, p in zip(blocks, pieces)], weight, rows, shards)

    joined = dot(normed[...], weight[:, :HEAD + HALF], (1, 0))
    head, half = place[2], place[1]
    joined_low = joined[:, :HEAD] + part(bias, head * 3 * HEAD + half * HEAD, HEAD)
    mine[:, :HALF] = turn(joined_low[:, :HALF], cosine[...], sine[...]).astype(BF16)
    mine[:, HALF:HEAD] = joined_low[:, HALF:].astype(BF16)
    mine[:, HEAD:] = (joined[:, HEAD:] + part(bias, head * 3 * HEAD + 2 * HEAD + half * HALF, HALF)).astype(BF16)


def context_kernel(place, first, second, weight, mine):
    mine[...] = dot(either(first, second), weight[:, HEAD + HALF:], (1, 0)).astype(BF16)


def attention_kernel(place, starts, mine, got, grad_mine, grad_got, cosine, sine, context, grad, queries, keys, values, grads, acc, value_acc, back):
    core = place[1]
    length = mine.shape[0]
    half, block = length // 2, length // 4
    scale = HEAD ** (-0.5)
    for p in range(4):
        rows = slice(p * block, (p + 1) * block)
        first = (p * block + half) % length
        theirs = slice(first, first + block)

        @pl.when(core == 0)
        def _():
            queries[rows] = mine[rows, :HEAD]
            keys[rows] = got[theirs, :HEAD]

        @pl.when(core == 1)
        def _():
            queries[rows] = got[theirs, :HEAD]
            keys[rows] = mine[rows, :HEAD]

        values[rows, :HALF] = mine[rows, HEAD:]
        values[rows, HALF:] = got[theirs, HEAD:]
        grads[rows, :HALF] = grad_mine[rows]
        grads[rows, HALF:] = grad_got[theirs]

    def numbers(index):
        label = jnp.zeros_like(index)
        for j in range(PIECES):
            label = jnp.where((index >= starts[j]) & (index < starts[j] + PIECE), j + 1, label)
        return label

    key_index = global_index(place, lax.broadcasted_iota(jnp.int32, (1, length), 1), block)
    key_piece = numbers(key_index)
    for p in range(4):
        rows = slice(p * block, (p + 1) * block)
        query_index = lax.broadcasted_iota(jnp.int32, (block, 1), 0) + (place[0] ^ ORDER[p]) * block
        query_piece = numbers(query_index)
        allowed = (key_index <= query_index) | ((key_piece == query_piece) & (query_piece > 0))
        scores = jnp.where(allowed, dot(queries[rows], keys[...], (1, 1)) * scale, -1e30)
        weights = jnp.exp(scores - jnp.max(scores, axis=1, keepdims=True))
        weights = weights / jnp.sum(weights, axis=1, keepdims=True)
        low = weights.astype(BF16)
        context[rows] = dot(low, values[:, :HALF], (1, 0)).astype(BF16)
        term = dot(low, grads[rows, :HALF], (0, 0))
        value_acc[...] = term if p == 0 else value_acc[...] + term
        grad_weights = dot(grads[rows], values[...], (1, 1))
        centre = jnp.sum(weights * grad_weights, axis=1, keepdims=True)
        back[rows] = (weights * (grad_weights - centre)).astype(BF16)

    @pl.when(core == 0)
    def _():
        acc[...] = dot(back[...], keys[...], (1, 0)) * scale

    @pl.when(core == 1)
    def _():
        acc[...] = dot(back[...], queries[...], (0, 0)) * scale

    grad[:, HEAD:] = value_acc[...].astype(BF16)
    grad[:, HALF:HEAD] = acc[:, HALF:].astype(BF16)
    grad[:, :HALF] = turn(acc[:, :HALF], cosine[...], -sine[...]).astype(BF16)


def hidden_kernel(rows, shards, pieces, place, normed, bias, *refs):
    blocks, (hidden, slope, weight) = refs[:-3], refs[-3:]

    @pl.when(pl.program_id(0) == 0)
    def _():
        assemble(place, [(ref,) + p for ref, p in zip(blocks, pieces)], weight, rows, shards)

    width = hidden.shape[1]
    pre = dot(normed[...], weight[...], (1, 0)) + part(bias, place[0] * width, width)
    cdf = 0.5 + 0.5 * lax.erf(pre * (0.5 ** 0.5))
    hidden[...] = (pre * cdf).astype(BF16)
    slope[...] = cdf + pre * jnp.exp(-0.5 * pre * pre) * ((0.5 / np.pi) ** 0.5)


def inner_kernel(rows, shards, pieces, place, first, second, slope, *refs):
    blocks, (inner, weight) = refs[:-2], refs[-2:]

    @pl.when(pl.program_id(0) == 0)
    def _():
        assemble(place, [(ref,) + p for ref, p in zip(blocks, pieces)], weight, rows, shards)

    inner[...] = (dot(either(first, second), weight[...], (1, 0)) * slope[...]).astype(BF16)


def weight_kernel(rows, shards, steps, counts, groups, own_groups, place, *refs):
    lefts, rights, outs = refs[:sum(counts)], refs[sum(counts):sum(counts) + len(counts)], refs[sum(counts) + len(counts):]
    outs, owns, held = outs[:len(groups)], outs[len(groups):-1], outs[-1]
    turn_of, inner = pl.program_id(0), pl.program_id(1)
    size = 4 * rows // steps
    start = 0
    give, owns = owns[-1], owns[:-1]
    for count, right in zip(counts, rights):
        width, length = right.shape[1], right.shape[0] // count
        block = sum(dot(lefts[k][...], right[k * length:(k + 1) * length], (0, 0)) for k in range(count))
        held[pl.ds(pl.multiple_of(inner * size, 16), size), start:start + width] = block
        start, lefts = start + width, lefts[count:]

    def rows_of(mask):
        return held[pl.ds(pl.multiple_of((place[0] ^ mask) * rows, 16), rows), :].astype(BF16)

    @pl.when(inner == steps - 1)
    def _():
        for k, mask in enumerate(own_groups[-1]):
            give[0, k * rows:(k + 1) * rows] = rows_of(mask)

    @pl.when((inner == steps - 1) & (turn_of < shards - 1))
    def _():
        for out, masks in zip(outs, groups):
            for k, mask in enumerate(masks):
                out[0, k * rows:(k + 1) * rows] = rows_of(mask)

    @pl.when((inner == steps - 1) & (turn_of == shards - 1))
    def _():
        for out, masks in zip(owns, own_groups):
            for k, mask in enumerate(masks):
                out[k * rows:(k + 1) * rows] = rows_of(mask)


def weight_grad(place, lefts, rights, rows, shards, groups, own_groups):
    width = sum(right.shape[1] for right in rights)
    flat = [array for arrays in lefts for array in arrays]
    steps = max(1, 4 * rows // 512)
    others = max(shards - 1, 1)

    def block(turn_of, inner, place):
        step = jnp.where(turn_of == shards - 1, 0, turn_of + 1)
        return (0, lax.rem(place[3] + step, shards) * steps + inner)

    def other(turn_of, inner, place):
        return (jnp.minimum(turn_of, others - 1), 0, 0)

    return call(
        functools.partial(weight_kernel, rows, shards, steps, [len(arrays) for arrays in lefts], groups, own_groups),
        [shape(others, len(masks) * rows, width) for masks in groups] + [shape(len(masks) * rows, width) for masks in own_groups[:-1]] + [shape(shards, len(own_groups[-1]) * rows, width)],
        [place, *flat, *rights], flops=2 * rights[0].shape[0] * flat[0].shape[1] * width, grid=(shards, steps),
        in_specs=[pl.BlockSpec((array.shape[0], 4 * rows // steps), block) for array in flat] + [whole(right) for right in rights],
        out_specs=[pl.BlockSpec((1, len(masks) * rows, width), other) for masks in groups]
        + [pl.BlockSpec((len(masks) * rows, width), lambda *_: (0, 0)) for masks in own_groups[:-1]]
        + [pl.BlockSpec((1, len(own_groups[-1]) * rows, width), lambda turn_of, inner, place: (turn_of, 0, 0))],
        scratch=[pltpu.VMEM((4 * rows, width), F32)])


def total_of(own, first, got, start, rows):
    own = own.at[own.shape[0] - 1] if len(own.shape) == 3 else own
    total = own[first:first + rows].astype(F32)
    for array in got:
        total = total + array[start:start + rows].astype(F32)
    return total.astype(BF16)


def sum_kernel(first, place, own, *refs):
    refs[-1][...] = total_of(own, first, refs[:-1], 0, refs[-1].shape[0])


def sum_two_kernel(place, keep, give, *refs):
    got, (first, second, away) = refs[:-3], refs[-3:]
    rows, half = first.shape[0], len(got) // 2
    for own, arrays, out, start in ((keep, got[:half], first, 0), (give, got[half:], second, rows)):
        out[...] = total_of(own, 0, arrays, 0, rows)
        away[start:start + rows] = total_of(own, rows, arrays, rows, rows)


def place_inner(column, starts, place, *refs):
    pieces, out = refs[:-1], refs[-1]
    rows, width = out.shape[0], out.shape[1] // 4
    for mask, (piece, start) in enumerate(zip(pieces, starts)):
        out[:, pl.ds(pl.multiple_of((place[0] ^ mask) * width, 128), width)] = piece[start:start + rows, column:column + width].astype(F32)


def place_joint(place, *refs):
    pieces, (qkv, dense) = refs[:-2], refs[-2:]
    for ctx in range(4):
        @pl.when(place[0] == ctx)
        def _(ctx=ctx):
            for mask, piece in enumerate(pieces):
                head, half = (ctx ^ mask) // 2, (ctx ^ mask) % 2
                for out, start, size, first in ((qkv, half * HEAD, HEAD, 0), (qkv, 2 * HEAD + half * HALF, HALF, HEAD),
                                                (dense, half * HALF, HALF, HEAD + HALF)):
                    out[:, head, start:start + size] = piece[:, first:first + size].astype(F32)


def output_kernel(place, context, hidden, joint, weight, keep, send):
    step, size = pl.program_id(0), 512
    for first in range(0, keep.shape[1], size):
        here = slice(first, first + size)
        block = (dot(context[...], joint[here, HEAD + HALF:], (1, 1)) + dot(hidden[...], weight[here], (1, 1))).astype(BF16)
        keep[:, here] = jnp.where(step < 2, block, keep[:, here])
        send[:, here] = block


def back_kernel(place, grad, inner, joint, weight, gain_one, gain_two, plain, total, keep, send, small):
    step = pl.program_id(0)

    @pl.when(step == 0)
    def _():
        small[...] = jnp.zeros_like(small)
        small[4:5] = total[...]

    size = 512
    for first in range(0, keep.shape[1], size):
        here = slice(first, first + size)
        one = dot(grad[...], joint[here, :HEAD + HALF], (1, 1))
        two = dot(inner[...], weight[here], (1, 1))
        mixed = (one * gain_one[:, here] + two * gain_two[:, here]).astype(BF16)
        keep[:, here] = jnp.where(step < 2, mixed, keep[:, here])
        send[:, here] = mixed
        normal = plain[:, here].astype(F32)
        for row, value in ((0, one * normal), (1, one), (2, two * normal), (3, two)):
            small[row:row + 1, here] += jnp.sum(value, axis=0, keepdims=True)
    head, half = place[2], place[1]
    joined = jnp.sum(grad[...].astype(F32), axis=0, keepdims=True)
    for first, start, size in ((0, head * 3 * HEAD + half * HEAD, HEAD), (HEAD, head * 3 * HEAD + 2 * HEAD + half * HALF, HALF)):
        small[5:6, pl.ds(pl.multiple_of(start, 128), size)] += joined[:, first:first + size]
    width = inner.shape[1]
    small[6:7, pl.ds(pl.multiple_of(place[0] * width, 128), width)] += jnp.sum(inner[...].astype(F32), axis=0, keepdims=True)


def core_kernel(place, keep, got, *outs):
    rows = outs[0].shape[0]
    for k, out in enumerate(outs):
        here = slice(k * rows, (k + 1) * rows)
        out[...] = (keep[here].astype(F32) + got[here].astype(F32)).astype(BF16)


def add_kernel(choice, place, *refs):
    count = len(refs) // 3
    outer = (place[4] == 0) | (place[4] == 3)
    for k, out in enumerate(refs[2 * count:3 * count]):
        total = (refs[2 * k][...].astype(F32) + refs[2 * k + 1][...].astype(F32)).astype(BF16)
        out[...] = total
        if choice and k in choice:
            pl.when(outer if k == choice[0] else jnp.logical_not(outer))(lambda total=total: refs[-1].__setitem__(..., total))


def finished(place, refs, use):
    outer = (place[4] == 0) | (place[4] == 3)
    for k in range(0, len(refs), 2):
        rows = refs[k].shape[0]
        here = slice(k // 2 * rows, (k // 2 + 1) * rows)
        pl.when(outer)(lambda here=here, k=k: use(here, refs[k + 1][...].astype(F32)))
        pl.when(jnp.logical_not(outer))(lambda here=here, k=k: use(here, refs[k][...].astype(F32)))


def finish_output(place, values, bias, *refs):
    out = refs[-1]

    def use(here, total):
        out[here] = (values[here].astype(F32) + total + bias[...]).astype(BF16)

    finished(place, refs[:-1], use)


def finish_grad(place, values, grads, inner, outer, *refs):
    out = refs[-1]

    def use(total):
        residual = values[...].astype(F32)
        centred = residual - jnp.mean(residual, axis=1, keepdims=True)
        scale = lax.rsqrt(jnp.mean(centred * centred, axis=1, keepdims=True) + EPSILON)
        normal = centred * scale
        back = total - jnp.mean(total, axis=1, keepdims=True) - normal * jnp.mean(total * normal, axis=1, keepdims=True)
        out[...] = grads[...].astype(F32) + back * scale

    on_edge = (place[4] == 0) | (place[4] == 3)
    pl.when(on_edge)(lambda: use(outer[...].astype(F32)))
    pl.when(jnp.logical_not(on_edge))(lambda: use(inner[...].astype(F32)))


def local(inputs, cotangent, piece_starts, positions, w_qkv, b_qkv, w_dense, w_fc1, b_fc1, w_fc2, out_bias,
          ln1_gain, ln1_bias, ln2_gain, ln2_bias):
    span, width = inputs.shape[1:]
    rows = w_fc1.shape[0]
    shards = lax.axis_size("shard")
    shard, ctx, level = lax.axis_index("shard"), lax.axis_index("ctx"), lax.axis_index("tensor")
    place = jnp.stack([ctx, ctx % 2, ctx // 2, shard, level])
    length = 4 * span
    quarter = w_fc1.shape[1] // 4
    joint = 2 * HEAD
    values, grads = inputs.reshape(span, width), cotangent.reshape(span, width)
    starts = piece_starts.reshape(-1)
    row = lambda vector: vector.reshape(1, -1)
    steps = range(1, shards)

    recent = []

    def done(*values):
        recent.extend(values)
        del recent[:-8]

    def go(value):
        return after(value, *recent) if recent else value

    def half_of(block):
        size = span // 2
        return lax.dynamic_slice(block, ((level % 2) * size, 0), (size, width))

    def send(value, mask):
        return swap(go(value), mask)

    def send_y(value, sign=-1):
        value = go(value)
        return [shift(value if value.ndim == 2 else value[k - 1], sign * k) for k in steps]

    def send_z(value, mask):
        return level_swap(go(value), mask)

    def run(kernel, outs, args, **options):
        results = call(kernel, outs, [go(args[0]), *args[1:]], **options)
        done(results[0])
        return results

    def grad_of(lefts, rights, groups, own_groups):
        results = weight_grad(go(place), lefts, rights, rows, shards, groups, own_groups)
        done(results[-1])
        return results

    def columns(first):
        return [pl.BlockSpec((rows, quarter), lambda i, place: (0, place[0] ^ (first + i)))] * 2

    def blocked(array, count=4):
        return pl.BlockSpec((array.shape[0] // count, array.shape[1]), lambda i, *_: (i, 0))

    def gathered(near, near_y, x, x_y, d, d_y, first=0):
        found = [(array, (first, mask, 0)) for array, first, mask in near]
        found += [(array, (first, mask, k)) for arrays, first, mask in near_y for k, array in zip(steps, arrays)]
        for mask, array, arrays in ((2, x, x_y), (3, d, d_y)):
            found += [(array, (0, mask, 0))] + [(value, (0, mask, k)) for k, value in zip(steps, arrays)]
        return [array for array, _ in found], [piece for _, piece in found]

    def add(*pairs):
        return run(functools.partial(add_kernel, ()), [shape(*mine.shape) for mine, _ in pairs], [place, *[array for both in pairs for array in both]])

    def level_send(value, pairs):
        return lax.ppermute(go(value), "tensor", pairs)

    inward, across, outward, ends = [(0, 1), (3, 2)], [(1, 2), (2, 1)], [(1, 0), (2, 3)], [(0, 1), (1, 0), (2, 3), (3, 2)]

    def add_choose(choice, *pairs):
        some = pairs[0][0]
        return run(functools.partial(add_kernel, choice), [shape(*some.shape)] * (len(pairs) + 1), [place, *[array for both in pairs for array in both]])

    def finish_half(which, inner, outer, *before):
        half = pl.BlockSpec((span // 2, width), lambda i, *_: (which, 0))
        return run(finish_grad, [shape(span, width, kind=F32)], [place, values, grads, inner, outer, *before], grid=(1,),
                   in_specs=[half, half, whole(inner), whole(outer)] + [pl.BlockSpec(memory_space=pl.ANY)] * len(before), out_specs=[half],
                   alias={5: 0} if before else {})[0]

    first_half = pl.BlockSpec((span, width), lambda i, *_: (jnp.minimum(i, 1), 0))
    second_half = pl.BlockSpec((span, width), lambda i, *_: (jnp.maximum(i - 2, 0), 0))
    halves = [first_half, second_half]
    eighth = pl.BlockSpec((span // 2, width), lambda i, *_: (i, 0))
    gains = [row(vector) for vector in (ln1_gain, ln1_bias, ln2_gain, ln2_bias)]
    lanes = np.arange(HALF)
    frequency = np.where(lanes < ROT, ROPE_BASE ** (-(lanes % (ROT // 2)) * 2.0 / ROT), 0.0).astype(np.float32)[None]

    near_values = send(half_of(values), 2)
    outs = [shape(2 * rows, quarter)] * 2
    own, core = run(prepare_near, outs, [place, w_fc1, w_fc2], grid=(2,), limit=58, in_specs=columns(0), out_specs=[whole(o) for o in outs])
    own_y = send_y(own)
    core = send(core, 1)
    near_grads = send(half_of(grads), 2)
    joint_own, joint_core, joint_x, joint_d = run(
        prepare_joint, [shape(rows, joint)] * 4, [place, w_qkv, w_dense])
    joint_core = send(joint_core, 1)
    done(core)
    core_y = send_y(core)
    done(joint_core)
    cosine, sine = run(table_kernel, [shape(length, HALF, kind=F32)] * 2, [place, starts, jnp.asarray(frequency)], prefetch=1)
    done(*own_y)
    joint_near = jnp.concatenate([joint_own, joint_core])
    joint_near_y = send_y(joint_near)
    done(near_values)
    far_values = send_z(near_values, 1)
    joint_x = send(joint_x, 2)
    outs = [shape(rows, quarter)] * 4
    one_x, one_d, two_x, two_d = run(prepare_far, outs, [place, w_fc1, w_fc2], grid=(2,), in_specs=columns(2), out_specs=[whole(o) for o in outs])
    done(near_grads)
    joint_d = send(joint_d, 3)
    done(*core_y)
    far_grads = send_z(near_grads, 1)
    done(far_values)
    values_mine, = run(copy_kernel, [shape(2 * span, width)], [place, values, near_values, far_values], grid=(4,),
                       in_specs=[whole(values), whole(near_values), whole(far_values)], out_specs=[eighth])
    values_sib = send(values_mine, 1)
    done(values_sib)
    outs = [shape(length, width)] * 3
    normed_one, normed_two, plain = run(norm_kernel, outs, [place, values_mine, values_sib, *gains], grid=(4,),
                                        in_specs=halves + [whole(a) for a in gains], out_specs=[blocked(o) for o in outs])
    done(joint_x, joint_d, *joint_near_y, far_grads)
    joint_x_y = send_y(joint_x)
    joint_d_y = send_y(joint_d)
    one_x = send(one_x, 2)
    one_d = send(one_d, 3)
    grads_mine, grad_total = run(
        pair_kernel, [shape(2 * span, width), shape(1, width, kind=F32)], [place, grads, near_grads, far_grads], grid=(4,),
        in_specs=[whole(grads), whole(near_grads), whole(far_grads)], out_specs=[eighth, pl.BlockSpec((1, width), lambda *_: (0, 0))])
    pair = (grads_mine, send(grads_mine, 1))
    done(*joint_x_y, one_x, *joint_d_y, one_d, pair[1])
    two_x = send(two_x, 2)
    one_x_y = send_y(one_x)
    two_d = send(two_d, 3)
    one_d_y = send_y(one_d)
    joint_blocks = gathered([(joint_near, 0, 0), (joint_near, rows, 1)], [(joint_near_y, 0, 0), (joint_near_y, rows, 1)], joint_x, joint_x_y, joint_d, joint_d_y)
    args = [row(b_qkv.reshape(-1)), *joint_blocks[0]]
    outs = [shape(length, HEAD + HALF), shape(width, joint)]
    mine, w_joint = run(
        functools.partial(joint_kernel, rows, shards, joint_blocks[1]), outs, [place, normed_one, cosine, sine, *args],
        flops=2 * length * width * (HEAD + HALF), grid=(4,), in_specs=[blocked(normed_one), blocked(cosine), blocked(sine)] + [whole(a) for a in args],
        out_specs=[blocked(outs[0]), whole(outs[1])])
    outs = [shape(length, HALF)]
    grad_mine, = run(context_kernel, outs, [place, *pair, w_joint], flops=2 * length * width * HALF, grid=(4,),
                     in_specs=halves + [whole(w_joint)], out_specs=[blocked(outs[0])])
    done(*one_x_y, two_x, *one_d_y, two_d)
    two_x_y = send_y(two_x)
    two_d_y = send_y(two_d)
    got, grad_got = send(mine, 1), send(grad_mine, 1)
    one_blocks = gathered([(own, 0, 0), (core, 0, 1)], [(own_y, 0, 0), (core_y, 0, 1)], one_x, one_x_y, one_d, one_d_y)
    args = [row(b_fc1), *one_blocks[0]]
    outs = [shape(length, quarter), shape(length, quarter, kind=F32), shape(width, quarter)]
    hidden, slope, fc1 = run(
        functools.partial(hidden_kernel, rows, shards, one_blocks[1]), outs, [place, normed_two, *args],
        flops=2 * length * width * quarter, grid=(4,), in_specs=[blocked(normed_two)] + [whole(a) for a in args],
        out_specs=[blocked(o) for o in outs[:2]] + [whole(outs[2])])
    done(got, grad_got)
    context, grad_joined = run(
        attention_kernel, [shape(length, HALF), shape(length, HEAD + HALF)],
        [place, starts, mine, got, grad_mine, grad_got, cosine, sine], prefetch=1, flops=8 * length * length * HEAD,
        scratch=[pltpu.VMEM((length, HEAD), BF16)] * 4 + [pltpu.VMEM((length, HEAD), F32), pltpu.VMEM((length, HALF), F32), pltpu.VMEM((length, length), BF16)])
    done(*two_x_y, *two_d_y)
    two_blocks = gathered([(own, rows, 0), (core, rows, 1)], [(own_y, rows, 0), (core_y, rows, 1)], two_x, two_x_y, two_d, two_d_y)
    outs = [shape(length, quarter), shape(width, quarter)]
    grad_inner, fc2 = run(
        functools.partial(inner_kernel, rows, shards, two_blocks[1]), outs, [place, *pair, slope, *two_blocks[0]],
        flops=2 * length * width * quarter, grid=(4,), in_specs=halves + [blocked(slope)] + [whole(a) for a in two_blocks[0]],
        out_specs=[blocked(outs[0]), whole(outs[1])])
    args = [context, hidden, w_joint, fc2]
    keep, away = run(
        output_kernel, [shape(2 * span, width)] * 2, [place, *args], flops=2 * length * width * (HALF + quarter), grid=(4,),
        in_specs=[blocked(context), blocked(hidden), whole(w_joint), whole(fc2)], out_specs=halves)
    got = send(away, 1)
    two_keep_y, two_keep, two_give = grad_of([pair], [hidden], ((0, 2),), ((0, 2), (1, 3)))
    done(got)
    quarters = [shape(span // 2, width)] * 4
    out_a, out_b, away_a, away_b = run(core_kernel, quarters, [place, keep, got])

    got_a = send(away_a, 2)
    two_keep_y = send_y(two_keep_y, 1)
    two_give = send(two_give, 1)
    args = [grad_joined, grad_inner, w_joint, fc1, gains[0], gains[2], plain, grad_total]
    keep, away, small = run(
        back_kernel, [shape(2 * span, width)] * 2 + [shape(8, width, kind=F32)], [place, *args], flops=2 * length * width * (HEAD + HALF + quarter), grid=(4,),
        in_specs=[blocked(args[0]), blocked(args[1])] + [whole(a) for a in args[2:6]] + [blocked(plain), whole(grad_total)],
        out_specs=halves + [pl.BlockSpec((8, width), lambda *_: (0, 0))])
    done(got_a, *two_keep_y, two_give)
    out_a, = add((out_a, got_a))

    got_a = level_send(out_a, inward)
    got_b = send(away_b, 2)
    two_give_y = send_y(two_give, 1)
    got, small_got = send(away, 1), send(small, 1)
    far_y, near_y, rest, give = grad_of(
        [(normed_one,), pair, (normed_two,)], [grad_joined, context, grad_inner], ((2,), (0,)), ((2, 0), (3, 1)))
    done(small_got, got_a, got_b, *two_give_y, got)
    out_b, out_a = add((out_b, got_b), (out_a, got_a))
    back_a, back_b, back_away_a, back_away_b = run(core_kernel, quarters, [place, keep, got])

    got_b = level_send(out_b, inward)
    got_a = level_send(out_a, across)
    back_got_a = send(back_away_a, 2)
    far_y = send_y(far_y, 1)
    give = send(give, 1)
    two_first, two_second, two_away = run(sum_two_kernel, [shape(rows, quarter)] * 2 + [shape(2 * rows, quarter)],
                                          [place, two_keep, two_give, *two_keep_y, *two_give_y])
    small = small + small_got
    done(give, back_got_a, got_b, got_a, *far_y)
    back_a, out_a, out_b, away = add_choose((0, 1), (back_a, back_got_a), (out_a, got_a), (out_b, got_b))

    back_got_a = outer_a = level_send(away, ends)
    got_b = level_send(out_b, across)
    back_got_b = send(back_away_b, 2)
    give_far_y = send_y(give[:, :rows], 1)
    small_got = send(small, 2)
    wide = [shape(rows, joint + quarter)]
    away_one, = run(functools.partial(sum_kernel, 0), wide, [place, rest, *far_y])
    done(small_got, back_got_b, got_b, back_got_a, *give_far_y)
    back_a, out_b, back_b, away = add_choose((2, 1), (back_a, back_got_a), (out_b, got_b), (back_b, back_got_b))

    back_got_b = outer_b = level_send(away, ends)
    back_got_a = level_send(back_a, across)
    got_one = send(away_one, 2)
    near_y = send_y(near_y, 1)
    small = small + small_got
    small_got = send_z(small[:4], 1)
    away_two, = run(functools.partial(sum_kernel, 0), wide, [place, give, *give_far_y])
    done(small_got, got_one, back_got_b, back_got_a, *near_y)
    back_b, back_a = add((back_b, back_got_b), (back_a, back_got_a))

    back_got_a = level_send(back_a, outward)
    back_got_b = level_send(back_b, across)
    got_two = send(away_two, 2)
    give_near_y = send_y(give[:, rows:], 1)
    front = small[:4] + small_got
    small_got = send_z(front, 2)
    output, = run(finish_output, [shape(span, width)], [place, values, row(out_bias), out_a, outer_a, out_b, outer_b])
    first, = run(functools.partial(sum_kernel, rows), wide, [place, rest, *near_y])
    done(small_got, got_two, back_got_b, back_got_a, *give_near_y)
    back_b, = add((back_b, back_got_b))

    back_got_b = level_send(back_b, outward)
    two_got = send(two_away, 2)
    small = jnp.concatenate([front + small_got, small[4:]])
    small_got = send_y(small)
    second, = run(functools.partial(sum_kernel, rows), wide, [place, give, *give_near_y])
    pieces = [first, second, got_one, got_two]
    grad_inputs = finish_half(0, back_a, back_got_a)
    grad_w_qkv, grad_w_dense = run(place_joint, [shape(*w_qkv.shape, kind=F32), shape(*w_dense.shape, kind=F32)], [place, *pieces])
    full = [shape(rows, 4 * quarter, kind=F32)]
    grad_w_fc1, = run(functools.partial(place_inner, joint, (0, 0, 0, 0)), full, [place, *pieces])
    done(grad_w_qkv, grad_w_dense, *small_got)
    small = sum(small_got, small)
    done(two_got, back_got_b)
    grad_inputs = finish_half(1, back_b, back_got_b, grad_inputs)
    grad_w_fc2, = run(functools.partial(place_inner, 0, (0, 0, 0, rows)), full, [place, two_first, two_second, two_got, two_got])
    return (
        output[None],
        grad_inputs[None],
        grad_w_qkv,
        small[5, :b_qkv.size].reshape(b_qkv.shape),
        grad_w_dense,
        grad_w_fc1,
        small[6, :b_fc1.size],
        grad_w_fc2,
        small[4],
        small[0],
        small[1],
        small[2],
        small[3],
    )


def solution(mesh):
    rows = P(("shard", "ctx"), "tensor")
    tokens = P("shard", "ctx", None)
    heads = P(("shard", "ctx"), "tensor", None)
    in_specs = (tokens, tokens, P("shard", None), P("shard", "ctx"), heads, P("tensor", None), heads, rows, P("tensor"), rows,
                P(), P(), P(), P(), P())
    out_specs = (tokens, tokens, heads, P("tensor", None), heads, rows, P("tensor"), rows, P(), P(), P(), P(), P())
    return jax.shard_map(local, mesh=mesh, in_specs=in_specs, out_specs=out_specs, check_vma=False)
```

```python
import functools

import jax
import jax.numpy as jnp
import numpy as np
from jax import lax
from jax.experimental import pallas as pl
from jax.experimental.pallas import tpu as pltpu
from jax.sharding import PartitionSpec as P

HEAD = 256
HALF = HEAD // 2
ROT = 64
PIECE = 256
GRID = 16
PIECES = 3

EPSILON = 1e-05
ROPE_BASE = 10000.0
ORDER = (0, 2, 1, 3)
BF16 = jnp.bfloat16
F32 = jnp.float32
VMEM = pl.BlockSpec(memory_space=pltpu.VMEM)
LIMIT = 16
SMEM = pl.BlockSpec(memory_space=pltpu.SMEM)


def dot(left, right, dims):
    return lax.dot_general(left, right, ((dims[:1], dims[1:]), ((), ())), preferred_element_type=F32)


def shape(*dims, kind=BF16):
    return jax.ShapeDtypeStruct(dims, kind)


def call(kernel, outs, args, flops=0, grid=None, in_specs=None, out_specs=None, scratch=(), limit=LIMIT, prefetch=0, alias=()):
    if grid is None:
        extra = dict(in_specs=[SMEM] * (1 + prefetch) + [VMEM] * (len(args) - 1 - prefetch), out_specs=[VMEM] * len(outs), scratch_shapes=scratch)
    else:
        extra = dict(grid_spec=pltpu.PrefetchScalarGridSpec(num_scalar_prefetch=1 + prefetch, grid=grid, in_specs=in_specs, out_specs=out_specs, scratch_shapes=scratch))
    size = sum(a.size * a.dtype.itemsize for a in args) + sum(int(np.prod(o.shape)) * o.dtype.itemsize for o in outs)
    return pl.pallas_call(
        kernel, out_shape=outs, compiler_params=pltpu.CompilerParams(vmem_limit_bytes=limit * 2**20),
        cost_estimate=pl.CostEstimate(flops=1, bytes_accessed=1, transcendentals=0), input_output_aliases=dict(alias), **extra,
    )(*args)


def whole(array):
    return pl.BlockSpec(array.shape, lambda *_: (0,) * len(array.shape))


def swap(value, mask):
    return lax.ppermute(value, "ctx", [(i, i ^ mask) for i in range(4)])


def level_swap(value, mask):
    return lax.ppermute(value, "tensor", [(i, i ^ mask) for i in range(4)])


def after(value, *others):
    return lax.optimization_barrier((value,) + others)[0]


def shift(value, step):
    size = lax.axis_size("shard")
    return lax.ppermute(value, "shard", [(i, (i + step) % size) for i in range(size)])


def part(ref, start, size):
    return ref[:, pl.ds(pl.multiple_of(start, 128), size)]


def prepare_joint(place, qkv, dense, *outs):
    for ctx in range(4):
        @pl.when(place[0] == ctx)
        def _(ctx=ctx):
            for mask, out in enumerate(outs):
                head, half = (ctx ^ mask) // 2, (ctx ^ mask) % 2
                out[:, :HEAD] = qkv[:, head, half * HEAD:half * HEAD + HEAD].astype(BF16)
                out[:, HEAD:HEAD + HALF] = qkv[:, head, 2 * HEAD + half * HALF:2 * HEAD + half * HALF + HALF].astype(BF16)
                out[:, HEAD + HALF:] = dense[:, head, half * HALF:half * HALF + HALF].astype(BF16)


def prepare_near(place, one, two, own, core):
    rows = one.shape[0]
    for mask, out in ((0, own), (1, core)):
        @pl.when(pl.program_id(0) == mask)
        def _(out=out):
            out[:rows] = one[...].astype(BF16)
            out[rows:] = two[...].astype(BF16)


def prepare_far(place, one, two, one_x, one_d, two_x, two_d):
    for mask, first, second in ((0, one_x, two_x), (1, one_d, two_d)):
        @pl.when(pl.program_id(0) == mask)
        def _(first=first, second=second):
            first[...] = one[...].astype(BF16)
            second[...] = two[...].astype(BF16)


def assemble(place, pieces, out, rows, shards):
    for ref, first, mask, step in pieces:
        to = lax.rem(place[3] + step, shards) * 4 * rows + (place[0] ^ mask) * rows
        out[pl.ds(pl.multiple_of(to, 16), rows), :] = ref[first:first + rows, :]


def token_block(place, own, near, far, use):
    step, same = pl.program_id(0), place[4] & 1
    for k in (0, 1):
        pl.when(step == k)(lambda k=k: use(own[k * 128:(k + 1) * 128, :]))
    pl.when(step == 2 + same)(lambda: use(near[...]))
    pl.when(step == 3 - same)(lambda: use(far[...]))


def pair_kernel(place, own, near, far, out, total):
    token_block(place, own, near, far, lambda block: out.__setitem__(..., block))

    @pl.when(pl.program_id(0) == 0)
    def _():
        total[...] = jnp.sum(own[...].astype(F32), axis=0, keepdims=True)


def copy_kernel(place, own, near, far, out):
    token_block(place, own, near, far, lambda block: out.__setitem__(..., block))


def norm_kernel(place, first, second, gain_one, shift_one, gain_two, shift_two, one, two, plain):
    values = either(first, second).astype(F32)
    centred = values - jnp.mean(values, axis=1, keepdims=True)
    normal = centred * lax.rsqrt(jnp.mean(centred * centred, axis=1, keepdims=True) + EPSILON)
    one[...] = (normal * gain_one[...] + shift_one[...]).astype(BF16)
    two[...] = (normal * gain_two[...] + shift_two[...]).astype(BF16)
    plain[...] = normal.astype(BF16)


def either(first, second):
    return jnp.where(pl.program_id(0) < 2, first[...], second[...])


def global_index(place, local, block):
    index = local
    for p in range(4):
        index = jnp.where(local // block == p, local % block + (place[0] ^ ORDER[p]) * block, index)
    return index


def turn(front, cosine, sine):
    lane = lax.broadcasted_iota(jnp.int32, front.shape, 1)
    swapped = jnp.where(lane < ROT // 2, pltpu.roll(front, HALF - ROT // 2, 1), pltpu.roll(front, ROT // 2, 1))
    return front * cosine + swapped * sine


def table_kernel(place, starts, frequency, cosine, sine):
    length = cosine.shape[0]
    index = global_index(place, lax.broadcasted_iota(jnp.int32, (length, 1), 0), length // 4)
    places = index
    for j in range(PIECES):
        inside = jnp.clip(index - starts[j] + 1, 0, PIECE)
        places = places - inside + (inside + GRID - 1) // GRID
    angles = places.astype(F32) * frequency[...]
    lane = lax.broadcasted_iota(jnp.int32, cosine.shape, 1)
    cosine[...] = jnp.cos(angles)
    sine[...] = jnp.where(lane < ROT // 2, -1.0, 1.0) * jnp.sin(angles)


def joint_kernel(rows, shards, pieces, place, normed, cosine, sine, bias, *refs):
    blocks, (mine, weight) = refs[:-2], refs[-2:]

    @pl.when(pl.program_id(0) == 0)
    def _():
        assemble(place, [(ref,) + p for ref, p in zip(blocks, pieces)], weight, rows, shards)

    joined = dot(normed[...], weight[:, :HEAD + HALF], (1, 0))
    head, half = place[2], place[1]
    joined_low = joined[:, :HEAD] + part(bias, head * 3 * HEAD + half * HEAD, HEAD)
    mine[:, :HALF] = turn(joined_low[:, :HALF], cosine[...], sine[...]).astype(BF16)
    mine[:, HALF:HEAD] = joined_low[:, HALF:].astype(BF16)
    mine[:, HEAD:] = (joined[:, HEAD:] + part(bias, head * 3 * HEAD + 2 * HEAD + half * HALF, HALF)).astype(BF16)


def context_kernel(place, first, second, weight, mine):
    mine[...] = dot(either(first, second), weight[:, HEAD + HALF:], (1, 0)).astype(BF16)


def attention_kernel(place, starts, mine, got, grad_mine, grad_got, cosine, sine, context, grad, queries, keys, values, grads, acc, value_acc, back):
    core = place[1]
    length = mine.shape[0]
    half, block = length // 2, length // 4
    scale = HEAD ** (-0.5)
    for p in range(4):
        rows = slice(p * block, (p + 1) * block)
        first = (p * block + half) % length
        theirs = slice(first, first + block)

        @pl.when(core == 0)
        def _():
            queries[rows] = mine[rows, :HEAD]
            keys[rows] = got[theirs, :HEAD]

        @pl.when(core == 1)
        def _():
            queries[rows] = got[theirs, :HEAD]
            keys[rows] = mine[rows, :HEAD]

        values[rows, :HALF] = mine[rows, HEAD:]
        values[rows, HALF:] = got[theirs, HEAD:]
        grads[rows, :HALF] = grad_mine[rows]
        grads[rows, HALF:] = grad_got[theirs]

    def numbers(index):
        label = jnp.zeros_like(index)
        for j in range(PIECES):
            label = jnp.where((index >= starts[j]) & (index < starts[j] + PIECE), j + 1, label)
        return label

    key_index = global_index(place, lax.broadcasted_iota(jnp.int32, (1, length), 1), block)
    key_piece = numbers(key_index)
    for p in range(4):
        rows = slice(p * block, (p + 1) * block)
        query_index = lax.broadcasted_iota(jnp.int32, (block, 1), 0) + (place[0] ^ ORDER[p]) * block
        query_piece = numbers(query_index)
        allowed = (key_index <= query_index) | ((key_piece == query_piece) & (query_piece > 0))
        scores = jnp.where(allowed, dot(queries[rows], keys[...], (1, 1)) * scale, -1e30)
        weights = jnp.exp(scores - jnp.max(scores, axis=1, keepdims=True))
        weights = weights / jnp.sum(weights, axis=1, keepdims=True)
        low = weights.astype(BF16)
        context[rows] = dot(low, values[:, :HALF], (1, 0)).astype(BF16)
        term = dot(low, grads[rows, :HALF], (0, 0))
        value_acc[...] = term if p == 0 else value_acc[...] + term
        grad_weights = dot(grads[rows], values[...], (1, 1))
        centre = jnp.sum(weights * grad_weights, axis=1, keepdims=True)
        back[rows] = (weights * (grad_weights - centre)).astype(BF16)

    @pl.when(core == 0)
    def _():
        acc[...] = dot(back[...], keys[...], (1, 0)) * scale

    @pl.when(core == 1)
    def _():
        acc[...] = dot(back[...], queries[...], (0, 0)) * scale

    grad[:, HEAD:] = value_acc[...].astype(BF16)
    grad[:, HALF:HEAD] = acc[:, HALF:].astype(BF16)
    grad[:, :HALF] = turn(acc[:, :HALF], cosine[...], -sine[...]).astype(BF16)


def hidden_kernel(rows, shards, pieces, place, normed, bias, *refs):
    blocks, (hidden, slope, weight) = refs[:-3], refs[-3:]

    @pl.when(pl.program_id(0) == 0)
    def _():
        assemble(place, [(ref,) + p for ref, p in zip(blocks, pieces)], weight, rows, shards)

    width = hidden.shape[1]
    pre = dot(normed[...], weight[...], (1, 0)) + part(bias, place[0] * width, width)
    cdf = 0.5 + 0.5 * lax.erf(pre * (0.5 ** 0.5))
    hidden[...] = (pre * cdf).astype(BF16)
    slope[...] = cdf + pre * jnp.exp(-0.5 * pre * pre) * ((0.5 / np.pi) ** 0.5)


def inner_kernel(place, first, second, slope, weight, inner):
    inner[...] = (dot(either(first, second), weight[...], (1, 0)) * slope[...]).astype(BF16)


def weight_kernel(rows, shards, steps, counts, groups, own_groups, place, *refs):
    lefts, rights, outs = refs[:sum(counts)], refs[sum(counts):sum(counts) + len(counts)], refs[sum(counts) + len(counts):]
    outs, owns, held = outs[:len(groups)], outs[len(groups):-1], outs[-1]
    turn_of, inner = pl.program_id(0), pl.program_id(1)
    size = 4 * rows // steps
    start = 0
    give, owns = owns[-1], owns[:-1]
    for count, right in zip(counts, rights):
        width, length = right.shape[1], right.shape[0] // count
        block = sum(dot(lefts[k][...], right[k * length:(k + 1) * length], (0, 0)) for k in range(count))
        held[pl.ds(pl.multiple_of(inner * size, 16), size), start:start + width] = block
        start, lefts = start + width, lefts[count:]

    def rows_of(mask):
        return held[pl.ds(pl.multiple_of((place[0] ^ mask) * rows, 16), rows), :].astype(BF16)

    @pl.when(inner == steps - 1)
    def _():
        for k, mask in enumerate(own_groups[-1]):
            give[0, k * rows:(k + 1) * rows] = rows_of(mask)

    @pl.when((inner == steps - 1) & (turn_of < shards - 1))
    def _():
        for out, masks in zip(outs, groups):
            for k, mask in enumerate(masks):
                out[0, k * rows:(k + 1) * rows] = rows_of(mask)

    @pl.when((inner == steps - 1) & (turn_of == shards - 1))
    def _():
        for out, masks in zip(owns, own_groups):
            for k, mask in enumerate(masks):
                out[k * rows:(k + 1) * rows] = rows_of(mask)


def weight_grad(place, lefts, rights, rows, shards, groups, own_groups):
    width = sum(right.shape[1] for right in rights)
    flat = [array for arrays in lefts for array in arrays]
    steps = max(1, 4 * rows // 512)
    others = max(shards - 1, 1)

    def block(turn_of, inner, place):
        step = jnp.where(turn_of == shards - 1, 0, turn_of + 1)
        return (0, lax.rem(place[3] + step, shards) * steps + inner)

    def other(turn_of, inner, place):
        return (jnp.minimum(turn_of, others - 1), 0, 0)

    return call(
        functools.partial(weight_kernel, rows, shards, steps, [len(arrays) for arrays in lefts], groups, own_groups),
        [shape(others, len(masks) * rows, width) for masks in groups] + [shape(len(masks) * rows, width) for masks in own_groups[:-1]] + [shape(shards, len(own_groups[-1]) * rows, width)],
        [place, *flat, *rights], flops=2 * rights[0].shape[0] * flat[0].shape[1] * width, grid=(shards, steps),
        in_specs=[pl.BlockSpec((array.shape[0], 4 * rows // steps), block) for array in flat] + [whole(right) for right in rights],
        out_specs=[pl.BlockSpec((1, len(masks) * rows, width), other) for masks in groups]
        + [pl.BlockSpec((len(masks) * rows, width), lambda *_: (0, 0)) for masks in own_groups[:-1]]
        + [pl.BlockSpec((1, len(own_groups[-1]) * rows, width), lambda turn_of, inner, place: (turn_of, 0, 0))],
        scratch=[pltpu.VMEM((4 * rows, width), F32)])


def total_of(own, first, got, start, rows):
    own = own.at[own.shape[0] - 1] if len(own.shape) == 3 else own
    total = own[first:first + rows].astype(F32)
    for array in got:
        total = total + array[start:start + rows].astype(F32)
    return total.astype(BF16)


def sum_kernel(first, place, own, *refs):
    refs[-1][...] = total_of(own, first, refs[:-1], 0, refs[-1].shape[0])


def sum_two_kernel(place, keep, give, *refs):
    got, (first, second, away) = refs[:-3], refs[-3:]
    rows, half = first.shape[0], len(got) // 2
    for own, arrays, out, start in ((keep, got[:half], first, 0), (give, got[half:], second, rows)):
        out[...] = total_of(own, 0, arrays, 0, rows)
        away[start:start + rows] = total_of(own, rows, arrays, rows, rows)


def place_inner(column, starts, place, *refs):
    pieces, out = refs[:-1], refs[-1]
    rows, width = out.shape[0], out.shape[1] // 4
    for mask, (piece, start) in enumerate(zip(pieces, starts)):
        out[:, pl.ds(pl.multiple_of((place[0] ^ mask) * width, 128), width)] = piece[start:start + rows, column:column + width].astype(F32)


def place_joint(place, *refs):
    pieces, (qkv, dense) = refs[:-2], refs[-2:]
    for ctx in range(4):
        @pl.when(place[0] == ctx)
        def _(ctx=ctx):
            for mask, piece in enumerate(pieces):
                head, half = (ctx ^ mask) // 2, (ctx ^ mask) % 2
                for out, start, size, first in ((qkv, half * HEAD, HEAD, 0), (qkv, 2 * HEAD + half * HALF, HALF, HEAD),
                                                (dense, half * HALF, HALF, HEAD + HALF)):
                    out[:, head, start:start + size] = piece[:, first:first + size].astype(F32)


def output_kernel(rows, shards, pieces, place, context, hidden, joint, *refs):
    blocks, (keep, send, weight) = refs[:-3], refs[-3:]

    @pl.when(pl.program_id(0) == 0)
    def _():
        assemble(place, [(ref,) + p for ref, p in zip(blocks, pieces)], weight, rows, shards)

    step, size = pl.program_id(0), 512
    for first in range(0, keep.shape[1], size):
        here = slice(first, first + size)
        block = (dot(context[...], joint[here, HEAD + HALF:], (1, 1)) + dot(hidden[...], weight[here], (1, 1))).astype(BF16)
        keep[:, here] = jnp.where(step < 2, block, keep[:, here])
        send[:, here] = block


def back_kernel(place, grad, inner, joint, weight, gain_one, gain_two, plain, total, keep, send, small):
    step = pl.program_id(0)

    @pl.when(step == 0)
    def _():
        small[...] = jnp.zeros_like(small)
        small[4:5] = total[...]

    size = 512
    for first in range(0, keep.shape[1], size):
        here = slice(first, first + size)
        one = dot(grad[...], joint[here, :HEAD + HALF], (1, 1))
        two = dot(inner[...], weight[here], (1, 1))
        mixed = (one * gain_one[:, here] + two * gain_two[:, here]).astype(BF16)
        keep[:, here] = jnp.where(step < 2, mixed, keep[:, here])
        send[:, here] = mixed
        normal = plain[:, here].astype(F32)
        for row, value in ((0, one * normal), (1, one), (2, two * normal), (3, two)):
            small[row:row + 1, here] += jnp.sum(value, axis=0, keepdims=True)
    head, half = place[2], place[1]
    joined = jnp.sum(grad[...].astype(F32), axis=0, keepdims=True)
    for first, start, size in ((0, head * 3 * HEAD + half * HEAD, HEAD), (HEAD, head * 3 * HEAD + 2 * HEAD + half * HALF, HALF)):
        small[5:6, pl.ds(pl.multiple_of(start, 128), size)] += joined[:, first:first + size]
    width = inner.shape[1]
    small[6:7, pl.ds(pl.multiple_of(place[0] * width, 128), width)] += jnp.sum(inner[...].astype(F32), axis=0, keepdims=True)


def core_kernel(place, keep, got, *outs):
    rows = outs[0].shape[0]
    for k, out in enumerate(outs):
        here = slice(k * rows, (k + 1) * rows)
        out[...] = (keep[here].astype(F32) + got[here].astype(F32)).astype(BF16)


def add_kernel(choice, place, *refs):
    count = len(refs) // 3
    outer = (place[4] == 0) | (place[4] == 3)
    for k, out in enumerate(refs[2 * count:3 * count]):
        total = (refs[2 * k][...].astype(F32) + refs[2 * k + 1][...].astype(F32)).astype(BF16)
        out[...] = total
        if choice and k in choice:
            pl.when(outer if k == choice[0] else jnp.logical_not(outer))(lambda total=total: refs[-1].__setitem__(..., total))


def finished(place, refs, use):
    outer = (place[4] == 0) | (place[4] == 3)
    for k in range(0, len(refs), 2):
        rows = refs[k].shape[0]
        here = slice(k // 2 * rows, (k // 2 + 1) * rows)
        pl.when(outer)(lambda here=here, k=k: use(here, refs[k + 1][...].astype(F32)))
        pl.when(jnp.logical_not(outer))(lambda here=here, k=k: use(here, refs[k][...].astype(F32)))


def finish_output(place, values, bias, *refs):
    out = refs[-1]

    def use(here, total):
        out[here] = (values[here].astype(F32) + total + bias[...]).astype(BF16)

    finished(place, refs[:-1], use)


def finish_grad(place, values, grads, inner, outer, *refs):
    out = refs[-1]

    def use(total):
        residual = values[...].astype(F32)
        centred = residual - jnp.mean(residual, axis=1, keepdims=True)
        scale = lax.rsqrt(jnp.mean(centred * centred, axis=1, keepdims=True) + EPSILON)
        normal = centred * scale
        back = total - jnp.mean(total, axis=1, keepdims=True) - normal * jnp.mean(total * normal, axis=1, keepdims=True)
        out[...] = grads[...].astype(F32) + back * scale

    on_edge = (place[4] == 0) | (place[4] == 3)
    pl.when(on_edge)(lambda: use(outer[...].astype(F32)))
    pl.when(jnp.logical_not(on_edge))(lambda: use(inner[...].astype(F32)))


def local(inputs, cotangent, piece_starts, positions, w_qkv, b_qkv, w_dense, w_fc1, b_fc1, w_fc2, out_bias,
          ln1_gain, ln1_bias, ln2_gain, ln2_bias):
    span, width = inputs.shape[1:]
    rows = w_fc1.shape[0]
    shards = lax.axis_size("shard")
    shard, ctx, level = lax.axis_index("shard"), lax.axis_index("ctx"), lax.axis_index("tensor")
    place = jnp.stack([ctx, ctx % 2, ctx // 2, shard, level])
    length = 4 * span
    quarter = w_fc1.shape[1] // 4
    joint = 2 * HEAD
    values, grads = inputs.reshape(span, width), cotangent.reshape(span, width)
    starts = piece_starts.reshape(-1)
    row = lambda vector: vector.reshape(1, -1)
    steps = range(1, shards)

    recent = []

    def done(*values):
        recent.extend(values)
        del recent[:-8]

    def go(value):
        return after(value, *recent) if recent else value

    def half_of(block):
        size = span // 2
        return lax.dynamic_slice(block, ((level % 2) * size, 0), (size, width))

    def send(value, mask):
        return swap(go(value), mask)

    def send_y(value, sign=-1):
        value = go(value)
        return [shift(value if value.ndim == 2 else value[k - 1], sign * k) for k in steps]

    def send_z(value, mask):
        return level_swap(go(value), mask)

    def run(kernel, outs, args, **options):
        results = call(kernel, outs, [go(args[0]), *args[1:]], **options)
        done(results[0])
        return results

    def grad_of(lefts, rights, groups, own_groups):
        results = weight_grad(go(place), lefts, rights, rows, shards, groups, own_groups)
        done(results[-1])
        return results

    def columns(first):
        return [pl.BlockSpec((rows, quarter), lambda i, place: (0, place[0] ^ (first + i)))] * 2

    def blocked(array, count=4):
        return pl.BlockSpec((array.shape[0] // count, array.shape[1]), lambda i, *_: (i, 0))

    def gathered(near, near_y, x, x_y, d, d_y, first=0):
        found = [(array, (first, mask, 0)) for array, first, mask in near]
        found += [(array, (first, mask, k)) for arrays, first, mask in near_y for k, array in zip(steps, arrays)]
        for mask, array, arrays in ((2, x, x_y), (3, d, d_y)):
            found += [(array, (0, mask, 0))] + [(value, (0, mask, k)) for k, value in zip(steps, arrays)]
        return [array for array, _ in found], [piece for _, piece in found]

    def add(*pairs):
        return run(functools.partial(add_kernel, ()), [shape(*mine.shape) for mine, _ in pairs], [place, *[array for both in pairs for array in both]])

    def level_send(value, pairs):
        return lax.ppermute(go(value), "tensor", pairs)

    inward, across, outward, ends = [(0, 1), (3, 2)], [(1, 2), (2, 1)], [(1, 0), (2, 3)], [(0, 1), (1, 0), (2, 3), (3, 2)]

    def add_choose(choice, *pairs):
        some = pairs[0][0]
        return run(functools.partial(add_kernel, choice), [shape(*some.shape)] * (len(pairs) + 1), [place, *[array for both in pairs for array in both]])

    def finish_half(which, inner, outer, *before):
        half = pl.BlockSpec((span // 2, width), lambda i, *_: (which, 0))
        return run(finish_grad, [shape(span, width, kind=F32)], [place, values, grads, inner, outer, *before], grid=(1,),
                   in_specs=[half, half, whole(inner), whole(outer)] + [pl.BlockSpec(memory_space=pl.ANY)] * len(before), out_specs=[half],
                   alias={5: 0} if before else {})[0]

    first_half = pl.BlockSpec((span, width), lambda i, *_: (jnp.minimum(i, 1), 0))
    second_half = pl.BlockSpec((span, width), lambda i, *_: (jnp.maximum(i - 2, 0), 0))
    halves = [first_half, second_half]
    eighth = pl.BlockSpec((span // 2, width), lambda i, *_: (i, 0))
    gains = [row(vector) for vector in (ln1_gain, ln1_bias, ln2_gain, ln2_bias)]
    lanes = np.arange(HALF)
    frequency = np.where(lanes < ROT, ROPE_BASE ** (-(lanes % (ROT // 2)) * 2.0 / ROT), 0.0).astype(np.float32)[None]

    near_values = send(half_of(values), 2)
    outs = [shape(2 * rows, quarter)] * 2
    own, core = run(prepare_near, outs, [place, w_fc1, w_fc2], grid=(2,), limit=58, in_specs=columns(0), out_specs=[whole(o) for o in outs])
    own_y = send_y(own)
    core = send(core, 1)
    near_grads = send(half_of(grads), 2)
    joint_own, joint_core, joint_x, joint_d = run(
        prepare_joint, [shape(rows, joint)] * 4, [place, w_qkv, w_dense])
    joint_core = send(joint_core, 1)
    done(core)
    core_y = send_y(core)
    done(joint_core)
    cosine, sine = run(table_kernel, [shape(length, HALF, kind=F32)] * 2, [place, starts, jnp.asarray(frequency)], prefetch=1)
    done(*own_y)
    joint_near = jnp.concatenate([joint_own, joint_core])
    joint_near_y = send_y(joint_near)
    done(near_values)
    far_values = send_z(near_values, 1)
    joint_x = send(joint_x, 2)
    outs = [shape(rows, quarter)] * 4
    one_x, one_d, two_x, two_d = run(prepare_far, outs, [place, w_fc1, w_fc2], grid=(2,), in_specs=columns(2), out_specs=[whole(o) for o in outs])
    done(near_grads)
    joint_d = send(joint_d, 3)
    done(*core_y)
    far_grads = send_z(near_grads, 1)
    done(far_values)
    values_mine, = run(copy_kernel, [shape(2 * span, width)], [place, values, near_values, far_values], grid=(4,),
                       in_specs=[whole(values), whole(near_values), whole(far_values)], out_specs=[eighth])
    values_sib = send(values_mine, 1)
    done(values_sib)
    outs = [shape(length, width)] * 3
    normed_one, normed_two, plain = run(norm_kernel, outs, [place, values_mine, values_sib, *gains], grid=(4,),
                                        in_specs=halves + [whole(a) for a in gains], out_specs=[blocked(o) for o in outs])
    done(joint_x, joint_d, *joint_near_y, far_grads)
    joint_x_y = send_y(joint_x)
    joint_d_y = send_y(joint_d)
    one_x = send(one_x, 2)
    one_d = send(one_d, 3)
    grads_mine, grad_total = run(
        pair_kernel, [shape(2 * span, width), shape(1, width, kind=F32)], [place, grads, near_grads, far_grads], grid=(4,),
        in_specs=[whole(grads), whole(near_grads), whole(far_grads)], out_specs=[eighth, pl.BlockSpec((1, width), lambda *_: (0, 0))])
    pair = (grads_mine, send(grads_mine, 1))
    done(*joint_x_y, one_x, *joint_d_y, one_d, pair[1])
    two_x = send(two_x, 2)
    one_x_y = send_y(one_x)
    two_d = send(two_d, 3)
    one_d_y = send_y(one_d)
    joint_blocks = gathered([(joint_near, 0, 0), (joint_near, rows, 1)], [(joint_near_y, 0, 0), (joint_near_y, rows, 1)], joint_x, joint_x_y, joint_d, joint_d_y)
    args = [row(b_qkv.reshape(-1)), *joint_blocks[0]]
    outs = [shape(length, HEAD + HALF), shape(width, joint)]
    mine, w_joint = run(
        functools.partial(joint_kernel, rows, shards, joint_blocks[1]), outs, [place, normed_one, cosine, sine, *args],
        flops=2 * length * width * (HEAD + HALF), grid=(4,), in_specs=[blocked(normed_one), blocked(cosine), blocked(sine)] + [whole(a) for a in args],
        out_specs=[blocked(outs[0]), whole(outs[1])])
    outs = [shape(length, HALF)]
    grad_mine, = run(context_kernel, outs, [place, *pair, w_joint], flops=2 * length * width * HALF, grid=(4,),
                     in_specs=halves + [whole(w_joint)], out_specs=[blocked(outs[0])])
    done(*one_x_y, two_x, *one_d_y, two_d)
    two_x_y = send_y(two_x)
    two_d_y = send_y(two_d)
    got, grad_got = send(mine, 1), send(grad_mine, 1)
    one_blocks = gathered([(own, 0, 0), (core, 0, 1)], [(own_y, 0, 0), (core_y, 0, 1)], one_x, one_x_y, one_d, one_d_y)
    args = [row(b_fc1), *one_blocks[0]]
    outs = [shape(length, quarter), shape(length, quarter, kind=F32), shape(width, quarter)]
    hidden, slope, fc1 = run(
        functools.partial(hidden_kernel, rows, shards, one_blocks[1]), outs, [place, normed_two, *args],
        flops=2 * length * width * quarter, grid=(4,), in_specs=[blocked(normed_two)] + [whole(a) for a in args],
        out_specs=[blocked(o) for o in outs[:2]] + [whole(outs[2])])
    done(got, grad_got)
    context, grad_joined = run(
        attention_kernel, [shape(length, HALF), shape(length, HEAD + HALF)],
        [place, starts, mine, got, grad_mine, grad_got, cosine, sine], prefetch=1, flops=8 * length * length * HEAD,
        scratch=[pltpu.VMEM((length, HEAD), BF16)] * 4 + [pltpu.VMEM((length, HEAD), F32), pltpu.VMEM((length, HALF), F32), pltpu.VMEM((length, length), BF16)])
    done(*two_x_y, *two_d_y)
    two_blocks = gathered([(own, rows, 0), (core, rows, 1)], [(own_y, rows, 0), (core_y, rows, 1)], two_x, two_x_y, two_d, two_d_y)
    args = [context, hidden, w_joint, *two_blocks[0]]
    keep, away, fc2 = run(
        functools.partial(output_kernel, rows, shards, two_blocks[1]), [shape(2 * span, width)] * 2 + [shape(width, quarter)], [place, *args],
        flops=2 * length * width * (HALF + quarter), grid=(4,),
        in_specs=[blocked(context), blocked(hidden)] + [whole(a) for a in args[2:]], out_specs=halves + [whole(shape(width, quarter))])
    got = send(away, 1)
    two_keep_y, two_keep, two_give = grad_of([pair], [hidden], ((0, 2),), ((0, 2), (1, 3)))
    done(got)
    quarters = [shape(span // 2, width)] * 4
    out_a, out_b, away_a, away_b = run(core_kernel, quarters, [place, keep, got])

    got_a = send(away_a, 2)
    two_keep_y = send_y(two_keep_y, 1)
    two_give = send(two_give, 1)
    outs = [shape(length, quarter)]
    grad_inner, = run(inner_kernel, outs, [place, *pair, slope, fc2], flops=2 * length * width * quarter, grid=(4,),
                      in_specs=halves + [blocked(slope), whole(fc2)], out_specs=[blocked(outs[0])])
    args = [grad_joined, grad_inner, w_joint, fc1, gains[0], gains[2], plain, grad_total]
    keep, away, small = run(
        back_kernel, [shape(2 * span, width)] * 2 + [shape(8, width, kind=F32)], [place, *args], flops=2 * length * width * (HEAD + HALF + quarter), grid=(4,),
        in_specs=[blocked(args[0]), blocked(args[1])] + [whole(a) for a in args[2:6]] + [blocked(plain), whole(grad_total)],
        out_specs=halves + [pl.BlockSpec((8, width), lambda *_: (0, 0))])
    done(got_a, *two_keep_y, two_give)
    out_a, = add((out_a, got_a))

    got_a = level_send(out_a, inward)
    got_b = send(away_b, 2)
    two_give_y = send_y(two_give, 1)
    got, small_got = send(away, 1), send(small, 1)
    far_y, near_y, rest, give = grad_of(
        [(normed_one,), pair, (normed_two,)], [grad_joined, context, grad_inner], ((2,), (0,)), ((2, 0), (3, 1)))
    done(small_got, got_a, got_b, *two_give_y, got)
    out_b, out_a = add((out_b, got_b), (out_a, got_a))
    back_a, back_b, back_away_a, back_away_b = run(core_kernel, quarters, [place, keep, got])

    got_b = level_send(out_b, inward)
    got_a = level_send(out_a, across)
    back_got_a = send(back_away_a, 2)
    far_y = send_y(far_y, 1)
    give = send(give, 1)
    two_first, two_second, two_away = run(sum_two_kernel, [shape(rows, quarter)] * 2 + [shape(2 * rows, quarter)],
                                          [place, two_keep, two_give, *two_keep_y, *two_give_y])
    small = small + small_got
    done(give, back_got_a, got_b, got_a, *far_y)
    back_a, out_a, out_b, away = add_choose((0, 1), (back_a, back_got_a), (out_a, got_a), (out_b, got_b))

    back_got_a = outer_a = level_send(away, ends)
    got_b = level_send(out_b, across)
    back_got_b = send(back_away_b, 2)
    give_far_y = send_y(give[:, :rows], 1)
    small_got = send(small, 2)
    wide = [shape(rows, joint + quarter)]
    away_one, = run(functools.partial(sum_kernel, 0), wide, [place, rest, *far_y])
    done(small_got, back_got_b, got_b, back_got_a, *give_far_y)
    back_a, out_b, back_b, away = add_choose((2, 1), (back_a, back_got_a), (out_b, got_b), (back_b, back_got_b))

    back_got_b = outer_b = level_send(away, ends)
    back_got_a = level_send(back_a, across)
    got_one = send(away_one, 2)
    near_y = send_y(near_y, 1)
    small = small + small_got
    small_got = send_z(small[:4], 1)
    away_two, = run(functools.partial(sum_kernel, 0), wide, [place, give, *give_far_y])
    done(small_got, got_one, back_got_b, back_got_a, *near_y)
    back_b, back_a = add((back_b, back_got_b), (back_a, back_got_a))

    back_got_a = level_send(back_a, outward)
    back_got_b = level_send(back_b, across)
    got_two = send(away_two, 2)
    give_near_y = send_y(give[:, rows:], 1)
    front = small[:4] + small_got
    small_got = send_z(front, 2)
    output, = run(finish_output, [shape(span, width)], [place, values, row(out_bias), out_a, outer_a, out_b, outer_b])
    first, = run(functools.partial(sum_kernel, rows), wide, [place, rest, *near_y])
    done(small_got, got_two, back_got_b, back_got_a, *give_near_y)
    back_b, = add((back_b, back_got_b))

    back_got_b = level_send(back_b, outward)
    two_got = send(two_away, 2)
    small = jnp.concatenate([front + small_got, small[4:]])
    small_got = send_y(small)
    second, = run(functools.partial(sum_kernel, rows), wide, [place, give, *give_near_y])
    pieces = [first, second, got_one, got_two]
    grad_inputs = finish_half(0, back_a, back_got_a)
    grad_w_qkv, grad_w_dense = run(place_joint, [shape(*w_qkv.shape, kind=F32), shape(*w_dense.shape, kind=F32)], [place, *pieces])
    full = [shape(rows, 4 * quarter, kind=F32)]
    grad_w_fc1, = run(functools.partial(place_inner, joint, (0, 0, 0, 0)), full, [place, *pieces])
    done(grad_w_qkv, grad_w_dense, *small_got)
    small = sum(small_got, small)
    done(two_got, back_got_b)
    grad_inputs = finish_half(1, back_b, back_got_b, grad_inputs)
    grad_w_fc2, = run(functools.partial(place_inner, 0, (0, 0, 0, rows)), full, [place, two_first, two_second, two_got, two_got])
    return (
        output[None],
        grad_inputs[None],
        grad_w_qkv,
        small[5, :b_qkv.size].reshape(b_qkv.shape),
        grad_w_dense,
        grad_w_fc1,
        small[6, :b_fc1.size],
        grad_w_fc2,
        small[4],
        small[0],
        small[1],
        small[2],
        small[3],
    )


def solution(mesh):
    rows = P(("shard", "ctx"), "tensor")
    tokens = P("shard", "ctx", None)
    heads = P(("shard", "ctx"), "tensor", None)
    in_specs = (tokens, tokens, P("shard", None), P("shard", "ctx"), heads, P("tensor", None), heads, rows, P("tensor"), rows,
                P(), P(), P(), P(), P())
    out_specs = (tokens, tokens, heads, P("tensor", None), heads, rows, P("tensor"), rows, P(), P(), P(), P(), P())
    return jax.shard_map(local, mesh=mesh, in_specs=in_specs, out_specs=out_specs, check_vma=False)
```

```python
import functools

import jax
import jax.numpy as jnp
import numpy as np
from jax import lax
from jax.experimental import pallas as pl
from jax.experimental.pallas import tpu as pltpu
from jax.sharding import PartitionSpec as P

HEAD = 256
HALF = HEAD // 2
ROT = 64
PIECE = 256
GRID = 16
PIECES = 3

EPSILON = 1e-05
ROPE_BASE = 10000.0
ORDER = (0, 2, 1, 3)
BF16 = jnp.bfloat16
F32 = jnp.float32
VMEM = pl.BlockSpec(memory_space=pltpu.VMEM)
LIMIT = 16
SMEM = pl.BlockSpec(memory_space=pltpu.SMEM)


def dot(left, right, dims):
    return lax.dot_general(left, right, ((dims[:1], dims[1:]), ((), ())), preferred_element_type=F32)


def shape(*dims, kind=BF16):
    return jax.ShapeDtypeStruct(dims, kind)


def call(kernel, outs, args, flops=0, grid=None, in_specs=None, out_specs=None, scratch=(), limit=LIMIT, prefetch=0, alias=()):
    if grid is None:
        extra = dict(in_specs=[SMEM] * (1 + prefetch) + [VMEM] * (len(args) - 1 - prefetch), out_specs=[VMEM] * len(outs), scratch_shapes=scratch)
    else:
        extra = dict(grid_spec=pltpu.PrefetchScalarGridSpec(num_scalar_prefetch=1 + prefetch, grid=grid, in_specs=in_specs, out_specs=out_specs, scratch_shapes=scratch))
    size = sum(a.size * a.dtype.itemsize for a in args) + sum(int(np.prod(o.shape)) * o.dtype.itemsize for o in outs)
    return pl.pallas_call(
        kernel, out_shape=outs, compiler_params=pltpu.CompilerParams(vmem_limit_bytes=limit * 2**20),
        cost_estimate=pl.CostEstimate(flops=1, bytes_accessed=1, transcendentals=0), input_output_aliases=dict(alias), **extra,
    )(*args)


def whole(array):
    return pl.BlockSpec(array.shape, lambda *_: (0,) * len(array.shape))


def swap(value, mask):
    return lax.ppermute(value, "ctx", [(i, i ^ mask) for i in range(4)])


def level_swap(value, mask):
    return lax.ppermute(value, "tensor", [(i, i ^ mask) for i in range(4)])


def after(value, *others):
    return lax.optimization_barrier((value,) + others)[0]


def shift(value, step):
    size = lax.axis_size("shard")
    return lax.ppermute(value, "shard", [(i, (i + step) % size) for i in range(size)])


def part(ref, start, size):
    return ref[:, pl.ds(pl.multiple_of(start, 128), size)]


def prepare_joint(place, qkv, dense, *outs):
    for ctx in range(4):
        @pl.when(place[0] == ctx)
        def _(ctx=ctx):
            for mask, out in enumerate(outs):
                head, half = (ctx ^ mask) // 2, (ctx ^ mask) % 2
                out[:, :HEAD] = qkv[:, head, half * HEAD:half * HEAD + HEAD].astype(BF16)
                out[:, HEAD:HEAD + HALF] = qkv[:, head, 2 * HEAD + half * HALF:2 * HEAD + half * HALF + HALF].astype(BF16)
                out[:, HEAD + HALF:] = dense[:, head, half * HALF:half * HALF + HALF].astype(BF16)


def prepare_near(place, one, two, own, core):
    rows = one.shape[0]
    for mask, out in ((0, own), (1, core)):
        @pl.when(pl.program_id(0) == mask)
        def _(out=out):
            out[:rows] = one[...].astype(BF16)
            out[rows:] = two[...].astype(BF16)


def prepare_far(place, one, two, one_x, one_d, two_x, two_d):
    for mask, first, second in ((0, one_x, two_x), (1, one_d, two_d)):
        @pl.when(pl.program_id(0) == mask)
        def _(first=first, second=second):
            first[...] = one[...].astype(BF16)
            second[...] = two[...].astype(BF16)


def assemble(place, pieces, out, rows, shards):
    for ref, first, mask, step in pieces:
        to = lax.rem(place[3] + step, shards) * 4 * rows + (place[0] ^ mask) * rows
        out[pl.ds(pl.multiple_of(to, 16), rows), :] = ref[first:first + rows, :]


def token_block(place, own, near, far, use):
    step, same = pl.program_id(0), place[4] & 1
    for k in (0, 1):
        pl.when(step == k)(lambda k=k: use(own[k * 128:(k + 1) * 128, :]))
    pl.when(step == 2 + same)(lambda: use(near[...]))
    pl.when(step == 3 - same)(lambda: use(far[...]))


def pair_kernel(place, own, near, far, out, total):
    token_block(place, own, near, far, lambda block: out.__setitem__(..., block))

    @pl.when(pl.program_id(0) == 0)
    def _():
        total[...] = jnp.sum(own[...].astype(F32), axis=0, keepdims=True)


def copy_kernel(place, own, near, far, out):
    token_block(place, own, near, far, lambda block: out.__setitem__(..., block))


def norm_kernel(place, first, second, gain_one, shift_one, gain_two, shift_two, one, two, plain):
    values = either(first, second).astype(F32)
    centred = values - jnp.mean(values, axis=1, keepdims=True)
    normal = centred * lax.rsqrt(jnp.mean(centred * centred, axis=1, keepdims=True) + EPSILON)
    one[...] = (normal * gain_one[...] + shift_one[...]).astype(BF16)
    two[...] = (normal * gain_two[...] + shift_two[...]).astype(BF16)
    plain[...] = normal.astype(BF16)


def either(first, second):
    return jnp.where(pl.program_id(0) < 2, first[...], second[...])


def global_index(place, local, block):
    index = local
    for p in range(4):
        index = jnp.where(local // block == p, local % block + (place[0] ^ ORDER[p]) * block, index)
    return index


def turn(front, cosine, sine):
    lane = lax.broadcasted_iota(jnp.int32, front.shape, 1)
    swapped = jnp.where(lane < ROT // 2, pltpu.roll(front, HALF - ROT // 2, 1), pltpu.roll(front, ROT // 2, 1))
    return front * cosine + swapped * sine


def table_kernel(place, starts, frequency, cosine, sine):
    length = cosine.shape[0]
    index = global_index(place, lax.broadcasted_iota(jnp.int32, (length, 1), 0), length // 4)
    places = index
    for j in range(PIECES):
        inside = jnp.clip(index - starts[j] + 1, 0, PIECE)
        places = places - inside + (inside + GRID - 1) // GRID
    angles = places.astype(F32) * frequency[...]
    lane = lax.broadcasted_iota(jnp.int32, cosine.shape, 1)
    cosine[...] = jnp.cos(angles)
    sine[...] = jnp.where(lane < ROT // 2, -1.0, 1.0) * jnp.sin(angles)


def joint_kernel(rows, shards, pieces, place, normed, cosine, sine, bias, *refs):
    blocks, (mine, weight) = refs[:-2], refs[-2:]

    @pl.when(pl.program_id(0) == 0)
    def _():
        assemble(place, [(ref,) + p for ref, p in zip(blocks, pieces)], weight, rows, shards)

    joined = dot(normed[...], weight[:, :HEAD + HALF], (1, 0))
    head, half = place[2], place[1]
    joined_low = joined[:, :HEAD] + part(bias, head * 3 * HEAD + half * HEAD, HEAD)
    mine[:, :HALF] = turn(joined_low[:, :HALF], cosine[...], sine[...]).astype(BF16)
    mine[:, HALF:HEAD] = joined_low[:, HALF:].astype(BF16)
    mine[:, HEAD:] = (joined[:, HEAD:] + part(bias, head * 3 * HEAD + 2 * HEAD + half * HALF, HALF)).astype(BF16)


def context_kernel(place, first, second, weight, mine, out):
    out[:, :HEAD + HALF] = mine[...]
    out[:, HEAD + HALF:] = dot(either(first, second), weight[:, HEAD + HALF:], (1, 0)).astype(BF16)


def attention_kernel(place, starts, mine, got, cosine, sine, context, grad, queries, keys, values, grads, acc, value_acc, back):
    core = place[1]
    length = mine.shape[0]
    half, block = length // 2, length // 4
    scale = HEAD ** (-0.5)
    for p in range(4):
        rows = slice(p * block, (p + 1) * block)
        first = (p * block + half) % length
        theirs = slice(first, first + block)

        @pl.when(core == 0)
        def _():
            queries[rows] = mine[rows, :HEAD]
            keys[rows] = got[theirs, :HEAD]

        @pl.when(core == 1)
        def _():
            queries[rows] = got[theirs, :HEAD]
            keys[rows] = mine[rows, :HEAD]

        values[rows, :HALF] = mine[rows, HEAD:HEAD + HALF]
        values[rows, HALF:] = got[theirs, HEAD:HEAD + HALF]
        grads[rows, :HALF] = mine[rows, HEAD + HALF:]
        grads[rows, HALF:] = got[theirs, HEAD + HALF:]

    def numbers(index):
        label = jnp.zeros_like(index)
        for j in range(PIECES):
            label = jnp.where((index >= starts[j]) & (index < starts[j] + PIECE), j + 1, label)
        return label

    key_index = global_index(place, lax.broadcasted_iota(jnp.int32, (1, length), 1), block)
    key_piece = numbers(key_index)
    for p in range(4):
        rows = slice(p * block, (p + 1) * block)
        query_index = lax.broadcasted_iota(jnp.int32, (block, 1), 0) + (place[0] ^ ORDER[p]) * block
        query_piece = numbers(query_index)
        allowed = (key_index <= query_index) | ((key_piece == query_piece) & (query_piece > 0))
        scores = jnp.where(allowed, dot(queries[rows], keys[...], (1, 1)) * scale, -1e30)
        weights = jnp.exp(scores - jnp.max(scores, axis=1, keepdims=True))
        weights = weights / jnp.sum(weights, axis=1, keepdims=True)
        low = weights.astype(BF16)
        context[rows] = dot(low, values[:, :HALF], (1, 0)).astype(BF16)
        term = dot(low, grads[rows, :HALF], (0, 0))
        value_acc[...] = term if p == 0 else value_acc[...] + term
        grad_weights = dot(grads[rows], values[...], (1, 1))
        centre = jnp.sum(weights * grad_weights, axis=1, keepdims=True)
        back[rows] = (weights * (grad_weights - centre)).astype(BF16)

    @pl.when(core == 0)
    def _():
        acc[...] = dot(back[...], keys[...], (1, 0)) * scale

    @pl.when(core == 1)
    def _():
        acc[...] = dot(back[...], queries[...], (0, 0)) * scale

    grad[:, HEAD:] = value_acc[...].astype(BF16)
    grad[:, HALF:HEAD] = acc[:, HALF:].astype(BF16)
    grad[:, :HALF] = turn(acc[:, :HALF], cosine[...], -sine[...]).astype(BF16)


def hidden_kernel(rows, shards, pieces, place, normed, bias, *refs):
    blocks, (hidden, slope, weight) = refs[:-3], refs[-3:]

    @pl.when(pl.program_id(0) == 0)
    def _():
        assemble(place, [(ref,) + p for ref, p in zip(blocks, pieces)], weight, rows, shards)

    width = hidden.shape[1]
    pre = dot(normed[...], weight[...], (1, 0)) + part(bias, place[0] * width, width)
    cdf = 0.5 + 0.5 * lax.erf(pre * (0.5 ** 0.5))
    hidden[...] = (pre * cdf).astype(BF16)
    slope[...] = cdf + pre * jnp.exp(-0.5 * pre * pre) * ((0.5 / np.pi) ** 0.5)


def inner_kernel(place, first, second, slope, weight, inner):
    inner[...] = (dot(either(first, second), weight[...], (1, 0)) * slope[...]).astype(BF16)


def weight_kernel(rows, shards, steps, counts, groups, own_groups, place, *refs):
    lefts, rights, outs = refs[:sum(counts)], refs[sum(counts):sum(counts) + len(counts)], refs[sum(counts) + len(counts):]
    outs, owns, held = outs[:len(groups)], outs[len(groups):-1], outs[-1]
    turn_of, inner = pl.program_id(0), pl.program_id(1)
    size = 4 * rows // steps
    start = 0
    give, owns = owns[-1], owns[:-1]
    for count, right in zip(counts, rights):
        width, length = right.shape[1], right.shape[0] // count
        block = sum(dot(lefts[k][...], right[k * length:(k + 1) * length], (0, 0)) for k in range(count))
        held[pl.ds(pl.multiple_of(inner * size, 16), size), start:start + width] = block
        start, lefts = start + width, lefts[count:]

    def rows_of(mask):
        return held[pl.ds(pl.multiple_of((place[0] ^ mask) * rows, 16), rows), :].astype(BF16)

    @pl.when(inner == steps - 1)
    def _():
        for k, mask in enumerate(own_groups[-1]):
            give[0, k * rows:(k + 1) * rows] = rows_of(mask)

    @pl.when((inner == steps - 1) & (turn_of < shards - 1))
    def _():
        for out, masks in zip(outs, groups):
            for k, mask in enumerate(masks):
                out[0, k * rows:(k + 1) * rows] = rows_of(mask)

    @pl.when((inner == steps - 1) & (turn_of == shards - 1))
    def _():
        for out, masks in zip(owns, own_groups):
            for k, mask in enumerate(masks):
                out[k * rows:(k + 1) * rows] = rows_of(mask)


def weight_grad(place, lefts, rights, rows, shards, groups, own_groups):
    width = sum(right.shape[1] for right in rights)
    flat = [array for arrays in lefts for array in arrays]
    steps = max(1, 4 * rows // 512)
    others = max(shards - 1, 1)

    def block(turn_of, inner, place):
        step = jnp.where(turn_of == shards - 1, 0, turn_of + 1)
        return (0, lax.rem(place[3] + step, shards) * steps + inner)

    def other(turn_of, inner, place):
        return (jnp.minimum(turn_of, others - 1), 0, 0)

    return call(
        functools.partial(weight_kernel, rows, shards, steps, [len(arrays) for arrays in lefts], groups, own_groups),
        [shape(others, len(masks) * rows, width) for masks in groups] + [shape(len(masks) * rows, width) for masks in own_groups[:-1]] + [shape(shards, len(own_groups[-1]) * rows, width)],
        [place, *flat, *rights], flops=2 * rights[0].shape[0] * flat[0].shape[1] * width, grid=(shards, steps),
        in_specs=[pl.BlockSpec((array.shape[0], 4 * rows // steps), block) for array in flat] + [whole(right) for right in rights],
        out_specs=[pl.BlockSpec((1, len(masks) * rows, width), other) for masks in groups]
        + [pl.BlockSpec((len(masks) * rows, width), lambda *_: (0, 0)) for masks in own_groups[:-1]]
        + [pl.BlockSpec((1, len(own_groups[-1]) * rows, width), lambda turn_of, inner, place: (turn_of, 0, 0))],
        scratch=[pltpu.VMEM((4 * rows, width), F32)])


def total_of(own, first, got, start, rows):
    own = own.at[own.shape[0] - 1] if len(own.shape) == 3 else own
    total = own[first:first + rows].astype(F32)
    for array in got:
        total = total + array[start:start + rows].astype(F32)
    return total.astype(BF16)


def sum_kernel(first, place, own, *refs):
    refs[-1][...] = total_of(own, first, refs[:-1], 0, refs[-1].shape[0])


def sum_two_kernel(place, keep, give, *refs):
    got, (first, second, away) = refs[:-3], refs[-3:]
    rows, half = first.shape[0], len(got) // 2
    for own, arrays, out, start in ((keep, got[:half], first, 0), (give, got[half:], second, rows)):
        out[...] = total_of(own, 0, arrays, 0, rows)
        away[start:start + rows] = total_of(own, rows, arrays, rows, rows)


def place_inner(column, starts, place, *refs):
    pieces, out = refs[:-1], refs[-1]
    rows, width = out.shape[0], out.shape[1] // 4
    for mask, (piece, start) in enumerate(zip(pieces, starts)):
        out[:, pl.ds(pl.multiple_of((place[0] ^ mask) * width, 128), width)] = piece[start:start + rows, column:column + width].astype(F32)


def place_joint(place, *refs):
    pieces, (qkv, dense) = refs[:-2], refs[-2:]
    for ctx in range(4):
        @pl.when(place[0] == ctx)
        def _(ctx=ctx):
            for mask, piece in enumerate(pieces):
                head, half = (ctx ^ mask) // 2, (ctx ^ mask) % 2
                for out, start, size, first in ((qkv, half * HEAD, HEAD, 0), (qkv, 2 * HEAD + half * HALF, HALF, HEAD),
                                                (dense, half * HALF, HALF, HEAD + HALF)):
                    out[:, head, start:start + size] = piece[:, first:first + size].astype(F32)


def output_kernel(rows, shards, pieces, place, context, hidden, joint, *refs):
    blocks, (keep, send, weight) = refs[:-3], refs[-3:]

    @pl.when(pl.program_id(0) == 0)
    def _():
        assemble(place, [(ref,) + p for ref, p in zip(blocks, pieces)], weight, rows, shards)

    step, size = pl.program_id(0), 512
    for first in range(0, keep.shape[1], size):
        here = slice(first, first + size)
        block = (dot(context[...], joint[here, HEAD + HALF:], (1, 1)) + dot(hidden[...], weight[here], (1, 1))).astype(BF16)
        keep[:, here] = jnp.where(step < 2, block, keep[:, here])
        send[:, here] = block


def back_kernel(place, grad, inner, joint, weight, gain_one, gain_two, plain, total, keep, send, small):
    step = pl.program_id(0)

    @pl.when(step == 0)
    def _():
        small[...] = jnp.zeros_like(small)
        small[4:5] = total[...]

    size = 512
    for first in range(0, keep.shape[1], size):
        here = slice(first, first + size)
        one = dot(grad[...], joint[here, :HEAD + HALF], (1, 1))
        two = dot(inner[...], weight[here], (1, 1))
        mixed = (one * gain_one[:, here] + two * gain_two[:, here]).astype(BF16)
        keep[:, here] = jnp.where(step < 2, mixed, keep[:, here])
        send[:, here] = mixed
        normal = plain[:, here].astype(F32)
        for row, value in ((0, one * normal), (1, one), (2, two * normal), (3, two)):
            small[row:row + 1, here] += jnp.sum(value, axis=0, keepdims=True)
    head, half = place[2], place[1]
    joined = jnp.sum(grad[...].astype(F32), axis=0, keepdims=True)
    for first, start, size in ((0, head * 3 * HEAD + half * HEAD, HEAD), (HEAD, head * 3 * HEAD + 2 * HEAD + half * HALF, HALF)):
        small[5:6, pl.ds(pl.multiple_of(start, 128), size)] += joined[:, first:first + size]
    width = inner.shape[1]
    small[6:7, pl.ds(pl.multiple_of(place[0] * width, 128), width)] += jnp.sum(inner[...].astype(F32), axis=0, keepdims=True)


def core_kernel(place, keep, got, *outs):
    rows = outs[0].shape[0]
    for k, out in enumerate(outs):
        here = slice(k * rows, (k + 1) * rows)
        out[...] = (keep[here].astype(F32) + got[here].astype(F32)).astype(BF16)


def add_kernel(choice, place, *refs):
    count = len(refs) // 3
    outer = (place[4] == 0) | (place[4] == 3)
    for k, out in enumerate(refs[2 * count:3 * count]):
        total = (refs[2 * k][...].astype(F32) + refs[2 * k + 1][...].astype(F32)).astype(BF16)
        out[...] = total
        if choice and k in choice:
            pl.when(outer if k == choice[0] else jnp.logical_not(outer))(lambda total=total: refs[-1].__setitem__(..., total))


def finished(place, refs, use):
    outer = (place[4] == 0) | (place[4] == 3)
    for k in range(0, len(refs), 2):
        rows = refs[k].shape[0]
        here = slice(k // 2 * rows, (k // 2 + 1) * rows)
        pl.when(outer)(lambda here=here, k=k: use(here, refs[k + 1][...].astype(F32)))
        pl.when(jnp.logical_not(outer))(lambda here=here, k=k: use(here, refs[k][...].astype(F32)))


def finish_output(place, values, bias, *refs):
    out = refs[-1]

    def use(here, total):
        out[here] = (values[here].astype(F32) + total + bias[...]).astype(BF16)

    finished(place, refs[:-1], use)


def finish_grad(place, values, grads, inner, outer, *refs):
    out = refs[-1]

    def use(total):
        residual = values[...].astype(F32)
        centred = residual - jnp.mean(residual, axis=1, keepdims=True)
        scale = lax.rsqrt(jnp.mean(centred * centred, axis=1, keepdims=True) + EPSILON)
        normal = centred * scale
        back = total - jnp.mean(total, axis=1, keepdims=True) - normal * jnp.mean(total * normal, axis=1, keepdims=True)
        out[...] = grads[...].astype(F32) + back * scale

    on_edge = (place[4] == 0) | (place[4] == 3)
    pl.when(on_edge)(lambda: use(outer[...].astype(F32)))
    pl.when(jnp.logical_not(on_edge))(lambda: use(inner[...].astype(F32)))


def local(inputs, cotangent, piece_starts, positions, w_qkv, b_qkv, w_dense, w_fc1, b_fc1, w_fc2, out_bias,
          ln1_gain, ln1_bias, ln2_gain, ln2_bias):
    span, width = inputs.shape[1:]
    rows = w_fc1.shape[0]
    shards = lax.axis_size("shard")
    shard, ctx, level = lax.axis_index("shard"), lax.axis_index("ctx"), lax.axis_index("tensor")
    place = jnp.stack([ctx, ctx % 2, ctx // 2, shard, level])
    length = 4 * span
    quarter = w_fc1.shape[1] // 4
    joint = 2 * HEAD
    values, grads = inputs.reshape(span, width), cotangent.reshape(span, width)
    starts = piece_starts.reshape(-1)
    row = lambda vector: vector.reshape(1, -1)
    steps = range(1, shards)

    recent = []

    def done(*values):
        recent.extend(values)
        del recent[:-8]

    def go(value):
        return after(value, *recent) if recent else value

    def half_of(block):
        size = span // 2
        return lax.dynamic_slice(block, ((level % 2) * size, 0), (size, width))

    def send(value, mask):
        return swap(go(value), mask)

    def send_y(value, sign=-1):
        value = go(value)
        return [shift(value if value.ndim == 2 else value[k - 1], sign * k) for k in steps]

    def send_z(value, mask):
        return level_swap(go(value), mask)

    def run(kernel, outs, args, **options):
        results = call(kernel, outs, [go(args[0]), *args[1:]], **options)
        done(results[0])
        return results

    def grad_of(lefts, rights, groups, own_groups):
        results = weight_grad(go(place), lefts, rights, rows, shards, groups, own_groups)
        done(results[-1])
        return results

    def columns(first):
        return [pl.BlockSpec((rows, quarter), lambda i, place: (0, place[0] ^ (first + i)))] * 2

    def blocked(array, count=4):
        return pl.BlockSpec((array.shape[0] // count, array.shape[1]), lambda i, *_: (i, 0))

    def gathered(near, near_y, x, x_y, d, d_y, first=0):
        found = [(array, (first, mask, 0)) for array, first, mask in near]
        found += [(array, (first, mask, k)) for arrays, first, mask in near_y for k, array in zip(steps, arrays)]
        for mask, array, arrays in ((2, x, x_y), (3, d, d_y)):
            found += [(array, (0, mask, 0))] + [(value, (0, mask, k)) for k, value in zip(steps, arrays)]
        return [array for array, _ in found], [piece for _, piece in found]

    def add(*pairs):
        return run(functools.partial(add_kernel, ()), [shape(*mine.shape) for mine, _ in pairs], [place, *[array for both in pairs for array in both]])

    def level_send(value, pairs):
        return lax.ppermute(go(value), "tensor", pairs)

    inward, across, outward, ends = [(0, 1), (3, 2)], [(1, 2), (2, 1)], [(1, 0), (2, 3)], [(0, 1), (1, 0), (2, 3), (3, 2)]

    def add_choose(choice, *pairs):
        some = pairs[0][0]
        return run(functools.partial(add_kernel, choice), [shape(*some.shape)] * (len(pairs) + 1), [place, *[array for both in pairs for array in both]])

    def finish_half(which, inner, outer, *before):
        half = pl.BlockSpec((span // 2, width), lambda i, *_: (which, 0))
        return run(finish_grad, [shape(span, width, kind=F32)], [place, values, grads, inner, outer, *before], grid=(1,),
                   in_specs=[half, half, whole(inner), whole(outer)] + [pl.BlockSpec(memory_space=pl.ANY)] * len(before), out_specs=[half],
                   alias={5: 0} if before else {})[0]

    first_half = pl.BlockSpec((span, width), lambda i, *_: (jnp.minimum(i, 1), 0))
    second_half = pl.BlockSpec((span, width), lambda i, *_: (jnp.maximum(i - 2, 0), 0))
    halves = [first_half, second_half]
    eighth = pl.BlockSpec((span // 2, width), lambda i, *_: (i, 0))
    gains = [row(vector) for vector in (ln1_gain, ln1_bias, ln2_gain, ln2_bias)]
    lanes = np.arange(HALF)
    frequency = np.where(lanes < ROT, ROPE_BASE ** (-(lanes % (ROT // 2)) * 2.0 / ROT), 0.0).astype(np.float32)[None]

    near_values = send(half_of(values), 2)
    outs = [shape(2 * rows, quarter)] * 2
    own, core = run(prepare_near, outs, [place, w_fc1, w_fc2], grid=(2,), limit=58, in_specs=columns(0), out_specs=[whole(o) for o in outs])
    own_y = send_y(own)
    core = send(core, 1)
    near_grads = send(half_of(grads), 2)
    joint_own, joint_core, joint_x, joint_d = run(
        prepare_joint, [shape(rows, joint)] * 4, [place, w_qkv, w_dense])
    joint_core = send(joint_core, 1)
    done(core)
    core_y = send_y(core)
    done(joint_core)
    cosine, sine = run(table_kernel, [shape(length, HALF, kind=F32)] * 2, [place, starts, jnp.asarray(frequency)], prefetch=1)
    done(*own_y)
    joint_near = jnp.concatenate([joint_own, joint_core])
    joint_near_y = send_y(joint_near)
    done(near_values)
    far_values = send_z(near_values, 1)
    joint_x = send(joint_x, 2)
    outs = [shape(rows, quarter)] * 4
    one_x, one_d, two_x, two_d = run(prepare_far, outs, [place, w_fc1, w_fc2], grid=(2,), in_specs=columns(2), out_specs=[whole(o) for o in outs])
    done(near_grads)
    joint_d = send(joint_d, 3)
    done(*core_y)
    far_grads = send_z(near_grads, 1)
    done(far_values)
    values_mine, = run(copy_kernel, [shape(2 * span, width)], [place, values, near_values, far_values], grid=(4,),
                       in_specs=[whole(values), whole(near_values), whole(far_values)], out_specs=[eighth])
    values_sib = send(values_mine, 1)
    done(values_sib)
    outs = [shape(length, width)] * 3
    normed_one, normed_two, plain = run(norm_kernel, outs, [place, values_mine, values_sib, *gains], grid=(4,),
                                        in_specs=halves + [whole(a) for a in gains], out_specs=[blocked(o) for o in outs])
    done(joint_x, joint_d, *joint_near_y, far_grads)
    joint_x_y = send_y(joint_x)
    joint_d_y = send_y(joint_d)
    one_x = send(one_x, 2)
    one_d = send(one_d, 3)
    grads_mine, grad_total = run(
        pair_kernel, [shape(2 * span, width), shape(1, width, kind=F32)], [place, grads, near_grads, far_grads], grid=(4,),
        in_specs=[whole(grads), whole(near_grads), whole(far_grads)], out_specs=[eighth, pl.BlockSpec((1, width), lambda *_: (0, 0))])
    pair = (grads_mine, send(grads_mine, 1))
    done(*joint_x_y, one_x, *joint_d_y, one_d, pair[1])
    two_x = send(two_x, 2)
    one_x_y = send_y(one_x)
    two_d = send(two_d, 3)
    one_d_y = send_y(one_d)
    joint_blocks = gathered([(joint_near, 0, 0), (joint_near, rows, 1)], [(joint_near_y, 0, 0), (joint_near_y, rows, 1)], joint_x, joint_x_y, joint_d, joint_d_y)
    args = [row(b_qkv.reshape(-1)), *joint_blocks[0]]
    outs = [shape(length, HEAD + HALF), shape(width, joint)]
    mine, w_joint = run(
        functools.partial(joint_kernel, rows, shards, joint_blocks[1]), outs, [place, normed_one, cosine, sine, *args],
        flops=2 * length * width * (HEAD + HALF), grid=(4,), in_specs=[blocked(normed_one), blocked(cosine), blocked(sine)] + [whole(a) for a in args],
        out_specs=[blocked(outs[0]), whole(outs[1])])
    outs = [shape(length, 2 * HEAD)]
    mine, = run(context_kernel, outs, [place, *pair, w_joint, mine], flops=2 * length * width * HALF, grid=(4,),
                in_specs=halves + [whole(w_joint), blocked(mine)], out_specs=[blocked(outs[0])])
    done(*one_x_y, two_x, *one_d_y, two_d)
    two_x_y = send_y(two_x)
    two_d_y = send_y(two_d)
    got = send(mine, 1)
    one_blocks = gathered([(own, 0, 0), (core, 0, 1)], [(own_y, 0, 0), (core_y, 0, 1)], one_x, one_x_y, one_d, one_d_y)
    args = [row(b_fc1), *one_blocks[0]]
    outs = [shape(length, quarter), shape(length, quarter, kind=F32), shape(width, quarter)]
    hidden, slope, fc1 = run(
        functools.partial(hidden_kernel, rows, shards, one_blocks[1]), outs, [place, normed_two, *args],
        flops=2 * length * width * quarter, grid=(4,), in_specs=[blocked(normed_two)] + [whole(a) for a in args],
        out_specs=[blocked(o) for o in outs[:2]] + [whole(outs[2])])
    done(got)
    context, grad_joined = run(
        attention_kernel, [shape(length, HALF), shape(length, HEAD + HALF)],
        [place, starts, mine, got, cosine, sine], prefetch=1, flops=8 * length * length * HEAD,
        scratch=[pltpu.VMEM((length, HEAD), BF16)] * 4 + [pltpu.VMEM((length, HEAD), F32), pltpu.VMEM((length, HALF), F32), pltpu.VMEM((length, length), BF16)])
    done(*two_x_y, *two_d_y)
    two_blocks = gathered([(own, rows, 0), (core, rows, 1)], [(own_y, rows, 0), (core_y, rows, 1)], two_x, two_x_y, two_d, two_d_y)
    args = [context, hidden, w_joint, *two_blocks[0]]
    keep, away, fc2 = run(
        functools.partial(output_kernel, rows, shards, two_blocks[1]), [shape(2 * span, width)] * 2 + [shape(width, quarter)], [place, *args],
        flops=2 * length * width * (HALF + quarter), grid=(4,),
        in_specs=[blocked(context), blocked(hidden)] + [whole(a) for a in args[2:]], out_specs=halves + [whole(shape(width, quarter))])
    got = send(away, 1)
    two_keep_y, two_keep, two_give = grad_of([pair], [hidden], ((0, 2),), ((0, 2), (1, 3)))
    done(got)
    quarters = [shape(span // 2, width)] * 4
    out_a, out_b, away_a, away_b = run(core_kernel, quarters, [place, keep, got])

    got_a = send(away_a, 2)
    two_keep_y = send_y(two_keep_y, 1)
    two_give = send(two_give, 1)
    outs = [shape(length, quarter)]
    grad_inner, = run(inner_kernel, outs, [place, *pair, slope, fc2], flops=2 * length * width * quarter, grid=(4,),
                      in_specs=halves + [blocked(slope), whole(fc2)], out_specs=[blocked(outs[0])])
    args = [grad_joined, grad_inner, w_joint, fc1, gains[0], gains[2], plain, grad_total]
    keep, away, small = run(
        back_kernel, [shape(2 * span, width)] * 2 + [shape(8, width, kind=F32)], [place, *args], flops=2 * length * width * (HEAD + HALF + quarter), grid=(4,),
        in_specs=[blocked(args[0]), blocked(args[1])] + [whole(a) for a in args[2:6]] + [blocked(plain), whole(grad_total)],
        out_specs=halves + [pl.BlockSpec((8, width), lambda *_: (0, 0))])
    done(got_a, *two_keep_y, two_give)
    out_a, = add((out_a, got_a))

    got_a = level_send(out_a, inward)
    got_b = send(away_b, 2)
    two_give_y = send_y(two_give, 1)
    got, small_got = send(away, 1), send(small, 1)
    far_y, near_y, rest, give = grad_of(
        [(normed_one,), pair, (normed_two,)], [grad_joined, context, grad_inner], ((2,), (0,)), ((2, 0), (3, 1)))
    done(small_got, got_a, got_b, *two_give_y, got)
    out_b, out_a = add((out_b, got_b), (out_a, got_a))
    back_a, back_b, back_away_a, back_away_b = run(core_kernel, quarters, [place, keep, got])

    got_b = level_send(out_b, inward)
    got_a = level_send(out_a, across)
    back_got_a = send(back_away_a, 2)
    far_y = send_y(far_y, 1)
    give = send(give, 1)
    two_first, two_second, two_away = run(sum_two_kernel, [shape(rows, quarter)] * 2 + [shape(2 * rows, quarter)],
                                          [place, two_keep, two_give, *two_keep_y, *two_give_y])
    small = small + small_got
    done(give, back_got_a, got_b, got_a, *far_y)
    back_a, out_a, out_b, away = add_choose((0, 1), (back_a, back_got_a), (out_a, got_a), (out_b, got_b))

    back_got_a = outer_a = level_send(away, ends)
    got_b = level_send(out_b, across)
    back_got_b = send(back_away_b, 2)
    give_far_y = send_y(give[:, :rows], 1)
    small_got = send(small, 2)
    wide = [shape(rows, joint + quarter)]
    away_one, = run(functools.partial(sum_kernel, 0), wide, [place, rest, *far_y])
    done(small_got, back_got_b, got_b, back_got_a, *give_far_y)
    back_a, out_b, back_b, away = add_choose((2, 1), (back_a, back_got_a), (out_b, got_b), (back_b, back_got_b))

    back_got_b = outer_b = level_send(away, ends)
    back_got_a = level_send(back_a, across)
    got_one = send(away_one, 2)
    near_y = send_y(near_y, 1)
    small = small + small_got
    small_got = send_z(small[:4], 1)
    away_two, = run(functools.partial(sum_kernel, 0), wide, [place, give, *give_far_y])
    done(small_got, got_one, back_got_b, back_got_a, *near_y)
    back_b, back_a = add((back_b, back_got_b), (back_a, back_got_a))

    back_got_a = level_send(back_a, outward)
    back_got_b = level_send(back_b, across)
    got_two = send(away_two, 2)
    give_near_y = send_y(give[:, rows:], 1)
    front = small[:4] + small_got
    small_got = send_z(front, 2)
    output, = run(finish_output, [shape(span, width)], [place, values, row(out_bias), out_a, outer_a, out_b, outer_b])
    first, = run(functools.partial(sum_kernel, rows), wide, [place, rest, *near_y])
    done(small_got, got_two, back_got_b, back_got_a, *give_near_y)
    back_b, = add((back_b, back_got_b))

    back_got_b = level_send(back_b, outward)
    two_got = send(two_away, 2)
    small = jnp.concatenate([front + small_got, small[4:]])
    small_got = send_y(small)
    second, = run(functools.partial(sum_kernel, rows), wide, [place, give, *give_near_y])
    pieces = [first, second, got_one, got_two]
    grad_inputs = finish_half(0, back_a, back_got_a)
    grad_w_qkv, grad_w_dense = run(place_joint, [shape(*w_qkv.shape, kind=F32), shape(*w_dense.shape, kind=F32)], [place, *pieces])
    full = [shape(rows, 4 * quarter, kind=F32)]
    grad_w_fc1, = run(functools.partial(place_inner, joint, (0, 0, 0, 0)), full, [place, *pieces])
    done(grad_w_qkv, grad_w_dense, *small_got)
    small = sum(small_got, small)
    done(two_got, back_got_b)
    grad_inputs = finish_half(1, back_b, back_got_b, grad_inputs)
    grad_w_fc2, = run(functools.partial(place_inner, 0, (0, 0, 0, rows)), full, [place, two_first, two_second, two_got, two_got])
    return (
        output[None],
        grad_inputs[None],
        grad_w_qkv,
        small[5, :b_qkv.size].reshape(b_qkv.shape),
        grad_w_dense,
        grad_w_fc1,
        small[6, :b_fc1.size],
        grad_w_fc2,
        small[4],
        small[0],
        small[1],
        small[2],
        small[3],
    )


def solution(mesh):
    rows = P(("shard", "ctx"), "tensor")
    tokens = P("shard", "ctx", None)
    heads = P(("shard", "ctx"), "tensor", None)
    in_specs = (tokens, tokens, P("shard", None), P("shard", "ctx"), heads, P("tensor", None), heads, rows, P("tensor"), rows,
                P(), P(), P(), P(), P())
    out_specs = (tokens, tokens, heads, P("tensor", None), heads, rows, P("tensor"), rows, P(), P(), P(), P(), P())
    return jax.shard_map(local, mesh=mesh, in_specs=in_specs, out_specs=out_specs, check_vma=False)
```

```python
import functools

import jax
import jax.numpy as jnp
import numpy as np
from jax import lax
from jax.experimental import pallas as pl
from jax.experimental.pallas import tpu as pltpu
from jax.sharding import PartitionSpec as P

HEAD = 256
HALF = HEAD // 2
ROT = 64
PIECE = 256
GRID = 16
PIECES = 3

EPSILON = 1e-05
ROPE_BASE = 10000.0
ORDER = (0, 2, 1, 3)
BF16 = jnp.bfloat16
F32 = jnp.float32
VMEM = pl.BlockSpec(memory_space=pltpu.VMEM)
LIMIT = 16
SMEM = pl.BlockSpec(memory_space=pltpu.SMEM)


def dot(left, right, dims):
    return lax.dot_general(left, right, ((dims[:1], dims[1:]), ((), ())), preferred_element_type=F32)


def shape(*dims, kind=BF16):
    return jax.ShapeDtypeStruct(dims, kind)


def call(kernel, outs, args, flops=0, grid=None, in_specs=None, out_specs=None, scratch=(), limit=LIMIT, prefetch=0, alias=()):
    if grid is None:
        extra = dict(in_specs=[SMEM] * (1 + prefetch) + [VMEM] * (len(args) - 1 - prefetch), out_specs=[VMEM] * len(outs), scratch_shapes=scratch)
    else:
        extra = dict(grid_spec=pltpu.PrefetchScalarGridSpec(num_scalar_prefetch=1 + prefetch, grid=grid, in_specs=in_specs, out_specs=out_specs, scratch_shapes=scratch))
    size = sum(a.size * a.dtype.itemsize for a in args) + sum(int(np.prod(o.shape)) * o.dtype.itemsize for o in outs)
    return pl.pallas_call(
        kernel, out_shape=outs, compiler_params=pltpu.CompilerParams(vmem_limit_bytes=limit * 2**20),
        cost_estimate=pl.CostEstimate(flops=1, bytes_accessed=1, transcendentals=0), input_output_aliases=dict(alias), **extra,
    )(*args)


def whole(array):
    return pl.BlockSpec(array.shape, lambda *_: (0,) * len(array.shape))


def swap(value, mask):
    return lax.ppermute(value, "ctx", [(i, i ^ mask) for i in range(4)])


def level_swap(value, mask):
    return lax.ppermute(value, "tensor", [(i, i ^ mask) for i in range(4)])


def after(value, *others):
    return lax.optimization_barrier((value,) + others)[0]


def shift(value, step):
    size = lax.axis_size("shard")
    return lax.ppermute(value, "shard", [(i, (i + step) % size) for i in range(size)])


def part(ref, start, size):
    return ref[:, pl.ds(pl.multiple_of(start, 128), size)]


def prepare_joint(place, qkv, dense, *outs):
    for ctx in range(4):
        @pl.when(place[0] == ctx)
        def _(ctx=ctx):
            for mask, out in enumerate(outs):
                head, half = (ctx ^ mask) // 2, (ctx ^ mask) % 2
                out[:, :HEAD] = qkv[:, head, half * HEAD:half * HEAD + HEAD].astype(BF16)
                out[:, HEAD:HEAD + HALF] = qkv[:, head, 2 * HEAD + half * HALF:2 * HEAD + half * HALF + HALF].astype(BF16)
                out[:, HEAD + HALF:] = dense[:, head, half * HALF:half * HALF + HALF].astype(BF16)


def prepare_near(place, one, two, own, core):
    rows = one.shape[0]
    for mask, out in ((0, own), (1, core)):
        @pl.when(pl.program_id(0) == mask)
        def _(out=out):
            out[:rows] = one[...].astype(BF16)
            out[rows:] = two[...].astype(BF16)


def prepare_far(place, one, two, one_x, one_d, two_x, two_d):
    for mask, first, second in ((0, one_x, two_x), (1, one_d, two_d)):
        @pl.when(pl.program_id(0) == mask)
        def _(first=first, second=second):
            first[...] = one[...].astype(BF16)
            second[...] = two[...].astype(BF16)


def assemble(place, pieces, out, rows, shards):
    for ref, first, mask, step in pieces:
        to = lax.rem(place[3] + step, shards) * 4 * rows + (place[0] ^ mask) * rows
        out[pl.ds(pl.multiple_of(to, 16), rows), :] = ref[first:first + rows, :]


def token_block(place, own, near, far, use):
    step, same = pl.program_id(0), place[4] & 1
    for k in (0, 1):
        pl.when(step == k)(lambda k=k: use(own[k * 128:(k + 1) * 128, :]))
    pl.when(step == 2 + same)(lambda: use(near[...]))
    pl.when(step == 3 - same)(lambda: use(far[...]))


def pair_kernel(place, own, near, far, out, total):
    token_block(place, own, near, far, lambda block: out.__setitem__(..., block))

    @pl.when(pl.program_id(0) == 0)
    def _():
        total[...] = jnp.sum(own[...].astype(F32), axis=0, keepdims=True)


def copy_kernel(place, own, near, far, out):
    token_block(place, own, near, far, lambda block: out.__setitem__(..., block))


def norm_kernel(place, first, second, gain_one, shift_one, gain_two, shift_two, one, two, plain):
    values = either(first, second).astype(F32)
    centred = values - jnp.mean(values, axis=1, keepdims=True)
    normal = centred * lax.rsqrt(jnp.mean(centred * centred, axis=1, keepdims=True) + EPSILON)
    one[...] = (normal * gain_one[...] + shift_one[...]).astype(BF16)
    two[...] = (normal * gain_two[...] + shift_two[...]).astype(BF16)
    plain[...] = normal.astype(BF16)


def either(first, second):
    return jnp.where(pl.program_id(0) < 2, first[...], second[...])


def global_index(place, local, block):
    index = local
    for p in range(4):
        index = jnp.where(local // block == p, local % block + (place[0] ^ ORDER[p]) * block, index)
    return index


def turn(front, cosine, sine):
    lane = lax.broadcasted_iota(jnp.int32, front.shape, 1)
    swapped = jnp.where(lane < ROT // 2, pltpu.roll(front, HALF - ROT // 2, 1), pltpu.roll(front, ROT // 2, 1))
    return front * cosine + swapped * sine


def table_kernel(place, starts, frequency, cosine, sine):
    length = cosine.shape[0]
    index = global_index(place, lax.broadcasted_iota(jnp.int32, (length, 1), 0), length // 4)
    places = index
    for j in range(PIECES):
        inside = jnp.clip(index - starts[j] + 1, 0, PIECE)
        places = places - inside + (inside + GRID - 1) // GRID
    angles = places.astype(F32) * frequency[...]
    lane = lax.broadcasted_iota(jnp.int32, cosine.shape, 1)
    cosine[...] = jnp.cos(angles)
    sine[...] = jnp.where(lane < ROT // 2, -1.0, 1.0) * jnp.sin(angles)


def joint_kernel(rows, shards, pieces, place, normed, cosine, sine, bias, *refs):
    blocks, (mine, weight) = refs[:-2], refs[-2:]

    @pl.when(pl.program_id(0) == 0)
    def _():
        assemble(place, [(ref,) + p for ref, p in zip(blocks, pieces)], weight, rows, shards)

    joined = dot(normed[...], weight[:, :HEAD + HALF], (1, 0))
    head, half = place[2], place[1]
    joined_low = joined[:, :HEAD] + part(bias, head * 3 * HEAD + half * HEAD, HEAD)
    mine[:, :HALF] = turn(joined_low[:, :HALF], cosine[...], sine[...]).astype(BF16)
    mine[:, HALF:HEAD] = joined_low[:, HALF:].astype(BF16)
    mine[:, HEAD:] = (joined[:, HEAD:] + part(bias, head * 3 * HEAD + 2 * HEAD + half * HALF, HALF)).astype(BF16)


def context_kernel(place, first, second, weight, mine, out):
    out[:, :HEAD + HALF] = mine[...]
    out[:, HEAD + HALF:] = dot(either(first, second), weight[:, HEAD + HALF:], (1, 0)).astype(BF16)


def attention_kernel(place, starts, mine, got, cosine, sine, context, grad, queries, keys, values, grads, acc, value_acc, back):
    core = place[1]
    length = mine.shape[0]
    half, block = length // 2, length // 4
    scale = HEAD ** (-0.5)
    for p in range(4):
        rows = slice(p * block, (p + 1) * block)
        first = (p * block + half) % length
        theirs = slice(first, first + block)

        @pl.when(core == 0)
        def _():
            queries[rows] = mine[rows, :HEAD]
            keys[rows] = got[theirs, :HEAD]

        @pl.when(core == 1)
        def _():
            queries[rows] = got[theirs, :HEAD]
            keys[rows] = mine[rows, :HEAD]

        values[rows, :HALF] = mine[rows, HEAD:HEAD + HALF]
        values[rows, HALF:] = got[theirs, HEAD:HEAD + HALF]
        grads[rows, :HALF] = mine[rows, HEAD + HALF:]
        grads[rows, HALF:] = got[theirs, HEAD + HALF:]

    def numbers(index):
        label = jnp.zeros_like(index)
        for j in range(PIECES):
            label = jnp.where((index >= starts[j]) & (index < starts[j] + PIECE), j + 1, label)
        return label

    key_index = global_index(place, lax.broadcasted_iota(jnp.int32, (1, length), 1), block)
    key_piece = numbers(key_index)
    for p in range(4):
        rows = slice(p * block, (p + 1) * block)
        query_index = lax.broadcasted_iota(jnp.int32, (block, 1), 0) + (place[0] ^ ORDER[p]) * block
        query_piece = numbers(query_index)
        allowed = (key_index <= query_index) | ((key_piece == query_piece) & (query_piece > 0))
        scores = jnp.where(allowed, dot(queries[rows], keys[...], (1, 1)) * scale, -1e30)
        weights = jnp.exp(scores - jnp.max(scores, axis=1, keepdims=True))
        weights = weights / jnp.sum(weights, axis=1, keepdims=True)
        low = weights.astype(BF16)
        context[rows] = dot(low, values[:, :HALF], (1, 0)).astype(BF16)
        term = dot(low, grads[rows, :HALF], (0, 0))
        value_acc[...] = term if p == 0 else value_acc[...] + term
        grad_weights = dot(grads[rows], values[...], (1, 1))
        centre = jnp.sum(weights * grad_weights, axis=1, keepdims=True)
        back[rows] = (weights * (grad_weights - centre)).astype(BF16)

    @pl.when(core == 0)
    def _():
        acc[...] = dot(back[...], keys[...], (1, 0)) * scale

    @pl.when(core == 1)
    def _():
        acc[...] = dot(back[...], queries[...], (0, 0)) * scale

    grad[:, HEAD:] = value_acc[...].astype(BF16)
    grad[:, HALF:HEAD] = acc[:, HALF:].astype(BF16)
    grad[:, :HALF] = turn(acc[:, :HALF], cosine[...], -sine[...]).astype(BF16)


def hidden_kernel(rows, shards, pieces, place, normed, bias, *refs):
    blocks, (hidden, slope, weight) = refs[:-3], refs[-3:]

    @pl.when(pl.program_id(0) == 0)
    def _():
        assemble(place, [(ref,) + p for ref, p in zip(blocks, pieces)], weight, rows, shards)

    width = hidden.shape[1]
    pre = dot(normed[...], weight[...], (1, 0)) + part(bias, place[0] * width, width)
    cdf = 0.5 + 0.5 * lax.erf(pre * (0.5 ** 0.5))
    hidden[...] = (pre * cdf).astype(BF16)
    slope[...] = cdf + pre * jnp.exp(-0.5 * pre * pre) * ((0.5 / np.pi) ** 0.5)


def inner_kernel(place, first, second, slope, weight, inner):
    inner[...] = (dot(either(first, second), weight[...], (1, 0)) * slope[...]).astype(BF16)


def weight_kernel(rows, shards, steps, counts, groups, own_groups, place, *refs):
    lefts, rights, outs = refs[:sum(counts)], refs[sum(counts):sum(counts) + len(counts)], refs[sum(counts) + len(counts):]
    outs, owns, held = outs[:len(groups)], outs[len(groups):-1], outs[-1]
    turn_of, inner = pl.program_id(0), pl.program_id(1)
    size = 4 * rows // steps
    start = 0
    give, owns = owns[-1], owns[:-1]
    for count, right in zip(counts, rights):
        width, length = right.shape[1], right.shape[0] // count
        block = sum(dot(lefts[k][...], right[k * length:(k + 1) * length], (0, 0)) for k in range(count))
        held[pl.ds(pl.multiple_of(inner * size, 16), size), start:start + width] = block
        start, lefts = start + width, lefts[count:]

    def rows_of(mask):
        return held[pl.ds(pl.multiple_of((place[0] ^ mask) * rows, 16), rows), :].astype(BF16)

    @pl.when(inner == steps - 1)
    def _():
        for k, mask in enumerate(own_groups[-1]):
            give[0, k * rows:(k + 1) * rows] = rows_of(mask)

    @pl.when((inner == steps - 1) & (turn_of < shards - 1))
    def _():
        for out, masks in zip(outs, groups):
            for k, mask in enumerate(masks):
                out[0, k * rows:(k + 1) * rows] = rows_of(mask)

    @pl.when((inner == steps - 1) & (turn_of == shards - 1))
    def _():
        for out, masks in zip(owns, own_groups):
            for k, mask in enumerate(masks):
                out[k * rows:(k + 1) * rows] = rows_of(mask)


def weight_grad(place, lefts, rights, rows, shards, groups, own_groups):
    width = sum(right.shape[1] for right in rights)
    flat = [array for arrays in lefts for array in arrays]
    steps = max(1, 4 * rows // 512)
    others = max(shards - 1, 1)

    def block(turn_of, inner, place):
        step = jnp.where(turn_of == shards - 1, 0, turn_of + 1)
        return (0, lax.rem(place[3] + step, shards) * steps + inner)

    def other(turn_of, inner, place):
        return (jnp.minimum(turn_of, others - 1), 0, 0)

    return call(
        functools.partial(weight_kernel, rows, shards, steps, [len(arrays) for arrays in lefts], groups, own_groups),
        [shape(others, len(masks) * rows, width) for masks in groups] + [shape(len(masks) * rows, width) for masks in own_groups[:-1]] + [shape(shards, len(own_groups[-1]) * rows, width)],
        [place, *flat, *rights], flops=2 * rights[0].shape[0] * flat[0].shape[1] * width, grid=(shards, steps),
        in_specs=[pl.BlockSpec((array.shape[0], 4 * rows // steps), block) for array in flat] + [whole(right) for right in rights],
        out_specs=[pl.BlockSpec((1, len(masks) * rows, width), other) for masks in groups]
        + [pl.BlockSpec((len(masks) * rows, width), lambda *_: (0, 0)) for masks in own_groups[:-1]]
        + [pl.BlockSpec((1, len(own_groups[-1]) * rows, width), lambda turn_of, inner, place: (turn_of, 0, 0))],
        scratch=[pltpu.VMEM((4 * rows, width), F32)])


def total_of(own, first, got, start, rows):
    own = own.at[own.shape[0] - 1] if len(own.shape) == 3 else own
    total = own[first:first + rows].astype(F32)
    for array in got:
        total = total + array[start:start + rows].astype(F32)
    return total.astype(BF16)


def sum_kernel(first, place, own, *refs):
    refs[-1][...] = total_of(own, first, refs[:-1], 0, refs[-1].shape[0])


def sum_two_kernel(place, keep, give, *refs):
    got, (first, second, away) = refs[:-3], refs[-3:]
    rows, half = first.shape[0], len(got) // 2
    for own, arrays, out, start in ((keep, got[:half], first, 0), (give, got[half:], second, rows)):
        out[...] = total_of(own, 0, arrays, 0, rows)
        away[start:start + rows] = total_of(own, rows, arrays, rows, rows)


def place_inner(column, starts, place, *refs):
    pieces, out = refs[:-1], refs[-1]
    rows, width = out.shape[0], out.shape[1] // 4
    for mask, (piece, start) in enumerate(zip(pieces, starts)):
        out[:, pl.ds(pl.multiple_of((place[0] ^ mask) * width, 128), width)] = piece[start:start + rows, column:column + width].astype(F32)


def place_joint(place, *refs):
    pieces, (qkv, dense) = refs[:-2], refs[-2:]
    for ctx in range(4):
        @pl.when(place[0] == ctx)
        def _(ctx=ctx):
            for mask, piece in enumerate(pieces):
                head, half = (ctx ^ mask) // 2, (ctx ^ mask) % 2
                for out, start, size, first in ((qkv, half * HEAD, HEAD, 0), (qkv, 2 * HEAD + half * HALF, HALF, HEAD),
                                                (dense, half * HALF, HALF, HEAD + HALF)):
                    out[:, head, start:start + size] = piece[:, first:first + size].astype(F32)


def output_kernel(rows, shards, pieces, place, context, hidden, joint, *refs):
    blocks, (keep, send, weight) = refs[:-3], refs[-3:]

    @pl.when(pl.program_id(0) == 0)
    def _():
        assemble(place, [(ref,) + p for ref, p in zip(blocks, pieces)], weight, rows, shards)

    step, size = pl.program_id(0), 512
    for first in range(0, keep.shape[1], size):
        here = slice(first, first + size)
        block = (dot(context[...], joint[here, HEAD + HALF:], (1, 1)) + dot(hidden[...], weight[here], (1, 1))).astype(BF16)
        keep[:, here] = jnp.where(step < 2, block, keep[:, here])
        send[:, here] = block


def back_kernel(place, grad, inner, joint, weight, gain_one, gain_two, plain, total, keep, send, small):
    step = pl.program_id(0)

    @pl.when(step == 0)
    def _():
        small[...] = jnp.zeros_like(small)
        small[4:5] = total[...]

    size = 512
    for first in range(0, keep.shape[1], size):
        here = slice(first, first + size)
        one = dot(grad[...], joint[here, :HEAD + HALF], (1, 1))
        two = dot(inner[...], weight[here], (1, 1))
        mixed = (one * gain_one[:, here] + two * gain_two[:, here]).astype(BF16)
        keep[:, here] = jnp.where(step < 2, mixed, keep[:, here])
        send[:, here] = mixed
        normal = plain[:, here].astype(F32)
        for row, value in ((0, one * normal), (1, one), (2, two * normal), (3, two)):
            small[row:row + 1, here] += jnp.sum(value, axis=0, keepdims=True)
    head, half = place[2], place[1]
    joined = jnp.sum(grad[...].astype(F32), axis=0, keepdims=True)
    for first, start, size in ((0, head * 3 * HEAD + half * HEAD, HEAD), (HEAD, head * 3 * HEAD + 2 * HEAD + half * HALF, HALF)):
        small[5:6, pl.ds(pl.multiple_of(start, 128), size)] += joined[:, first:first + size]
    width = inner.shape[1]
    small[6:7, pl.ds(pl.multiple_of(place[0] * width, 128), width)] += jnp.sum(inner[...].astype(F32), axis=0, keepdims=True)


def core_kernel(place, keep, got, *outs):
    rows = outs[0].shape[0]
    for k, out in enumerate(outs):
        here = slice(k * rows, (k + 1) * rows)
        out[...] = (keep[here].astype(F32) + got[here].astype(F32)).astype(BF16)


def add_kernel(choice, place, *refs):
    count = len(refs) // 3
    outer = (place[4] == 0) | (place[4] == 3)
    for k, out in enumerate(refs[2 * count:3 * count]):
        total = (refs[2 * k][...].astype(F32) + refs[2 * k + 1][...].astype(F32)).astype(BF16)
        out[...] = total
        if choice and k in choice:
            pl.when(outer if k == choice[0] else jnp.logical_not(outer))(lambda total=total: refs[-1].__setitem__(..., total))


def finished(place, refs, use):
    outer = (place[4] == 0) | (place[4] == 3)
    for k in range(0, len(refs), 2):
        rows = refs[k].shape[0]
        here = slice(k // 2 * rows, (k // 2 + 1) * rows)
        pl.when(outer)(lambda here=here, k=k: use(here, refs[k + 1][...].astype(F32)))
        pl.when(jnp.logical_not(outer))(lambda here=here, k=k: use(here, refs[k][...].astype(F32)))


def finish_output(place, values, bias, *refs):
    out = refs[-1]

    def use(here, total):
        out[here] = (values[here].astype(F32) + total + bias[...]).astype(BF16)

    finished(place, refs[:-1], use)


def finish_grad(place, values, grads, inner, outer, *refs):
    out = refs[-1]

    def use(total):
        residual = values[...].astype(F32)
        centred = residual - jnp.mean(residual, axis=1, keepdims=True)
        scale = lax.rsqrt(jnp.mean(centred * centred, axis=1, keepdims=True) + EPSILON)
        normal = centred * scale
        back = total - jnp.mean(total, axis=1, keepdims=True) - normal * jnp.mean(total * normal, axis=1, keepdims=True)
        out[...] = grads[...].astype(F32) + back * scale

    on_edge = (place[4] == 0) | (place[4] == 3)
    pl.when(on_edge)(lambda: use(outer[...].astype(F32)))
    pl.when(jnp.logical_not(on_edge))(lambda: use(inner[...].astype(F32)))


def local(inputs, cotangent, piece_starts, positions, w_qkv, b_qkv, w_dense, w_fc1, b_fc1, w_fc2, out_bias,
          ln1_gain, ln1_bias, ln2_gain, ln2_bias):
    span, width = inputs.shape[1:]
    rows = w_fc1.shape[0]
    shards = lax.axis_size("shard")
    shard, ctx, level = lax.axis_index("shard"), lax.axis_index("ctx"), lax.axis_index("tensor")
    place = jnp.stack([ctx, ctx % 2, ctx // 2, shard, level])
    length = 4 * span
    quarter = w_fc1.shape[1] // 4
    joint = 2 * HEAD
    values, grads = inputs.reshape(span, width), cotangent.reshape(span, width)
    starts = piece_starts.reshape(-1)
    row = lambda vector: vector.reshape(1, -1)
    steps = range(1, shards)

    recent = []

    def done(*values):
        recent.extend(values)
        del recent[:-8]

    def go(value):
        return after(value, *recent) if recent else value

    def half_of(block):
        size = span // 2
        return lax.dynamic_slice(block, ((level % 2) * size, 0), (size, width))

    def send(value, mask):
        return swap(go(value), mask)

    def send_y(value, sign=-1):
        value = go(value)
        return [shift(value if value.ndim == 2 else value[k - 1], sign * k) for k in steps]

    def send_z(value, mask):
        return level_swap(go(value), mask)

    def run(kernel, outs, args, **options):
        results = call(kernel, outs, [go(args[0]), *args[1:]], **options)
        done(results[0])
        return results

    def grad_of(lefts, rights, groups, own_groups):
        results = weight_grad(go(place), lefts, rights, rows, shards, groups, own_groups)
        done(results[-1])
        return results

    def columns(first):
        return [pl.BlockSpec((rows, quarter), lambda i, place: (0, place[0] ^ (first + i)))] * 2

    def blocked(array, count=4):
        return pl.BlockSpec((array.shape[0] // count, array.shape[1]), lambda i, *_: (i, 0))

    def gathered(near, near_y, x, x_y, d, d_y, first=0):
        found = [(array, (first, mask, 0)) for array, first, mask in near]
        found += [(array, (first, mask, k)) for arrays, first, mask in near_y for k, array in zip(steps, arrays)]
        for mask, array, arrays in ((2, x, x_y), (3, d, d_y)):
            found += [(array, (0, mask, 0))] + [(value, (0, mask, k)) for k, value in zip(steps, arrays)]
        return [array for array, _ in found], [piece for _, piece in found]

    def add(*pairs):
        return run(functools.partial(add_kernel, ()), [shape(*mine.shape) for mine, _ in pairs], [place, *[array for both in pairs for array in both]])

    def level_send(value, pairs):
        return lax.ppermute(go(value), "tensor", pairs)

    inward, across, outward, ends = [(0, 1), (3, 2)], [(1, 2), (2, 1)], [(1, 0), (2, 3)], [(0, 1), (1, 0), (2, 3), (3, 2)]

    def add_choose(choice, *pairs):
        some = pairs[0][0]
        return run(functools.partial(add_kernel, choice), [shape(*some.shape)] * (len(pairs) + 1), [place, *[array for both in pairs for array in both]])

    def finish_half(which, inner, outer, *before):
        half = pl.BlockSpec((span // 4, width), lambda i, *_: (2 * which + i, 0))
        piece = pl.BlockSpec((span // 4, width), lambda i, *_: (i, 0))
        return run(finish_grad, [shape(span, width, kind=F32)], [place, values, grads, inner, outer, *before], grid=(2,),
                   in_specs=[half, half, piece, piece] + [pl.BlockSpec(memory_space=pl.ANY)] * len(before), out_specs=[half],
                   alias={5: 0} if before else {})[0]

    first_half = pl.BlockSpec((span, width), lambda i, *_: (jnp.minimum(i, 1), 0))
    second_half = pl.BlockSpec((span, width), lambda i, *_: (jnp.maximum(i - 2, 0), 0))
    halves = [first_half, second_half]
    eighth = pl.BlockSpec((span // 2, width), lambda i, *_: (i, 0))
    gains = [row(vector) for vector in (ln1_gain, ln1_bias, ln2_gain, ln2_bias)]
    lanes = np.arange(HALF)
    frequency = np.where(lanes < ROT, ROPE_BASE ** (-(lanes % (ROT // 2)) * 2.0 / ROT), 0.0).astype(np.float32)[None]

    near_values = send(half_of(values), 2)
    outs = [shape(2 * rows, quarter)] * 2
    own, core = run(prepare_near, outs, [place, w_fc1, w_fc2], grid=(2,), limit=58, in_specs=columns(0), out_specs=[whole(o) for o in outs])
    own_y = send_y(own)
    core = send(core, 1)
    near_grads = send(half_of(grads), 2)
    joint_own, joint_core, joint_x, joint_d = run(
        prepare_joint, [shape(rows, joint)] * 4, [place, w_qkv, w_dense])
    joint_core = send(joint_core, 1)
    done(core)
    core_y = send_y(core)
    done(joint_core)
    cosine, sine = run(table_kernel, [shape(length, HALF, kind=F32)] * 2, [place, starts, jnp.asarray(frequency)], prefetch=1)
    done(*own_y)
    joint_near = jnp.concatenate([joint_own, joint_core])
    joint_near_y = send_y(joint_near)
    done(near_values)
    far_values = send_z(near_values, 1)
    joint_x = send(joint_x, 2)
    outs = [shape(rows, quarter)] * 4
    one_x, one_d, two_x, two_d = run(prepare_far, outs, [place, w_fc1, w_fc2], grid=(2,), in_specs=columns(2), out_specs=[whole(o) for o in outs])
    done(near_grads)
    joint_d = send(joint_d, 3)
    done(*core_y)
    far_grads = send_z(near_grads, 1)
    done(far_values)
    values_mine, = run(copy_kernel, [shape(2 * span, width)], [place, values, near_values, far_values], grid=(4,),
                       in_specs=[whole(values), whole(near_values), whole(far_values)], out_specs=[eighth])
    values_sib = send(values_mine, 1)
    done(values_sib)
    outs = [shape(length, width)] * 3
    normed_one, normed_two, plain = run(norm_kernel, outs, [place, values_mine, values_sib, *gains], grid=(4,),
                                        in_specs=halves + [whole(a) for a in gains], out_specs=[blocked(o) for o in outs])
    done(joint_x, joint_d, *joint_near_y, far_grads)
    joint_x_y = send_y(joint_x)
    joint_d_y = send_y(joint_d)
    one_x = send(one_x, 2)
    one_d = send(one_d, 3)
    grads_mine, grad_total = run(
        pair_kernel, [shape(2 * span, width), shape(1, width, kind=F32)], [place, grads, near_grads, far_grads], grid=(4,),
        in_specs=[whole(grads), whole(near_grads), whole(far_grads)], out_specs=[eighth, pl.BlockSpec((1, width), lambda *_: (0, 0))])
    pair = (grads_mine, send(grads_mine, 1))
    done(*joint_x_y, one_x, *joint_d_y, one_d, pair[1])
    two_x = send(two_x, 2)
    one_x_y = send_y(one_x)
    two_d = send(two_d, 3)
    one_d_y = send_y(one_d)
    joint_blocks = gathered([(joint_near, 0, 0), (joint_near, rows, 1)], [(joint_near_y, 0, 0), (joint_near_y, rows, 1)], joint_x, joint_x_y, joint_d, joint_d_y)
    args = [row(b_qkv.reshape(-1)), *joint_blocks[0]]
    outs = [shape(length, HEAD + HALF), shape(width, joint)]
    mine, w_joint = run(
        functools.partial(joint_kernel, rows, shards, joint_blocks[1]), outs, [place, normed_one, cosine, sine, *args],
        flops=2 * length * width * (HEAD + HALF), grid=(4,), in_specs=[blocked(normed_one), blocked(cosine), blocked(sine)] + [whole(a) for a in args],
        out_specs=[blocked(outs[0]), whole(outs[1])])
    outs = [shape(length, 2 * HEAD)]
    mine, = run(context_kernel, outs, [place, *pair, w_joint, mine], flops=2 * length * width * HALF, grid=(4,),
                in_specs=halves + [whole(w_joint), blocked(mine)], out_specs=[blocked(outs[0])])
    done(*one_x_y, two_x, *one_d_y, two_d)
    two_x_y = send_y(two_x)
    two_d_y = send_y(two_d)
    got = send(mine, 1)
    one_blocks = gathered([(own, 0, 0), (core, 0, 1)], [(own_y, 0, 0), (core_y, 0, 1)], one_x, one_x_y, one_d, one_d_y)
    args = [row(b_fc1), *one_blocks[0]]
    outs = [shape(length, quarter), shape(length, quarter, kind=F32), shape(width, quarter)]
    hidden, slope, fc1 = run(
        functools.partial(hidden_kernel, rows, shards, one_blocks[1]), outs, [place, normed_two, *args],
        flops=2 * length * width * quarter, grid=(4,), in_specs=[blocked(normed_two)] + [whole(a) for a in args],
        out_specs=[blocked(o) for o in outs[:2]] + [whole(outs[2])])
    done(got)
    context, grad_joined = run(
        attention_kernel, [shape(length, HALF), shape(length, HEAD + HALF)],
        [place, starts, mine, got, cosine, sine], prefetch=1, flops=8 * length * length * HEAD,
        scratch=[pltpu.VMEM((length, HEAD), BF16)] * 4 + [pltpu.VMEM((length, HEAD), F32), pltpu.VMEM((length, HALF), F32), pltpu.VMEM((length, length), BF16)])
    done(*two_x_y, *two_d_y)
    two_blocks = gathered([(own, rows, 0), (core, rows, 1)], [(own_y, rows, 0), (core_y, rows, 1)], two_x, two_x_y, two_d, two_d_y)
    args = [context, hidden, w_joint, *two_blocks[0]]
    keep, away, fc2 = run(
        functools.partial(output_kernel, rows, shards, two_blocks[1]), [shape(2 * span, width)] * 2 + [shape(width, quarter)], [place, *args],
        flops=2 * length * width * (HALF + quarter), grid=(4,),
        in_specs=[blocked(context), blocked(hidden)] + [whole(a) for a in args[2:]], out_specs=halves + [whole(shape(width, quarter))])
    got = send(away, 1)
    two_keep_y, two_keep, two_give = grad_of([pair], [hidden], ((0, 2),), ((0, 2), (1, 3)))
    done(got)
    quarters = [shape(span // 2, width)] * 4
    out_a, out_b, away_a, away_b = run(core_kernel, quarters, [place, keep, got])

    got_a = send(away_a, 2)
    two_keep_y = send_y(two_keep_y, 1)
    two_give = send(two_give, 1)
    outs = [shape(length, quarter)]
    grad_inner, = run(inner_kernel, outs, [place, *pair, slope, fc2], flops=2 * length * width * quarter, grid=(4,),
                      in_specs=halves + [blocked(slope), whole(fc2)], out_specs=[blocked(outs[0])])
    args = [grad_joined, grad_inner, w_joint, fc1, gains[0], gains[2], plain, grad_total]
    keep, away, small = run(
        back_kernel, [shape(2 * span, width)] * 2 + [shape(8, width, kind=F32)], [place, *args], flops=2 * length * width * (HEAD + HALF + quarter), grid=(4,),
        in_specs=[blocked(args[0]), blocked(args[1])] + [whole(a) for a in args[2:6]] + [blocked(plain), whole(grad_total)],
        out_specs=halves + [pl.BlockSpec((8, width), lambda *_: (0, 0))])
    done(got_a, *two_keep_y, two_give)
    out_a, = add((out_a, got_a))

    got_a = level_send(out_a, inward)
    got_b = send(away_b, 2)
    two_give_y = send_y(two_give, 1)
    got, small_got = send(away, 1), send(small, 1)
    far_y, near_y, rest, give = grad_of(
        [(normed_one,), pair, (normed_two,)], [grad_joined, context, grad_inner], ((2,), (0,)), ((2, 0), (3, 1)))
    done(small_got, got_a, got_b, *two_give_y, got)
    out_b, out_a = add((out_b, got_b), (out_a, got_a))
    back_a, back_b, back_away_a, back_away_b = run(core_kernel, quarters, [place, keep, got])

    got_b = level_send(out_b, inward)
    got_a = level_send(out_a, across)
    back_got_a = send(back_away_a, 2)
    far_y = send_y(far_y, 1)
    give = send(give, 1)
    two_first, two_second, two_away = run(sum_two_kernel, [shape(rows, quarter)] * 2 + [shape(2 * rows, quarter)],
                                          [place, two_keep, two_give, *two_keep_y, *two_give_y])
    small = small + small_got
    done(give, back_got_a, got_b, got_a, *far_y)
    back_a, out_a, out_b, away = add_choose((0, 1), (back_a, back_got_a), (out_a, got_a), (out_b, got_b))

    back_got_a = outer_a = level_send(away, ends)
    got_b = level_send(out_b, across)
    back_got_b = send(back_away_b, 2)
    give_far_y = send_y(give[:, :rows], 1)
    small_got = send(small, 2)
    wide = [shape(rows, joint + quarter)]
    away_one, = run(functools.partial(sum_kernel, 0), wide, [place, rest, *far_y])
    done(small_got, back_got_b, got_b, back_got_a, *give_far_y)
    back_a, out_b, back_b, away = add_choose((2, 1), (back_a, back_got_a), (out_b, got_b), (back_b, back_got_b))

    back_got_b = outer_b = level_send(away, ends)
    back_got_a = level_send(back_a, across)
    got_one = send(away_one, 2)
    near_y = send_y(near_y, 1)
    small = small + small_got
    small_got = send_z(small[:4], 1)
    away_two, = run(functools.partial(sum_kernel, 0), wide, [place, give, *give_far_y])
    done(small_got, got_one, back_got_b, back_got_a, *near_y)
    back_b, back_a = add((back_b, back_got_b), (back_a, back_got_a))

    back_got_a = level_send(back_a, outward)
    back_got_b = level_send(back_b, across)
    got_two = send(away_two, 2)
    give_near_y = send_y(give[:, rows:], 1)
    front = small[:4] + small_got
    small_got = send_z(front, 2)
    output, = run(finish_output, [shape(span, width)], [place, values, row(out_bias), out_a, outer_a, out_b, outer_b])
    first, = run(functools.partial(sum_kernel, rows), wide, [place, rest, *near_y])
    done(small_got, got_two, back_got_b, back_got_a, *give_near_y)
    back_b, = add((back_b, back_got_b))

    back_got_b = level_send(back_b, outward)
    two_got = send(two_away, 2)
    small = jnp.concatenate([front + small_got, small[4:]])
    small_got = send_y(small)
    second, = run(functools.partial(sum_kernel, rows), wide, [place, give, *give_near_y])
    pieces = [first, second, got_one, got_two]
    grad_inputs = finish_half(0, back_a, back_got_a)
    grad_w_qkv, grad_w_dense = run(place_joint, [shape(*w_qkv.shape, kind=F32), shape(*w_dense.shape, kind=F32)], [place, *pieces])
    full = [shape(rows, 4 * quarter, kind=F32)]
    grad_w_fc1, = run(functools.partial(place_inner, joint, (0, 0, 0, 0)), full, [place, *pieces])
    done(grad_w_qkv, grad_w_dense, *small_got)
    small = sum(small_got, small)
    done(two_got, back_got_b)
    grad_inputs = finish_half(1, back_b, back_got_b, grad_inputs)
    grad_w_fc2, = run(functools.partial(place_inner, 0, (0, 0, 0, rows)), full, [place, two_first, two_second, two_got, two_got])
    return (
        output[None],
        grad_inputs[None],
        grad_w_qkv,
        small[5, :b_qkv.size].reshape(b_qkv.shape),
        grad_w_dense,
        grad_w_fc1,
        small[6, :b_fc1.size],
        grad_w_fc2,
        small[4],
        small[0],
        small[1],
        small[2],
        small[3],
    )


def solution(mesh):
    rows = P(("shard", "ctx"), "tensor")
    tokens = P("shard", "ctx", None)
    heads = P(("shard", "ctx"), "tensor", None)
    in_specs = (tokens, tokens, P("shard", None), P("shard", "ctx"), heads, P("tensor", None), heads, rows, P("tensor"), rows,
                P(), P(), P(), P(), P())
    out_specs = (tokens, tokens, heads, P("tensor", None), heads, rows, P("tensor"), rows, P(), P(), P(), P(), P())
    return jax.shard_map(local, mesh=mesh, in_specs=in_specs, out_specs=out_specs, check_vma=False)
```
